32 devices in a mesh: expert: 4 (over x, core), shard: 8 (over z, y).
Axes of the slice: x: 2, y: 2, z: 4, core: 2. Of those that a mesh axis runs over, the one named last changes fastest.
Arguments:
- tokens: bfloat16 [65536, 512], P(('expert', 'shard')), may hold values from -6 to 6
- ln1_gain: float32 [512], P(('expert', 'shard')), may hold values from 0.5 to 1.5
- ln2_gain: float32 [512], P(('expert', 'shard')), may hold values from 0.5 to 1.5
- w_query: float32 [512, 512], P(('expert', 'shard')), may hold values from -0.25 to 0.25
- w_key: float32 [512, 512], P(('expert', 'shard')), may hold values from -0.25 to 0.25
- w_value: float32 [512, 512], P(('expert', 'shard')), may hold values from -0.25 to 0.25
- w_attn_out: float32 [512, 512], P(('expert', 'shard')), may hold values from -4 to 4
- w_ctrl: float32 [512, 32], P(('expert', 'shard')), may hold values from -0.1875 to 0.1875
- w_in: float32 [32, 512, 2048], P('expert', None, 'shard'), may hold values from -1 to 1
- b_in: float32 [32, 2048], P('expert', 'shard'), may hold values from -2 to 2
- w_exp_out: float32 [32, 2048, 512], P('expert', 'shard'), may hold values from -1.5 to 1.5
- routes: int32 [2048, 8], P(('expert', 'shard')), may hold values from 0 to 31, all different within a row; in each aligned block of 64 rows (0 to 63, 64 to 127, ...) at most 24 rows name the same one
- grad_out: bfloat16 [65536, 512], P(('expert', 'shard')), may hold values from -6 to 6
Outputs:
- output: bfloat16 [65536, 512], P(('expert', 'shard'))
- grad_tokens: bfloat16 [65536, 512], P(('expert', 'shard'))
- grad_ln1_gain: float32 [512], P(('expert', 'shard'))
- grad_ln2_gain: float32 [512], P(('expert', 'shard'))
- grad_w_query: float32 [512, 512], P(('expert', 'shard'))
- grad_w_key: float32 [512, 512], P(('expert', 'shard'))
- grad_w_value: float32 [512, 512], P(('expert', 'shard'))
- grad_w_attn_out: float32 [512, 512], P(('expert', 'shard'))
- grad_w_ctrl: float32 [512, 32], P(('expert', 'shard'))
- grad_w_in: float32 [32, 512, 2048], P('expert', None, 'shard')
- grad_b_in: float32 [32, 2048], P('expert', 'shard')
- grad_w_exp_out: float32 [32, 2048, 512], P('expert', 'shard')
The draws below stay inside these ranges and needn't reach their ends.
Inputs may be any that keep to these rules, and one draw needn't show every extreme that they name: `routes`: each row names 8 different experts. Among the rows of one device (aligned blocks of 64 groups) no expert is named more than 24 times, a bound that some block reaches.
All inputs are finite; a program needn't handle non-finite values.
Results may differ from the reference program's by a relative error of at most 0.02.
Values may be sent and summed in bfloat16 or wider, within the bound.
No kernel may reach another device: no remote copies, remote signals or barrier semaphores. Data moves between devices by JAX's collectives and lax.ppermute only.
A program may use at most 256 MiB of HBM per device.

```python
import math
import jax
import jax.numpy as jnp
import numpy as np
from jax import lax

D = 512
FF = 2048
EXPERTS = 32
HEAD_DIM = 64
HEADS = 8
GROUP = 32
ROUTES = 8
BLOCK = 256
TOK_DEV = 2048
CAP = 24
TOKENS = 65536
GROUPS = 2048


def draw_b_in(key, part):
    size_key = jax.random.fold_in(key, 11)
    sign_key = jax.random.fold_in(key, 12)
    magnitude = jax.random.uniform(size_key, (EXPERTS, FF), jnp.float32, 1.0, 2.0)
    signs = (2 * jax.random.randint(sign_key, (EXPERTS, FF), 0, 2) - 1).astype(jnp.float32)
    return magnitude * signs


def steps_of(key, dims, split, least, largest):
    def one(position, shards_of):
        draws = jax.random.uniform(jax.random.fold_in(jax.random.fold_in(key, 6), position), (shards_of,), jnp.float32, least / len(split), largest / len(split))
        return jnp.repeat(jnp.exp(draws), dims[position] // shards_of).reshape((-1,) + (1,) * (len(dims) - position - 1))

    loudness = one(*split[0])
    for cut in split[1:]:
        loudness = loudness * one(*cut)
    return loudness


def deal_out(stream_key, own, number, rows, count, top, most, skew):
    order = jax.random.permutation(stream_key, count)
    crowded, common = portions_of(count, rows * top, most, skew, True), portions_of(count, rows * top, most, skew, False)
    places = jnp.arange(count)

    def named(lengths, offset_by):
        used = int((lengths > 0).sum())
        fixed = max(1, used // 4)
        passed = fixed + (places - fixed + offset_by * (used - fixed)) % max(1, count - fixed)
        return jnp.zeros((count,), jnp.int32).at[order[jnp.where(places < fixed, places, passed)]].set(jnp.asarray(lengths, jnp.int32))

    lengths = jnp.where(number % 4 == 0, named(crowded, number // 4), named(common, number - number // 4 - 1))
    mixed = jax.random.permutation(jax.random.fold_in(own, 3), count)
    donor, sink = mixed[0:count // 2 * 2:2], mixed[1:count // 2 * 2:2]
    slack = jnp.minimum(lengths[donor] - 1, most - lengths[sink]) // 2
    slack = jnp.where((donor == order[0]) | (sink == order[0]) | (lengths[sink] == 0), 0, jnp.maximum(slack, 0))
    passed = jax.random.randint(jax.random.fold_in(own, 4), (count // 2,), 0, 1 << 20) % (slack + 1)
    lengths = lengths.at[donor].add(-passed).at[sink].add(passed)
    items = jnp.searchsorted(jnp.cumsum(lengths), jnp.arange(rows * top), side="right").astype(jnp.int32)
    listing = items.reshape(top, rows).T
    listing = listing[jax.random.permutation(jax.random.fold_in(own, 1), rows)]
    offset_by = jax.random.randint(jax.random.fold_in(own, 2), (rows, 1), 0, top)
    return jnp.take_along_axis(listing, (jnp.arange(top)[None, :] + offset_by) % top, axis=1)


def portions_of(number_of, total, reach, skew, full):
    portions = [(1 << 20) // math.isqrt(standing ** skew) + 1 for standing in range(1, number_of + 1)]
    largest = reach if full else min(reach, max(-(-total // number_of), total * portions[0] // sum(portions)))
    least = 1 if total - largest >= number_of - 1 else 0
    given, rest = [largest] + [least] * (number_of - 1), total - largest - least * (number_of - 1)
    while rest > 0:
        movable = [i for i in range(1, number_of) if given[i] < largest] or [i for i in range(1, number_of) if given[i] < reach]
        pool, left = sum([portions[i] for i in movable]), rest
        for i in movable:
            extra = min(reach - given[i], max(1, left * portions[i] // pool), rest)
            given[i] = given[i] + extra
            rest = rest - extra
    return np.array(given)


def bell_draw(stream_key, extent, scale, limit, pieces=(), held_as=jnp.bfloat16):
    entries = scale * jax.random.normal(stream_key, extent, jnp.float32)
    if pieces:
        entries = entries * steps_of(stream_key, extent, pieces, -0.22, 0.18)
    return jnp.clip(entries, -limit, limit).astype(held_as)


def setup_inputs(seed: int = 0) -> dict:
    arg_keys = jax.random.split(jax.random.key(seed), 14)
    tokens = bell_draw(arg_keys[0], (TOKENS, D), 1.0, 6.0, ((0, 32),))
    ln1_gain = jnp.clip(1.0 + 0.1 * jax.random.normal(arg_keys[1], (D,), jnp.float32), 0.5, 1.5)
    ln2_gain = jnp.clip(1.0 + 0.1 * jax.random.normal(arg_keys[2], (D,), jnp.float32), 0.5, 1.5)
    w_query = bell_draw(arg_keys[3], (D, D), D ** -0.5, 0.25, ((0, 32),), jnp.float32)
    w_key = bell_draw(arg_keys[4], (D, D), D ** -0.5, 0.25, ((0, 32),), jnp.float32)
    w_value = bell_draw(arg_keys[5], (D, D), D ** -0.5, 0.25, ((0, 32),), jnp.float32)
    w_attn_out = bell_draw(arg_keys[6], (D, D), (max(D // 256, 1)) ** -0.5, 4.0, ((0, 32),), jnp.float32)
    w_ctrl = bell_draw(arg_keys[7], (D, EXPERTS), (D * 2) ** -0.5, 0.1875, ((0, 32),), jnp.float32)
    w_in = bell_draw(arg_keys[8], (EXPERTS, D, FF), (D // 16) ** -0.5, 1.0, ((0, 4), (2, 8)), jnp.float32)
    b_in = draw_b_in(jax.random.fold_in(arg_keys[13], 71), 0)
    w_exp_out = bell_draw(arg_keys[10], (EXPERTS, FF, D), (FF // 128) ** -0.5, 1.5, ((0, 4), (1, 8)), jnp.float32)
    routes_keys = jax.random.split(jax.random.fold_in(arg_keys[11], 1), GROUPS // (TOK_DEV // GROUP))
    routes_turns = jax.random.permutation(jax.random.fold_in(arg_keys[11], 3), GROUPS // (TOK_DEV // GROUP))
    routes = jax.vmap(lambda own, number: deal_out(jax.random.fold_in(arg_keys[11], 2), own, number, TOK_DEV // GROUP, EXPERTS, ROUTES, CAP, 2))(routes_keys, routes_turns).reshape((GROUPS, ROUTES))
    grad_out = bell_draw(arg_keys[12], (TOKENS, D), 1.0, 6.0, ((0, 32),))
    return dict(tokens=tokens, ln1_gain=ln1_gain, ln2_gain=ln2_gain, w_query=w_query, w_key=w_key, w_value=w_value, w_attn_out=w_attn_out, w_ctrl=w_ctrl, w_in=w_in, b_in=b_in, w_exp_out=w_exp_out, routes=routes, grad_out=grad_out)


@jax.custom_vjp
def low(v):
    return lax.optimization_barrier(v.astype(jnp.bfloat16)).astype(jnp.float32)

@jax.custom_vjp
def low_back(v):
    return v

def low_keep(v):
    return (low(v), None)

def low_pass(kept, grad):
    return (grad,)

def back_keep(v):
    return (v, None)

def back_low(kept, grad):
    return (low(grad),)
low.defvjp(low_keep, low_pass)
low_back.defvjp(back_keep, back_low)

def matmul(left_op, right_op):
    return jnp.dot(left_op, right_op, precision=lax.Precision.HIGHEST, preferred_element_type=jnp.float32)

def layer_norm(matrix, scale_vec):
    average = lax.optimization_barrier(jnp.mean(matrix, axis=-1, keepdims=True))
    centered = matrix - average
    variance = lax.optimization_barrier(jnp.mean(centered * centered, axis=-1, keepdims=True))
    return centered * lax.rsqrt(variance + 1e-05) * scale_vec

def attend_sequence(matrix, gain_one, query_w, key_w, value_w, attn_out_w):
    length = matrix.shape[0]
    normed = low(layer_norm(matrix, gain_one))
    queries = low_back(low(matmul(normed, query_w))).reshape(length, HEADS, HEAD_DIM)
    key_rows = low_back(low(matmul(normed, key_w))).reshape(length, HEADS, HEAD_DIM)
    value_rows = low_back(low(matmul(normed, value_w))).reshape(length, HEADS, HEAD_DIM)
    scores = jnp.einsum('qhd,khd->hqk', queries, key_rows, precision=lax.Precision.HIGHEST) * 0.125
    scores = low_back(scores)
    positions = jnp.arange(length, dtype=jnp.int32) // BLOCK
    allowed = positions[:, None] >= positions[None, :]
    scores = jnp.where(allowed[None, :, :], scores, -1e+30)
    shares = low(jax.nn.softmax(scores, axis=-1))
    attended = jnp.einsum('hqk,khd->qhd', shares, value_rows, precision=lax.Precision.HIGHEST).reshape(length, D)
    attended = low_back(low(attended))
    return matrix + low_back(matmul(attended, attn_out_w))

def layer_forward(tokens, ln1_gain, ln2_gain, w_query, w_key, w_value, w_attn_out, w_ctrl, w_in, b_in, w_exp_out, routes):
    gain_one = low(ln1_gain)
    gain_two = low(ln2_gain)
    query_w = low(w_query)
    key_w = low(w_key)
    value_w = low(w_value)
    attn_out_w = low(w_attn_out)
    ctrl_w = low(w_ctrl)
    first_w = low(w_in)
    first_b = low(b_in)
    second_w = low(w_exp_out)

    def one_sequence(matrix):
        return attend_sequence(matrix, gain_one, query_w, key_w, value_w, attn_out_w)
    checked = jax.checkpoint(one_sequence)

    def scan_step(state_carry, matrix):
        return (state_carry, checked(matrix))
    sequences = tokens.reshape(-1, TOK_DEV, D)
    unused, hidden = lax.scan(scan_step, jnp.zeros((), jnp.float32), sequences)
    hidden = hidden.reshape(-1, D)
    normed = low(layer_norm(hidden, gain_two))
    logits = low_back(matmul(normed, ctrl_w))
    grouped = logits.reshape(-1, GROUP, EXPERTS)
    mix_probs = jax.nn.softmax(grouped, axis=1)
    chosen = low(jnp.take_along_axis(mix_probs, routes[:, None, :], axis=2))
    members = normed.reshape(-1, GROUP, D)
    mixed = jnp.einsum('gtk,gtd->gkd', chosen, members, precision=lax.Precision.HIGHEST)
    mixed = low_back(low(mixed))
    flat_rows = mixed.reshape(-1, D)
    expert_ids = routes.reshape(-1).astype(jnp.int32)
    onehot = (expert_ids[:, None] == jnp.arange(EXPERTS, dtype=jnp.int32)[None, :]).astype(jnp.int32)
    slot_rank = lax.optimization_barrier(jnp.sum((jnp.cumsum(onehot, axis=0) - 1) * onehot, axis=1)).astype(jnp.int32)
    slot_count = TOKENS // TOK_DEV * CAP
    buffer = jnp.zeros((EXPERTS, slot_count, D), jnp.float32).at[expert_ids, slot_rank].set(flat_rows)

    def expert_apply(packed):
        matrix, first_mat, bias_one, second_mat = packed
        pre_act = low_back(matmul(matrix, first_mat) + bias_one)
        inner_act = low_back(low(jax.nn.silu(pre_act)))
        return low_back(low(matmul(inner_act, second_mat)))
    outputs = lax.map(expert_apply, (buffer, first_w, first_b, second_w))
    returned = outputs[expert_ids, slot_rank].reshape(-1, ROUTES, D)
    combined = jnp.einsum('gtk,gkd->gtd', chosen, returned, precision=lax.Precision.HIGHEST).reshape(-1, D)
    return hidden + combined

def reference(tokens, ln1_gain, ln2_gain, w_query, w_key, w_value, w_attn_out, w_ctrl, w_in, b_in, w_exp_out, routes, grad_out):

    def forward(tok_f, gain_a, gain_b, wq_f, wk_f, wv_f, wo_f, wc_f, wi_f, bi_f, we_f):
        return layer_forward(tok_f, gain_a, gain_b, wq_f, wk_f, wv_f, wo_f, wc_f, wi_f, bi_f, we_f, routes)
    output, pullback = jax.vjp(forward, tokens.astype(jnp.float32), ln1_gain, ln2_gain, w_query, w_key, w_value, w_attn_out, w_ctrl, w_in, b_in, w_exp_out)
    grads = pullback(grad_out.astype(jnp.float32))
    return (output.astype(jnp.bfloat16), grads[0].astype(jnp.bfloat16), grads[1], grads[2], grads[3], grads[4], grads[5], grads[6], grads[7], grads[8], grads[9], grads[10])
```

```python
import jax
import jax.numpy as jnp
from jax import lax
from jax.experimental import pallas as pl
from jax.experimental.pallas import tpu as pltpu
from jax.sharding import PartitionSpec as P

D = 512
HEAD_DIM = 64
GROUP = 32
ROUTES = 8
BLOCK = 256
CAP = 24
EPSILON = 1e-05
SCALE = 0.125 * 1.4426950408889634
BOTH = ("expert", "shard")

bf16 = jnp.bfloat16
f32 = jnp.float32
VMEM = pltpu.CompilerParams(vmem_limit_bytes=56 * 2**20)


def norm_forward(matrix, scale_vec):
    average = jnp.mean(matrix, axis=1, keepdims=True)
    centered = matrix - average
    inverse = lax.rsqrt(jnp.mean(centered * centered, axis=1, keepdims=True) + EPSILON)
    scaled = centered * inverse
    return (scaled * scale_vec, scaled, inverse)


def norm_input_grad(upstream, scaled, inverse, scale_vec):
    adjusted = upstream * scale_vec
    first_mean = jnp.mean(adjusted, axis=1, keepdims=True)
    second_mean = jnp.mean(adjusted * scaled, axis=1, keepdims=True)
    return inverse * (adjusted - first_mean - scaled * second_mean)


def product(left_op, right_op):
    return jnp.dot(left_op, right_op, preferred_element_type=f32)


def transposed_product(left_op, right_op):
    return lax.dot_general(left_op, right_op, (((0,), (0,)), ((), ())), preferred_element_type=f32)


def against_rows(left_op, right_op):
    return lax.dot_general(left_op, right_op, (((1,), (1,)), ((), ())), preferred_element_type=f32)


def attention_forward_kernel(q_ref, k_ref, v_ref, o_ref, lse_ref):
    length = q_ref.shape[0]
    q_t = q_ref[...].T
    v_t = v_ref[...].T
    zero = jnp.zeros((HEAD_DIM, BLOCK), bf16)
    ones = jnp.ones((16, length), bf16)
    for b in range(length // BLOCK):
        n = (b + 1) * BLOCK
        cols = slice(b * BLOCK, n)
        q_b = q_t[:, cols]
        keys = k_ref[:n, :]
        outs = []
        for h in range(2):
            half = q_b[h * HEAD_DIM : (h + 1) * HEAD_DIM]
            scores = product(keys, jnp.concatenate([half, zero] if h == 0 else [zero, half], 0))
            top = jnp.max(scores, axis=0, keepdims=True)
            weights = jnp.exp2(scores * SCALE - top * SCALE).astype(bf16)
            values = jnp.concatenate([v_t[h * HEAD_DIM : (h + 1) * HEAD_DIM, :n], ones[:, :n]], 0)
            out = product(values, weights)
            total = out[HEAD_DIM : HEAD_DIM + 1]
            outs.append(out[:HEAD_DIM] / total)
            lse_ref[0, h : h + 1, cols] = top * SCALE + jnp.log2(total)
        o_ref[cols, :] = jnp.concatenate(outs, 0).T.astype(bf16)


def attention_backward_kernel(
    q_ref, k_ref, v_ref, g_ref, o_ref, lse_ref, dq_ref, dk_ref, dv_ref, dq_t
):
    length = q_ref.shape[0]
    q = q_ref[...]
    g = g_ref[...]
    q_t = q.T
    g_t = g.T
    k_t = k_ref[...].T
    both = (g.astype(f32) * o_ref[...].astype(f32)).T
    lane = lax.broadcasted_iota(jnp.int32, (1, 2 * HEAD_DIM), 1)
    zero = jnp.zeros((HEAD_DIM, length), bf16)
    heads = []
    for h in range(2):
        rows = slice(h * HEAD_DIM, (h + 1) * HEAD_DIM)
        mine = (lane < HEAD_DIM) if h == 0 else (lane >= HEAD_DIM)
        heads.append(
            (
                rows,
                jnp.concatenate([q_t[rows], zero] if h == 0 else [zero, q_t[rows]], 0),
                jnp.concatenate([g_t[rows], zero] if h == 0 else [zero, g_t[rows]], 0),
                jnp.where(mine, q, 0).astype(bf16),
                jnp.where(mine, g, 0).astype(bf16),
                jnp.sum(both[rows], axis=0, keepdims=True),
                lse_ref[0, h : h + 1, :],
            )
        )
    for j in range(length // BLOCK):
        lo = j * BLOCK
        here = slice(lo, lo + BLOCK)
        keys = k_ref[here, :]
        values = v_ref[here, :]
        key_grad = jnp.zeros((BLOCK, 2 * HEAD_DIM), f32)
        value_grad = jnp.zeros((BLOCK, 2 * HEAD_DIM), f32)
        for rows, q_side, g_side, q_mine, g_mine, delta, lse in heads:
            shares = jnp.exp2(product(keys, q_side[:, lo:]) * SCALE - lse[:, lo:])
            share_grad = product(values, g_side[:, lo:])
            score_grad = (shares * (share_grad - delta[:, lo:])).astype(bf16)
            value_grad = value_grad + product(shares.astype(bf16), g_mine[lo:])
            key_grad = key_grad + product(score_grad, q_mine[lo:])
            query_part = product(k_t[rows, here], score_grad)
            if j == 0:
                dq_t[rows, :] = query_part
            else:
                dq_t[rows, lo:] = dq_t[rows, lo:] + query_part
        dk_ref[here, :] = (key_grad * 0.125).astype(bf16)
        dv_ref[here, :] = value_grad.astype(bf16)
    dq_ref[...] = (dq_t[...] * 0.125).T.astype(bf16)


def pair_columns(length, offset):
    return pl.BlockSpec((length, 2 * HEAD_DIM), lambda pair: (0, pair + offset))


def attention_forward(qkv):
    length = qkv.shape[0]
    pairs = D // (2 * HEAD_DIM)
    stats = pl.BlockSpec((1, 2, length), lambda pair: (pair, 0, 0))
    return pl.pallas_call(
        attention_forward_kernel,
        grid=(pairs,),
        in_specs=[pair_columns(length, i * pairs) for i in range(3)],
        out_specs=[pair_columns(length, 0), stats],
        out_shape=[
            jax.ShapeDtypeStruct((length, D), bf16),
            jax.ShapeDtypeStruct((pairs, 2, length), f32),
        ],
        compiler_params=VMEM,
        cost_estimate=pl.CostEstimate(
            flops=40_000_000_000, bytes_accessed=8 * 2**20, transcendentals=20_000_000
        ),
        name="attention_forward",
    )(qkv, qkv, qkv)


def attention_backward(qkv, grad, attended, lse):
    length = qkv.shape[0]
    pairs = D // (2 * HEAD_DIM)
    stats = pl.BlockSpec((1, 2, length), lambda pair: (pair, 0, 0))
    return pl.pallas_call(
        attention_backward_kernel,
        grid=(pairs,),
        in_specs=[pair_columns(length, i * pairs) for i in range(3)]
        + [pair_columns(length, 0), pair_columns(length, 0), stats],
        out_specs=[pair_columns(length, 0)] * 3,
        out_shape=[jax.ShapeDtypeStruct((length, D), bf16)] * 3,
        scratch_shapes=[pltpu.VMEM((2 * HEAD_DIM, length), f32)],
        compiler_params=VMEM,
        cost_estimate=pl.CostEstimate(
            flops=50_000_000_000, bytes_accessed=16 * 2**20, transcendentals=20_000_000
        ),
        name="attention_backward",
    )(qkv, qkv, qkv, grad, attended, lse)


def gather_rows(block):
    n_shard = lax.axis_size("shard")
    n_expert = lax.axis_size("expert")
    here = lax.axis_index("shard")
    rows, width = block.shape
    held = jnp.zeros((n_shard, rows, width), block.dtype)
    held = lax.dynamic_update_slice(held, block[None], (here, 0, 0))
    for k in range(1, n_shard):
        got = lax.ppermute(block, "shard", [(i, (i + k) % n_shard) for i in range(n_shard)])
        held = lax.dynamic_update_slice(held, got[None], ((here - k) % n_shard, 0, 0))
    held = held.reshape(n_shard * rows, width)
    mine = lax.axis_index("expert")
    bit = n_expert // 2
    steps = 0
    while bit:
        got = lax.ppermute(held, "expert", [(i, i ^ bit) for i in range(n_expert)])
        low = (mine & bit) == 0
        held = jnp.stack([jnp.where(low, held, got), jnp.where(low, got, held)])
        bit //= 2
        steps += 1
    order = tuple(range(steps - 1, -1, -1)) + (steps, steps + 1)
    return held.transpose(order).reshape(n_expert * n_shard * rows, width)


def scatter_sum(partial):
    n_shard = lax.axis_size("shard")
    n_expert = lax.axis_size("expert")
    mine = lax.axis_index("expert")
    width = partial.shape[1]
    steps = n_expert.bit_length() - 1
    held = partial.reshape((2,) * steps + (-1, width))
    for step in range(steps):
        bit = 1 << step
        axis = steps - 1 - step
        low = (mine & bit) == 0
        first = lax.index_in_dim(held, 0, axis, keepdims=False)
        second = lax.index_in_dim(held, 1, axis, keepdims=False)
        away = jnp.where(low, second, first).astype(bf16)
        got = lax.ppermute(away, "expert", [(i, i ^ bit) for i in range(n_expert)])
        held = jnp.where(low, first, second) + got.astype(f32)
    pieces = lax.all_to_all(held.astype(bf16), "shard", split_axis=0, concat_axis=0, tiled=True)
    return jnp.sum(pieces.reshape(n_shard, -1, width).astype(f32), axis=0)


def to_experts(array, copies):
    if copies > 1:
        array = jnp.repeat(array, copies, axis=0)
    return lax.all_to_all(array, "shard", split_axis=0, concat_axis=0, tiled=True)


def from_experts(array, copies):
    back = lax.all_to_all(array, "shard", split_axis=0, concat_axis=0, tiled=True).astype(f32)
    if copies > 1:
        back = back.reshape((-1, copies) + back.shape[1:]).sum(axis=1)
    return back


def exchange(rows, copies):
    n_expert = lax.axis_size("expert")
    n_shard = lax.axis_size("shard")
    groups = None
    if copies > 1:
        groups = [
            [e * n_shard + s for e in range(n_expert) for s in range(p, n_shard, copies)]
            for p in range(copies)
        ]
    return lax.all_to_all(
        rows, BOTH, split_axis=0, concat_axis=0, tiled=True, axis_index_groups=groups
    )


def body(
    tokens,
    ln1_gain,
    ln2_gain,
    w_query,
    w_key,
    w_value,
    w_attn_out,
    w_ctrl,
    w_in,
    b_in,
    w_exp_out,
    routes,
    grad_out,
):
    n_expert = lax.axis_size("expert")
    n_shard = lax.axis_size("shard")
    experts = w_ctrl.shape[1]
    local_count = experts // n_expert
    copies = n_shard // local_count
    length = tokens.shape[0]
    groups = length // GROUP
    hidden = w_in.shape[2]

    small = jnp.concatenate(
        [
            w_query,
            w_key,
            w_value,
            w_attn_out,
            w_ctrl,
            ln1_gain[:, None],
            ln2_gain[:, None],
            jnp.zeros((w_query.shape[0], 128 - experts - 2), f32),
        ],
        axis=1,
    ).astype(bf16)
    whole = gather_rows(small)
    qkv_w = whole[:, : 3 * D]
    attn_out_w = whole[:, 3 * D : 4 * D]
    ctrl_w = whole[:, 4 * D : 4 * D + experts]
    gain_one = whole[:, 4 * D + experts].astype(f32)
    gain_two = whole[:, 4 * D + experts + 1].astype(f32)

    first_block = jnp.concatenate(
        [w_in, jnp.broadcast_to(b_in[:, None, :], (local_count, 16, hidden))], axis=1
    ).astype(bf16)
    whole, first_block, second_block = lax.optimization_barrier(
        (whole, first_block, w_exp_out.astype(bf16))
    )
    first_all = to_experts(first_block, copies)
    second_w = to_experts(second_block, copies)
    first_w = first_all[:, :D, :]
    first_b = first_all[:, D, :]

    inputs = tokens.astype(f32)
    normed_one, scaled_one, inverse_one = norm_forward(inputs, gain_one)
    normed_low = normed_one.astype(bf16)
    qkv = product(normed_low, qkv_w).astype(bf16)
    attended_low, lse = attention_forward(qkv)
    residual = inputs + product(attended_low, attn_out_w)
    normed_two, scaled_two, inverse_two = norm_forward(residual, gain_two)
    normed_mix = normed_two.astype(bf16)
    logits = product(normed_mix, ctrl_w)
    mix_probs = jax.nn.softmax(logits.reshape(groups, GROUP, experts), axis=1)
    selector = (routes[:, :, None] == jnp.arange(experts, dtype=jnp.int32)[None, None, :]).astype(f32)
    chosen = jnp.sum(mix_probs[:, :, None, :] * selector[:, None, :, :], axis=3)
    chosen_low = chosen.astype(bf16)
    members = normed_mix.reshape(groups, GROUP, D)
    members_up = grad_out.reshape(groups, GROUP, D)
    mixed = jnp.einsum("gtk,gtd->gkd", chosen_low, members, preferred_element_type=f32).astype(bf16)
    result_grad = jnp.einsum(
        "gtk,gtd->gkd", chosen_low, members_up, preferred_element_type=f32
    ).astype(bf16)

    named = jnp.sum(selector, axis=1)
    earlier = jnp.tril(jnp.ones((groups, groups), f32), -1)
    before = product(earlier.astype(bf16), named.astype(bf16))
    rank = jnp.sum(selector * before[:, None, :], axis=2).astype(jnp.int32)
    slot_of = (routes * CAP + rank).reshape(-1)
    dispatch = (
        jnp.arange(experts * CAP, dtype=jnp.int32)[:, None] == slot_of[None, :]
    ).astype(bf16)
    rows = jnp.concatenate([mixed.reshape(-1, D), result_grad.reshape(-1, D)], axis=1)
    outgoing = product(dispatch, rows).astype(bf16)
    arrived_all = exchange(outgoing, copies)
    arrived = arrived_all[:, :D]
    arrived_grad = arrived_all[:, D:]

    pre_act = (
        jnp.einsum("rd,sdf->srf", arrived, first_w, preferred_element_type=f32)
        + first_b.astype(f32)[:, None, :]
    )
    sigma = jax.nn.sigmoid(pre_act)
    active = (pre_act * sigma).astype(bf16)
    results = jnp.einsum("srf,sfd->rd", active, second_w, preferred_element_type=f32).astype(bf16)
    hidden_grad = jnp.einsum(
        "rd,sfd->srf", arrived_grad, second_w, preferred_element_type=f32
    ).astype(bf16)
    pre_grad = (hidden_grad.astype(f32) * (sigma * (1.0 + pre_act * (1.0 - sigma)))).astype(bf16)
    mixed_grad_rows = jnp.einsum(
        "srf,sdf->rd", pre_grad, first_w, preferred_element_type=f32
    ).astype(bf16)
    returned = exchange(jnp.concatenate([results, mixed_grad_rows], axis=1), copies)

    first_w_grad = jnp.einsum("rd,srf->sdf", arrived, pre_grad, preferred_element_type=f32)
    first_b_grad = jnp.sum(pre_grad.astype(f32), axis=1)
    second_w_grad = jnp.einsum("srf,rd->sfd", active, arrived_grad, preferred_element_type=f32)
    first_sum = from_experts(
        jnp.concatenate(
            [
                first_w_grad,
                jnp.broadcast_to(first_b_grad[:, None, :], (n_shard, 16, hidden)),
            ],
            axis=1,
        ).astype(bf16),
        copies,
    )
    w_in_grad = first_sum[:, :D, :]
    b_in_grad = first_sum[:, D, :]
    w_exp_out_grad = from_experts(second_w_grad.astype(bf16), copies)

    both_rows = transposed_product(dispatch, returned).astype(bf16)
    gathered_rows = both_rows[:, :D].reshape(groups, ROUTES, D)
    mixed_grad = both_rows[:, D:].reshape(groups, ROUTES, D)
    mixture = jnp.einsum(
        "gtk,gkd->gtd", chosen_low, gathered_rows, preferred_element_type=f32
    ).reshape(length, D)
    output = (residual + mixture).astype(bf16)
    upstream = grad_out.astype(f32)
    chosen_grad = jnp.einsum(
        "gtd,gkd->gtk", members_up, gathered_rows, preferred_element_type=f32
    ) + jnp.einsum("gtd,gkd->gtk", members, mixed_grad, preferred_element_type=f32)
    normed_grad = jnp.einsum(
        "gtk,gkd->gtd", chosen_low, mixed_grad, preferred_element_type=f32
    ).reshape(length, D)
    prob_grad = jnp.sum(chosen_grad[:, :, :, None] * selector[:, None, :, :], axis=2)
    logit_grad = (
        (mix_probs * (prob_grad - jnp.sum(mix_probs * prob_grad, axis=1, keepdims=True)))
        .reshape(length, experts)
        .astype(bf16)
    )
    normed_grad = normed_grad + against_rows(logit_grad, ctrl_w)
    ctrl_grad = transposed_product(normed_mix, logit_grad)
    gain_two_grad = jnp.sum(normed_grad * scaled_two, axis=0)
    residual_grad = upstream + norm_input_grad(normed_grad, scaled_two, inverse_two, gain_two)
    branch_grad = residual_grad.astype(bf16)
    attn_out_grad = transposed_product(attended_low, branch_grad)
    early = scatter_sum(
        jnp.concatenate(
            [
                attn_out_grad,
                ctrl_grad,
                gain_two_grad[:, None],
                jnp.zeros((D, 128 - experts - 1), f32),
            ],
            axis=1,
        )
    )
    wo_grad = early[:, :D]
    wc_grad = early[:, D : D + experts]
    ln2_grad = early[:, D + experts]

    attended_grad = against_rows(branch_grad, attn_out_w).astype(bf16)
    query_grad, key_grad, value_grad = attention_backward(qkv, attended_grad, attended_low, lse)
    late = scatter_sum(
        jnp.concatenate(
            [transposed_product(normed_low, g) for g in (query_grad, key_grad, value_grad)], axis=1
        )
    )
    small_own = small[:, : 3 * D].astype(f32)
    ln1_grad = jnp.sum(late * small_own, axis=1) / small[:, 4 * D + experts].astype(f32)
    normed_one_grad = (
        against_rows(query_grad, qkv_w[:, :D])
        + against_rows(key_grad, qkv_w[:, D : 2 * D])
        + against_rows(value_grad, qkv_w[:, 2 * D :])
    )
    input_grad = (
        residual_grad + norm_input_grad(normed_one_grad, scaled_one, inverse_one, gain_one)
    ).astype(bf16)
    return (
        output,
        input_grad,
        ln1_grad,
        ln2_grad,
        late[:, :D],
        late[:, D : 2 * D],
        late[:, 2 * D :],
        wo_grad,
        wc_grad,
        w_in_grad,
        b_in_grad,
        w_exp_out_grad,
    )


def solution(mesh):
    rows = P(BOTH, None)
    vector = P(BOTH)
    experts = (P("expert", None, "shard"), P("expert", "shard"), P("expert", "shard", None))
    in_specs = (rows, vector, vector) + (rows,) * 5 + experts + (rows, rows)
    out_specs = (rows, rows, vector, vector) + (rows,) * 5 + experts
    return jax.shard_map(body, mesh=mesh, in_specs=in_specs, out_specs=out_specs, check_vma=False)
```

```python
import jax
import jax.numpy as jnp
from jax import lax
from jax.experimental import pallas as pl
from jax.experimental.pallas import tpu as pltpu
from jax.sharding import PartitionSpec as P

D = 512
HEAD_DIM = 64
GROUP = 32
ROUTES = 8
BLOCK = 256
CAP = 24
EPSILON = 1e-05
SCALE = 0.125 * 1.4426950408889634
BOTH = ("expert", "shard")

bf16 = jnp.bfloat16
f32 = jnp.float32
VMEM = pltpu.CompilerParams(vmem_limit_bytes=56 * 2**20)


def product(left_op, right_op):
    return jnp.dot(left_op, right_op, preferred_element_type=f32)


def transposed_product(left_op, right_op):
    return lax.dot_general(left_op, right_op, (((0,), (0,)), ((), ())), preferred_element_type=f32)


def against_rows(left_op, right_op):
    return lax.dot_general(left_op, right_op, (((1,), (1,)), ((), ())), preferred_element_type=f32)


def attention_forward_kernel(q_ref, k_ref, v_ref, o_ref, lse_ref):
    length = q_ref.shape[0]
    q_t = q_ref[...].T
    v_t = v_ref[...].T
    zero = jnp.zeros((HEAD_DIM, BLOCK), bf16)
    ones = jnp.ones((16, length), bf16)
    for b in range(length // BLOCK):
        n = (b + 1) * BLOCK
        cols = slice(b * BLOCK, n)
        q_b = q_t[:, cols]
        keys = k_ref[:n, :]
        outs = []
        for h in range(2):
            half = q_b[h * HEAD_DIM : (h + 1) * HEAD_DIM]
            scores = product(keys, jnp.concatenate([half, zero] if h == 0 else [zero, half], 0))
            top = jnp.max(scores, axis=0, keepdims=True)
            weights = jnp.exp2(scores * SCALE - top * SCALE).astype(bf16)
            values = jnp.concatenate([v_t[h * HEAD_DIM : (h + 1) * HEAD_DIM, :n], ones[:, :n]], 0)
            out = product(values, weights)
            total = out[HEAD_DIM : HEAD_DIM + 1]
            outs.append(out[:HEAD_DIM] / total)
            lse_ref[0, h : h + 1, cols] = top * SCALE + jnp.log2(total)
        o_ref[cols, :] = jnp.concatenate(outs, 0).T.astype(bf16)


def attention_backward_kernel(
    q_ref, k_ref, v_ref, g_ref, o_ref, lse_ref, dq_ref, dk_ref, dv_ref, dq_t
):
    length = q_ref.shape[0]
    q = q_ref[...]
    g = g_ref[...]
    q_t = q.T
    g_t = g.T
    k_t = k_ref[...].T
    both = (g.astype(f32) * o_ref[...].astype(f32)).T
    lane = lax.broadcasted_iota(jnp.int32, (1, 2 * HEAD_DIM), 1)
    zero = jnp.zeros((HEAD_DIM, length), bf16)
    heads = []
    for h in range(2):
        rows = slice(h * HEAD_DIM, (h + 1) * HEAD_DIM)
        mine = (lane < HEAD_DIM) if h == 0 else (lane >= HEAD_DIM)
        heads.append(
            (
                rows,
                jnp.concatenate([q_t[rows], zero] if h == 0 else [zero, q_t[rows]], 0),
                jnp.concatenate([g_t[rows], zero] if h == 0 else [zero, g_t[rows]], 0),
                jnp.where(mine, q, 0).astype(bf16),
                jnp.where(mine, g, 0).astype(bf16),
                jnp.sum(both[rows], axis=0, keepdims=True),
                lse_ref[0, h : h + 1, :],
            )
        )
    for j in range(length // BLOCK):
        lo = j * BLOCK
        here = slice(lo, lo + BLOCK)
        keys = k_ref[here, :]
        values = v_ref[here, :]
        key_grad = jnp.zeros((BLOCK, 2 * HEAD_DIM), f32)
        value_grad = jnp.zeros((BLOCK, 2 * HEAD_DIM), f32)
        for rows, q_side, g_side, q_mine, g_mine, delta, lse in heads:
            shares = jnp.exp2(product(keys, q_side[:, lo:]) * SCALE - lse[:, lo:])
            share_grad = product(values, g_side[:, lo:])
            score_grad = (shares * (share_grad - delta[:, lo:])).astype(bf16)
            value_grad = value_grad + product(shares.astype(bf16), g_mine[lo:])
            key_grad = key_grad + product(score_grad, q_mine[lo:])
            query_part = product(k_t[rows, here], score_grad)
            if j == 0:
                dq_t[rows, :] = query_part
            else:
                dq_t[rows, lo:] = dq_t[rows, lo:] + query_part
        dk_ref[here, :] = (key_grad * 0.125).astype(bf16)
        dv_ref[here, :] = value_grad.astype(bf16)
    dq_ref[...] = (dq_t[...] * 0.125).T.astype(bf16)


def pair_columns(length, offset):
    return pl.BlockSpec((length, 2 * HEAD_DIM), lambda pair: (0, pair + offset))


def attention_forward(qkv):
    length = qkv.shape[0]
    pairs = D // (2 * HEAD_DIM)
    stats = pl.BlockSpec((1, 2, length), lambda pair: (pair, 0, 0))
    return pl.pallas_call(
        attention_forward_kernel,
        grid=(pairs,),
        in_specs=[pair_columns(length, i * pairs) for i in range(3)],
        out_specs=[pair_columns(length, 0), stats],
        out_shape=[
            jax.ShapeDtypeStruct((length, D), bf16),
            jax.ShapeDtypeStruct((pairs, 2, length), f32),
        ],
        compiler_params=VMEM,
        cost_estimate=pl.CostEstimate(
            flops=40_000_000_000, bytes_accessed=8 * 2**20, transcendentals=20_000_000
        ),
        name="attention_forward",
    )(qkv, qkv, qkv)


def attention_backward(qkv, grad, attended, lse):
    length = qkv.shape[0]
    pairs = D // (2 * HEAD_DIM)
    stats = pl.BlockSpec((1, 2, length), lambda pair: (pair, 0, 0))
    return pl.pallas_call(
        attention_backward_kernel,
        grid=(pairs,),
        in_specs=[pair_columns(length, i * pairs) for i in range(3)]
        + [pair_columns(length, 0), pair_columns(length, 0), stats],
        out_specs=[pair_columns(length, 0)] * 3,
        out_shape=[jax.ShapeDtypeStruct((length, D), bf16)] * 3,
        scratch_shapes=[pltpu.VMEM((2 * HEAD_DIM, length), f32)],
        compiler_params=VMEM,
        cost_estimate=pl.CostEstimate(
            flops=50_000_000_000, bytes_accessed=16 * 2**20, transcendentals=20_000_000
        ),
        name="attention_backward",
    )(qkv, qkv, qkv, grad, attended, lse)


CHUNK = 256
LANES = 128
BIAS_ROWS = 16


def call(kernel, grid, in_specs, out_specs, out_shape, scratch, flops, moved, name):
    return pl.pallas_call(
        kernel,
        grid=(grid,),
        in_specs=in_specs,
        out_specs=out_specs,
        out_shape=out_shape,
        scratch_shapes=scratch,
        compiler_params=VMEM,
        cost_estimate=pl.CostEstimate(flops=flops, bytes_accessed=moved, transcendentals=0),
        name=name,
    )


def fixed(*shape):
    return pl.BlockSpec(shape, lambda i: (0,) * len(shape))


def leading(*shape):
    return pl.BlockSpec(shape, lambda i: (i,) + (0,) * (len(shape) - 1))


def normalise(matrix):
    average = jnp.mean(matrix, axis=1, keepdims=True)
    centered = matrix - average
    inverse = lax.rsqrt(jnp.mean(centered * centered, axis=1, keepdims=True) + EPSILON)
    return centered * inverse, inverse


def norm_input_grad(upstream, scaled, inverse, gain):
    adjusted = upstream * gain
    first_mean = jnp.mean(adjusted, axis=1, keepdims=True)
    second_mean = jnp.mean(adjusted * scaled, axis=1, keepdims=True)
    return inverse * (adjusted - first_mean - scaled * second_mean)


def pack_kernel(first_ref, bias_ref, second_ref, out_ref):
    hidden = first_ref.shape[2]
    out_ref[0, :D, :] = first_ref[0].astype(bf16)
    out_ref[0, D : D + BIAS_ROWS, :] = jnp.broadcast_to(bias_ref[0], (BIAS_ROWS, hidden)).astype(bf16)
    for c in range(D // hidden):
        start = D + BIAS_ROWS + c * hidden
        out_ref[0, start : start + hidden, :] = second_ref[
            0, :, c * hidden : (c + 1) * hidden
        ].astype(bf16)


def pack_weights(w_in, b_in, w_exp_out):
    local, _, hidden = w_in.shape
    total = 2 * D + BIAS_ROWS
    return call(
        pack_kernel,
        local,
        [leading(1, D, hidden), leading(1, 1, hidden), leading(1, hidden, D)],
        leading(1, total, hidden),
        jax.ShapeDtypeStruct((local, total, hidden), bf16),
        [],
        1_000_000,
        12 * 2**20,
        "pack_weights",
    )(w_in, b_in[:, None, :], w_exp_out)


def unpack_kernel(in_ref, first_ref, bias_ref, second_ref):
    hidden = first_ref.shape[2]
    first_ref[0] = in_ref[0, :D, :].astype(f32)
    bias_ref[0] = in_ref[0, D : D + BIAS_ROWS, :].astype(f32)[:1]
    for c in range(D // hidden):
        start = D + BIAS_ROWS + c * hidden
        second_ref[0, :, c * hidden : (c + 1) * hidden] = in_ref[
            0, start : start + hidden, :
        ].astype(f32)


def unpack_grads(packed):
    local, total, hidden = packed.shape
    first, bias, second = call(
        unpack_kernel,
        local,
        [leading(1, total, hidden)],
        [leading(1, D, hidden), leading(1, 1, hidden), leading(1, hidden, D)],
        [
            jax.ShapeDtypeStruct((local, D, hidden), f32),
            jax.ShapeDtypeStruct((local, 1, hidden), f32),
            jax.ShapeDtypeStruct((local, hidden, D), f32),
        ],
        [],
        1_000_000,
        12 * 2**20,
        "unpack_grads",
    )(packed)
    return first, bias[:, 0, :], second


def expert_kernel(rows_ref, w_ref, out_ref, active_ref, pre_grad_ref, results, mixed_grad):
    step = pl.program_id(0)
    hidden = w_ref.shape[2]
    first = w_ref[0, :D, :]
    bias = w_ref[0, D : D + BIAS_ROWS, :].astype(f32)[:1]
    pre_act = product(rows_ref[:, :D], first) + bias
    sigma = 1.0 / (1.0 + jnp.exp(-pre_act))
    active = (pre_act * sigma).astype(bf16)
    active_ref[0] = active
    hidden_grad = jnp.zeros_like(pre_act)
    parts = []
    for c in range(D // hidden):
        start = D + BIAS_ROWS + c * hidden
        second = w_ref[0, start : start + hidden, :]
        cols = slice(D + c * hidden, D + (c + 1) * hidden)
        hidden_grad = hidden_grad + against_rows(rows_ref[:, cols], second)
        parts.append(product(active, second))
    pre_grad = (
        hidden_grad.astype(bf16).astype(f32) * (sigma * (1.0 + pre_act * (1.0 - sigma)))
    ).astype(bf16)
    pre_grad_ref[0] = pre_grad
    back = against_rows(pre_grad, first)

    @pl.when(step == 0)
    def _():
        for c, part in enumerate(parts):
            results[:, c * hidden : (c + 1) * hidden] = part
        mixed_grad[...] = back

    @pl.when(step > 0)
    def _():
        for c, part in enumerate(parts):
            cols = slice(c * hidden, (c + 1) * hidden)
            results[:, cols] = results[:, cols] + part
        mixed_grad[...] = mixed_grad[...] + back

    @pl.when(step == pl.num_programs(0) - 1)
    def _():
        out_ref[:, :D] = results[...].astype(bf16)
        out_ref[:, D:] = mixed_grad[...].astype(bf16)


def expert_rows(rows, weights):
    count = rows.shape[0]
    shards, total, hidden = weights.shape
    per_shard = jax.ShapeDtypeStruct((shards, count, hidden), bf16)
    return call(
        expert_kernel,
        shards,
        [fixed(count, 2 * D), leading(1, total, hidden)],
        [fixed(count, 2 * D), leading(1, count, hidden), leading(1, count, hidden)],
        [jax.ShapeDtypeStruct((count, 2 * D), bf16), per_shard, per_shard],
        [pltpu.VMEM((count, D), f32), pltpu.VMEM((count, D), f32)],
        8 * count * D * shards * hidden,
        14 * 2**20,
        "expert_rows",
    )(rows, weights)


def expert_grad_kernel(rows_ref, active_ref, pre_grad_ref, out_ref, rows_t):
    hidden = out_ref.shape[2]

    @pl.when(pl.program_id(0) == 0)
    def _():
        rows_t[...] = rows_ref[:, :D].T

    pre_grad = pre_grad_ref[0]
    out_ref[0, :D, :] = product(rows_t[...], pre_grad).astype(bf16)
    out_ref[0, D : D + BIAS_ROWS, :] = jnp.broadcast_to(
        jnp.sum(pre_grad.astype(f32), axis=0, keepdims=True), (BIAS_ROWS, hidden)
    ).astype(bf16)
    active_t = active_ref[0].T
    for c in range(D // hidden):
        start = D + BIAS_ROWS + c * hidden
        out_ref[0, start : start + hidden, :] = product(
            active_t, rows_ref[:, D + c * hidden : D + (c + 1) * hidden]
        ).astype(bf16)


def expert_grads(rows, active, pre_grad):
    count = rows.shape[0]
    shards, _, hidden = active.shape
    total = 2 * D + BIAS_ROWS
    return call(
        expert_grad_kernel,
        shards,
        [fixed(count, 2 * D), leading(1, count, hidden), leading(1, count, hidden)],
        leading(1, total, hidden),
        jax.ShapeDtypeStruct((shards, total, hidden), bf16),
        [pltpu.VMEM((D, count), bf16)],
        4 * count * D * shards * hidden,
        14 * 2**20,
        "expert_grads",
    )(rows, active, pre_grad)


def project_kernel(tokens_ref, w_ref, gain_ref, qkv_ref, normed_ref):
    scaled, _ = normalise(tokens_ref[...].astype(f32))
    normed = (scaled * gain_ref[...]).astype(bf16)
    normed_ref[...] = normed
    qkv_ref[...] = product(normed, w_ref[...]).astype(bf16)


def project(tokens, qkv_w, gain):
    length = tokens.shape[0]
    return call(
        project_kernel,
        length // CHUNK,
        [leading(CHUNK, D), fixed(D, 3 * D), fixed(1, D)],
        [leading(CHUNK, 3 * D), leading(CHUNK, D)],
        [jax.ShapeDtypeStruct((length, 3 * D), bf16), jax.ShapeDtypeStruct((length, D), bf16)],
        [],
        6 * length * D * D,
        12 * 2**20,
        "project",
    )(tokens, qkv_w, gain)


def choose(probs, routes):
    columns = routes.shape[1]
    shape = (LANES, columns)
    onehot = (lax.broadcasted_iota(jnp.int32, shape, 0) == routes).astype(bf16)
    tokens = probs.shape[0]
    own = lax.broadcasted_iota(jnp.int32, (tokens, columns), 0) // GROUP == (
        lax.broadcasted_iota(jnp.int32, (tokens, columns), 1) // ROUTES
    )
    chosen = jnp.where(own, product(probs.astype(bf16), onehot), 0.0).astype(bf16)
    return chosen, onehot, own


def mix_kernel(
    attended_ref, tokens_ref, grad_ref, wo_ref, ctrl_ref, gain_ref, routes_ref, slots_ref,
    residual_ref, probs_ref, out_ref, rows,
):
    step = pl.program_id(0)
    residual = tokens_ref[...].astype(f32) + product(attended_ref[...], wo_ref[...])
    residual_ref[...] = residual
    scaled, _ = normalise(residual)
    normed = (scaled * gain_ref[...]).astype(bf16)
    logits = product(normed, ctrl_ref[...]).reshape(CHUNK // GROUP, GROUP, LANES)
    weights = jnp.exp(logits - jnp.max(logits, axis=1, keepdims=True))
    probs = (weights / jnp.sum(weights, axis=1, keepdims=True)).reshape(CHUNK, LANES)
    probs_ref[...] = probs
    chosen, _, _ = choose(probs, routes_ref[0])
    columns = chosen.shape[1]
    here = pl.ds(pl.multiple_of(step * columns, columns), columns)
    rows[here, :D] = transposed_product(chosen, normed).astype(bf16)
    rows[here, D:] = transposed_product(chosen, grad_ref[...]).astype(bf16)

    @pl.when(step == pl.num_programs(0) - 1)
    def _():
        shape = (out_ref.shape[0], rows.shape[0])
        dispatch = (lax.broadcasted_iota(jnp.int32, shape, 0) == slots_ref[...]).astype(bf16)
        out_ref[...] = product(dispatch, rows[...]).astype(bf16)


def mix(attended, tokens, grad_out, attn_out_w, ctrl_w, gain, routes, slots, slot_count):
    length = tokens.shape[0]
    steps = length // CHUNK
    count = slots.shape[0]
    return call(
        mix_kernel,
        steps,
        [leading(CHUNK, D)] * 3
        + [fixed(D, D), fixed(D, LANES), fixed(1, D), leading(1, 1, count // steps), fixed(1, count)],
        [leading(CHUNK, D), leading(CHUNK, LANES), fixed(slot_count, 2 * D)],
        [
            jax.ShapeDtypeStruct((length, D), f32),
            jax.ShapeDtypeStruct((length, LANES), f32),
            jax.ShapeDtypeStruct((slot_count, 2 * D), bf16),
        ],
        [pltpu.VMEM((count, 2 * D), bf16)],
        4 * length * D * D,
        14 * 2**20,
        "mix",
    )(
        attended, tokens, grad_out, attn_out_w, ctrl_w, gain,
        routes.reshape(steps, 1, count // steps), slots.reshape(1, count),
    )


def combine_kernel(
    residual_ref, grad_ref, probs_ref, attended_ref, wo_ref, ctrl_ref, gain_ref, routes_ref,
    slots_ref, back_ref, output_ref, residual_grad_ref, attended_grad_ref, sums_ref, gain_sum,
):
    step = pl.program_id(0)
    gain = gain_ref[...]
    residual = residual_ref[...]
    scaled, inverse = normalise(residual)
    normed = (scaled * gain).astype(bf16)
    probs = probs_ref[...]
    grad = grad_ref[...]
    chosen, onehot, own = choose(probs, routes_ref[0])
    shape = (chosen.shape[1], back_ref.shape[0])
    collect = (lax.broadcasted_iota(jnp.int32, shape, 1) == slots_ref[...]).astype(bf16)
    rows = product(collect, back_ref[...]).astype(bf16)
    results = rows[:, :D]
    mixed_grad = rows[:, D:]
    output_ref[...] = (residual + product(chosen, results)).astype(bf16)
    chosen_grad = jnp.where(own, against_rows(grad, results) + against_rows(normed, mixed_grad), 0.0)
    high = chosen_grad.astype(bf16)
    low = (chosen_grad - high.astype(f32)).astype(bf16)
    prob_grad = against_rows(high, onehot) + against_rows(low, onehot)
    weighted = (probs * prob_grad).reshape(CHUNK // GROUP, GROUP, LANES)
    total = jnp.broadcast_to(jnp.sum(weighted, axis=1, keepdims=True), weighted.shape)
    logit_grad = (probs * (prob_grad - total.reshape(CHUNK, LANES))).astype(bf16)
    normed_grad = product(chosen, mixed_grad) + against_rows(logit_grad, ctrl_ref[...])
    gain_part = jnp.sum(normed_grad * scaled, axis=0, keepdims=True)
    residual_grad = grad.astype(f32) + norm_input_grad(normed_grad, scaled, inverse, gain)
    residual_grad_ref[...] = residual_grad
    branch = residual_grad.astype(bf16)
    attended_grad_ref[...] = against_rows(branch, wo_ref[...]).astype(bf16)
    wo_part = transposed_product(attended_ref[...], branch)
    ctrl_part = transposed_product(normed, logit_grad)

    @pl.when(step == 0)
    def _():
        sums_ref[:, :D] = wo_part
        sums_ref[:, D:] = ctrl_part
        gain_sum[...] = gain_part

    @pl.when(step > 0)
    def _():
        sums_ref[:, :D] = sums_ref[:, :D] + wo_part
        sums_ref[:, D:] = sums_ref[:, D:] + ctrl_part
        gain_sum[...] = gain_sum[...] + gain_part

    @pl.when(step == pl.num_programs(0) - 1)
    def _():
        column = jnp.broadcast_to(gain_sum[...], (LANES, D)).T
        lane = lax.broadcasted_iota(jnp.int32, (D, LANES), 1)
        sums_ref[:, D:] = jnp.where(lane == LANES - 1, column, sums_ref[:, D:])


def combine(residual, grad_out, probs, attended, attn_out_w, ctrl_w, gain, routes, slots, back):
    length = residual.shape[0]
    steps = length // CHUNK
    count = slots.shape[0]
    return call(
        combine_kernel,
        steps,
        [leading(CHUNK, D), leading(CHUNK, D), leading(CHUNK, LANES), leading(CHUNK, D)]
        + [fixed(D, D), fixed(D, LANES), fixed(1, D), leading(1, 1, count // steps)]
        + [leading(count // steps, 1), fixed(*back.shape)],
        [leading(CHUNK, D)] * 3 + [fixed(D, D + LANES)],
        [
            jax.ShapeDtypeStruct((length, D), bf16),
            jax.ShapeDtypeStruct((length, D), f32),
            jax.ShapeDtypeStruct((length, D), bf16),
            jax.ShapeDtypeStruct((D, D + LANES), f32),
        ],
        [pltpu.VMEM((1, D), f32)],
        6 * length * D * D,
        24 * 2**20,
        "combine",
    )(
        residual, grad_out, probs, attended, attn_out_w, ctrl_w, gain,
        routes.reshape(steps, 1, count // steps), slots.reshape(count, 1), back,
    )


def weight_grad_kernel(normed_ref, q_ref, k_ref, v_ref, sums_ref, out_ref):
    out_ref[:, 3 * D :] = sums_ref[...]
    normed_t = normed_ref[...].T
    for i, ref in enumerate((q_ref, k_ref, v_ref)):
        out_ref[:, i * D : (i + 1) * D] = product(normed_t, ref[...])


def weight_grads(normed, query_grad, key_grad, value_grad, sums):
    length = normed.shape[0]
    width = sums.shape[1]
    return call(
        weight_grad_kernel,
        1,
        [fixed(length, D)] * 4 + [fixed(D, width)],
        fixed(D, 3 * D + width),
        jax.ShapeDtypeStruct((D, 3 * D + width), f32),
        [],
        6 * length * D * D,
        12 * 2**20,
        "weight_grads",
    )(normed, query_grad, key_grad, value_grad, sums)


def input_grad_kernel(q_ref, k_ref, v_ref, w_ref, tokens_ref, residual_grad_ref, gain_ref, out_ref):
    upstream = against_rows(q_ref[...], w_ref[:, :D])
    upstream = upstream + against_rows(k_ref[...], w_ref[:, D : 2 * D])
    upstream = upstream + against_rows(v_ref[...], w_ref[:, 2 * D :])
    scaled, inverse = normalise(tokens_ref[...].astype(f32))
    out_ref[...] = (
        residual_grad_ref[...] + norm_input_grad(upstream, scaled, inverse, gain_ref[...])
    ).astype(bf16)


def input_grads(query_grad, key_grad, value_grad, qkv_w, tokens, residual_grad, gain):
    length = tokens.shape[0]
    return call(
        input_grad_kernel,
        length // CHUNK,
        [leading(CHUNK, D)] * 3
        + [fixed(D, 3 * D), leading(CHUNK, D), leading(CHUNK, D), fixed(1, D)],
        leading(CHUNK, D),
        jax.ShapeDtypeStruct((length, D), bf16),
        [],
        6 * length * D * D,
        18 * 2**20,
        "input_grads",
    )(query_grad, key_grad, value_grad, qkv_w, tokens, residual_grad, gain)


def swap(block, axis, bits):
    size = lax.axis_size(axis)
    return lax.ppermute(block, axis, [(i, i ^ bits) for i in range(size)])


def gather_shard(block):
    n_shard = lax.axis_size("shard")
    here = lax.axis_index("shard")
    rows, width = block.shape
    held = jnp.zeros((n_shard, rows, width), block.dtype)
    held = lax.dynamic_update_slice(held, block[None], (here, 0, 0))
    for k in range(1, n_shard):
        held = lax.dynamic_update_slice(held, swap(block, "shard", k)[None], (here ^ k, 0, 0))
    return held.reshape(n_shard * rows, width)


def gather_expert(held):
    n_expert = lax.axis_size("expert")
    mine = lax.axis_index("expert")
    rows, width = held.shape
    bit = n_expert // 2
    steps = 0
    while bit:
        got = swap(held, "expert", bit)
        low = (mine & bit) == 0
        held = jnp.stack([jnp.where(low, held, got), jnp.where(low, got, held)])
        bit //= 2
        steps += 1
    order = tuple(range(steps - 1, -1, -1)) + (steps, steps + 1)
    return held.transpose(order).reshape(n_expert * rows, width)


def scatter_sum(partial):
    n_shard = lax.axis_size("shard")
    n_expert = lax.axis_size("expert")
    mine = lax.axis_index("expert")
    here = lax.axis_index("shard")
    width = partial.shape[1]
    steps = n_expert.bit_length() - 1
    held = partial.reshape((2,) * steps + (-1, width))
    for step in range(steps):
        bit = 1 << step
        axis = steps - 1 - step
        high = (mine & bit) >> step
        away = lax.dynamic_index_in_dim(held, high ^ 1, axis, keepdims=False).astype(bf16)
        kept = lax.dynamic_index_in_dim(held, high, axis, keepdims=False)
        held = kept + swap(away, "expert", bit).astype(f32)
    pieces = held.reshape(n_shard, -1, width)
    low = pieces.astype(bf16)
    total = lax.dynamic_index_in_dim(pieces, here, 0, keepdims=False)
    for k in range(1, n_shard):
        away = lax.dynamic_index_in_dim(low, here ^ k, 0, keepdims=False)
        total = total + swap(away, "shard", k).astype(f32)
    return total


def to_experts(array, copies):
    if copies > 1:
        array = jnp.repeat(array, copies, axis=0)
    return lax.all_to_all(array, "shard", split_axis=0, concat_axis=0, tiled=True)


def from_experts(array, copies):
    back = lax.all_to_all(array, "shard", split_axis=0, concat_axis=0, tiled=True)
    if copies > 1:
        back = back.astype(f32).reshape((-1, copies) + back.shape[1:]).sum(axis=1)
    return back


def exchange(rows, copies):
    n_expert = lax.axis_size("expert")
    n_shard = lax.axis_size("shard")
    groups = None
    if copies > 1:
        groups = [
            [e * n_shard + s for e in range(n_expert) for s in range(p, n_shard, copies)]
            for p in range(copies)
        ]
    return lax.all_to_all(
        rows, BOTH, split_axis=0, concat_axis=0, tiled=True, axis_index_groups=groups
    )


def slots_of(routes, experts):
    groups = routes.shape[0]
    named = (routes[:, :, None] == jnp.arange(experts, dtype=jnp.int32)[None, None, :]).astype(f32)
    earlier = jnp.tril(jnp.ones((groups, groups), f32), -1).astype(bf16)
    before = product(earlier, jnp.sum(named, axis=1).astype(bf16))
    rank = jnp.sum(named * before[:, None, :], axis=2).astype(jnp.int32)
    return (routes * CAP + rank).reshape(-1)


def body(
    tokens,
    ln1_gain,
    ln2_gain,
    w_query,
    w_key,
    w_value,
    w_attn_out,
    w_ctrl,
    w_in,
    b_in,
    w_exp_out,
    routes,
    grad_out,
):
    experts = w_ctrl.shape[1]
    copies = lax.axis_size("shard") * lax.axis_size("expert") // experts
    block = w_query.shape[0]
    slots = slots_of(routes, experts)

    gain_lanes = jnp.zeros((block, LANES - 1), f32)
    first_small = jnp.concatenate(
        [w_query, w_key, w_value, ln1_gain[:, None], gain_lanes], axis=1
    ).astype(bf16)
    second_small = jnp.concatenate(
        [w_attn_out, w_ctrl, ln2_gain[:, None], gain_lanes[:, experts:]], axis=1
    ).astype(bf16)
    packed = pack_weights(w_in, b_in, w_exp_out)
    held = gather_shard(first_small)
    held, packed, second_small = lax.optimization_barrier((held, packed, second_small))
    expert_w = to_experts(packed, copies)
    held = gather_expert(held)
    qkv_w = held[:, : 3 * D]
    gain_one = held[:, 3 * D].astype(f32).reshape(1, D)

    held = gather_expert(gather_shard(second_small))
    attn_out_w = held[:, :D]
    ctrl_w = held[:, D:]
    gain_two = held[:, D + experts].astype(f32).reshape(1, D)

    qkv, normed_one = project(tokens, qkv_w, gain_one)
    attended, lse = attention_forward(qkv)
    residual, probs, outgoing = mix(
        attended, tokens, grad_out, attn_out_w, ctrl_w, gain_two, routes, slots, experts * CAP
    )
    outgoing, expert_w = lax.optimization_barrier((outgoing, expert_w))
    arrived = exchange(outgoing, copies)
    results, active, pre_grad = expert_rows(arrived, expert_w)
    returned = exchange(results, copies)
    expert_sums = expert_grads(arrived, active, pre_grad)
    returned, expert_sums = lax.optimization_barrier((returned, expert_sums))
    w_in_grad, b_in_grad, w_exp_out_grad = unpack_grads(from_experts(expert_sums, copies))
    output, residual_grad, attended_grad, sums = combine(
        residual, grad_out, probs, attended, attn_out_w, ctrl_w, gain_two, routes, slots, returned
    )
    query_grad, key_grad, value_grad = attention_backward(qkv, attended_grad, attended, lse)
    late = scatter_sum(weight_grads(normed_one, query_grad, key_grad, value_grad, sums))
    input_grad = input_grads(
        query_grad, key_grad, value_grad, qkv_w, tokens, residual_grad, gain_one
    )
    own = first_small.astype(f32)
    ln1_grad = jnp.sum(late[:, : 3 * D] * own[:, : 3 * D], axis=1) / own[:, 3 * D]
    early = late[:, 3 * D :]
    return (
        output,
        input_grad,
        ln1_grad,
        early[:, D + LANES - 1],
        late[:, :D],
        late[:, D : 2 * D],
        late[:, 2 * D : 3 * D],
        early[:, :D],
        early[:, D : D + experts],
        w_in_grad,
        b_in_grad,
        w_exp_out_grad,
    )


def solution(mesh):
    rows = P(BOTH, None)
    vector = P(BOTH)
    experts = (P("expert", None, "shard"), P("expert", "shard"), P("expert", "shard", None))
    in_specs = (rows, vector, vector) + (rows,) * 5 + experts + (rows, rows)
    out_specs = (rows, rows, vector, vector) + (rows,) * 5 + experts
    return jax.shard_map(body, mesh=mesh, in_specs=in_specs, out_specs=out_specs, check_vma=False)
```

```python
import jax
import jax.numpy as jnp
from jax import lax
from jax.experimental import pallas as pl
from jax.experimental.pallas import tpu as pltpu
from jax.sharding import PartitionSpec as P

D = 512
HEAD_DIM = 64
GROUP = 32
ROUTES = 8
BLOCK = 256
CAP = 24
EPSILON = 1e-05
SCALE = 0.125 * 1.4426950408889634
BOTH = ("expert", "shard")

bf16 = jnp.bfloat16
f32 = jnp.float32
VMEM = pltpu.CompilerParams(vmem_limit_bytes=56 * 2**20)


def product(left_op, right_op):
    return jnp.dot(left_op, right_op, preferred_element_type=f32)


def transposed_product(left_op, right_op):
    return lax.dot_general(left_op, right_op, (((0,), (0,)), ((), ())), preferred_element_type=f32)


def against_rows(left_op, right_op):
    return lax.dot_general(left_op, right_op, (((1,), (1,)), ((), ())), preferred_element_type=f32)


def attention_forward_kernel(q_ref, k_ref, v_ref, o_ref, lse_ref):
    length = q_ref.shape[0]
    q_t = q_ref[...].T
    v_t = v_ref[...].T
    zero = jnp.zeros((HEAD_DIM, BLOCK), bf16)
    ones = jnp.ones((16, length), bf16)
    for b in range(length // BLOCK):
        n = (b + 1) * BLOCK
        cols = slice(b * BLOCK, n)
        q_b = q_t[:, cols]
        keys = k_ref[:n, :]
        outs = []
        for h in range(2):
            half = q_b[h * HEAD_DIM : (h + 1) * HEAD_DIM]
            scores = product(keys, jnp.concatenate([half, zero] if h == 0 else [zero, half], 0))
            top = jnp.max(scores, axis=0, keepdims=True)
            weights = jnp.exp2(scores * SCALE - top * SCALE).astype(bf16)
            values = jnp.concatenate([v_t[h * HEAD_DIM : (h + 1) * HEAD_DIM, :n], ones[:, :n]], 0)
            out = product(values, weights)
            total = out[HEAD_DIM : HEAD_DIM + 1]
            outs.append(out[:HEAD_DIM] / total)
            lse_ref[0, h : h + 1, cols] = top * SCALE + jnp.log2(total)
        o_ref[cols, :] = jnp.concatenate(outs, 0).T.astype(bf16)


def attention_backward_kernel(
    q_ref, k_ref, v_ref, g_ref, o_ref, lse_ref, dq_ref, dk_ref, dv_ref, dq_t
):
    length = q_ref.shape[0]
    q = q_ref[...]
    g = g_ref[...]
    q_t = q.T
    g_t = g.T
    k_t = k_ref[...].T
    both = (g.astype(f32) * o_ref[...].astype(f32)).T
    lane = lax.broadcasted_iota(jnp.int32, (1, 2 * HEAD_DIM), 1)
    zero = jnp.zeros((HEAD_DIM, length), bf16)
    heads = []
    for h in range(2):
        rows = slice(h * HEAD_DIM, (h + 1) * HEAD_DIM)
        mine = (lane < HEAD_DIM) if h == 0 else (lane >= HEAD_DIM)
        heads.append(
            (
                rows,
                jnp.concatenate([q_t[rows], zero] if h == 0 else [zero, q_t[rows]], 0),
                jnp.concatenate([g_t[rows], zero] if h == 0 else [zero, g_t[rows]], 0),
                jnp.where(mine, q, 0).astype(bf16),
                jnp.where(mine, g, 0).astype(bf16),
                jnp.sum(both[rows], axis=0, keepdims=True),
                lse_ref[0, h : h + 1, :],
            )
        )
    for j in range(length // BLOCK):
        lo = j * BLOCK
        here = slice(lo, lo + BLOCK)
        keys = k_ref[here, :]
        values = v_ref[here, :]
        key_grad = jnp.zeros((BLOCK, 2 * HEAD_DIM), f32)
        value_grad = jnp.zeros((BLOCK, 2 * HEAD_DIM), f32)
        for rows, q_side, g_side, q_mine, g_mine, delta, lse in heads:
            shares = jnp.exp2(product(keys, q_side[:, lo:]) * SCALE - lse[:, lo:])
            share_grad = product(values, g_side[:, lo:])
            score_grad = (shares * (share_grad - delta[:, lo:])).astype(bf16)
            value_grad = value_grad + product(shares.astype(bf16), g_mine[lo:])
            key_grad = key_grad + product(score_grad, q_mine[lo:])
            query_part = product(k_t[rows, here], score_grad)
            if j == 0:
                dq_t[rows, :] = query_part
            else:
                dq_t[rows, lo:] = dq_t[rows, lo:] + query_part
        dk_ref[here, :] = (key_grad * 0.125).astype(bf16)
        dv_ref[here, :] = value_grad.astype(bf16)
    dq_ref[...] = (dq_t[...] * 0.125).T.astype(bf16)


def pair_columns(length, offset):
    return pl.BlockSpec((length, 2 * HEAD_DIM), lambda pair: (0, pair + offset))


def attention_forward(qkv):
    length = qkv.shape[0]
    pairs = D // (2 * HEAD_DIM)
    stats = pl.BlockSpec((1, 2, length), lambda pair: (pair, 0, 0))
    return pl.pallas_call(
        attention_forward_kernel,
        grid=(pairs,),
        in_specs=[pair_columns(length, i * pairs) for i in range(3)],
        out_specs=[pair_columns(length, 0), stats],
        out_shape=[
            jax.ShapeDtypeStruct((length, D), bf16),
            jax.ShapeDtypeStruct((pairs, 2, length), f32),
        ],
        compiler_params=VMEM,
        cost_estimate=pl.CostEstimate(
            flops=40_000_000_000, bytes_accessed=8 * 2**20, transcendentals=20_000_000
        ),
        name="attention_forward",
    )(qkv, qkv, qkv)


def attention_backward(qkv, grad, attended, lse):
    length = qkv.shape[0]
    pairs = D // (2 * HEAD_DIM)
    stats = pl.BlockSpec((1, 2, length), lambda pair: (pair, 0, 0))
    return pl.pallas_call(
        attention_backward_kernel,
        grid=(pairs,),
        in_specs=[pair_columns(length, i * pairs) for i in range(3)]
        + [pair_columns(length, 0), pair_columns(length, 0), stats],
        out_specs=[pair_columns(length, 0)] * 3,
        out_shape=[jax.ShapeDtypeStruct((length, D), bf16)] * 3,
        scratch_shapes=[pltpu.VMEM((2 * HEAD_DIM, length), f32)],
        compiler_params=VMEM,
        cost_estimate=pl.CostEstimate(
            flops=50_000_000_000, bytes_accessed=16 * 2**20, transcendentals=20_000_000
        ),
        name="attention_backward",
    )(qkv, qkv, qkv, grad, attended, lse)


CHUNK = 256
LANES = 128
BIAS_ROWS = 16
GAIN_ONE = LANES - 2
GAIN_TWO = LANES - 1


def call(kernel, grid, in_specs, out_specs, out_shape, scratch, flops, moved, name):
    return pl.pallas_call(
        kernel,
        grid=(grid,),
        in_specs=in_specs,
        out_specs=out_specs,
        out_shape=out_shape,
        scratch_shapes=scratch,
        compiler_params=VMEM,
        cost_estimate=pl.CostEstimate(flops=flops, bytes_accessed=moved, transcendentals=0),
        name=name,
    )


def fixed(*shape):
    return pl.BlockSpec(shape, lambda i: (0,) * len(shape))


def small_columns(width, start):
    return pl.BlockSpec((D, width), lambda i: (0, start // width))


def leading(*shape):
    return pl.BlockSpec(shape, lambda i: (i,) + (0,) * (len(shape) - 1))


def normalise(matrix):
    average = jnp.mean(matrix, axis=1, keepdims=True)
    centered = matrix - average
    inverse = lax.rsqrt(jnp.mean(centered * centered, axis=1, keepdims=True) + EPSILON)
    return centered * inverse, inverse


def norm_input_grad(upstream, scaled, inverse, gain):
    adjusted = upstream * gain
    first_mean = jnp.mean(adjusted, axis=1, keepdims=True)
    second_mean = jnp.mean(adjusted * scaled, axis=1, keepdims=True)
    return inverse * (adjusted - first_mean - scaled * second_mean)


def small_kernel(q_ref, k_ref, v_ref, o_ref, ctrl_ref, one_ref, two_ref, out_ref):
    rows, experts = ctrl_ref.shape
    for i, ref in enumerate((q_ref, k_ref, v_ref, o_ref)):
        out_ref[:, i * D : (i + 1) * D] = ref[...].astype(bf16)
    square = (rows, rows)
    own = lax.broadcasted_iota(jnp.int32, square, 0) == lax.broadcasted_iota(jnp.int32, square, 1)
    one = jnp.sum(jnp.where(own, one_ref[...], 0.0), axis=1, keepdims=True)
    two = jnp.sum(jnp.where(own, two_ref[...], 0.0), axis=1, keepdims=True)
    lane = lax.broadcasted_iota(jnp.int32, (rows, LANES), 1)
    out_ref[:, 4 * D :] = jnp.where(lane == GAIN_ONE, one, jnp.where(lane == GAIN_TWO, two, 0.0)).astype(bf16)
    out_ref[:, 4 * D : 4 * D + experts] = ctrl_ref[...].astype(bf16)


def pack_small(weights, ctrl, gain_one, gain_two):
    rows, experts = ctrl.shape
    width = 4 * D + LANES
    return call(
        small_kernel,
        1,
        [fixed(rows, D)] * 4 + [fixed(rows, experts), fixed(1, rows), fixed(1, rows)],
        fixed(rows, width),
        jax.ShapeDtypeStruct((rows, width), bf16),
        [],
        100_000,
        200_000,
        "pack_small",
    )(*weights, ctrl, gain_one.reshape(1, rows), gain_two.reshape(1, rows))


def gain_of(ctrl_block, lane):
    pick = (lax.broadcasted_iota(jnp.int32, (16, LANES), 1) == lane).astype(bf16)
    return against_rows(pick, ctrl_block)[:1]


def pack_kernel(first_ref, bias_ref, second_ref, out_ref):
    hidden = first_ref.shape[2]
    out_ref[0, :D, :] = first_ref[0].astype(bf16)
    out_ref[0, D : D + BIAS_ROWS, :] = jnp.broadcast_to(bias_ref[0], (BIAS_ROWS, hidden)).astype(bf16)
    for c in range(D // hidden):
        start = D + BIAS_ROWS + c * hidden
        out_ref[0, start : start + hidden, :] = second_ref[
            0, :, c * hidden : (c + 1) * hidden
        ].astype(bf16)


def pack_weights(w_in, b_in, w_exp_out):
    local, _, hidden = w_in.shape
    total = 2 * D + BIAS_ROWS
    return call(
        pack_kernel,
        local,
        [leading(1, D, hidden), leading(1, 1, hidden), leading(1, hidden, D)],
        leading(1, total, hidden),
        jax.ShapeDtypeStruct((local, total, hidden), bf16),
        [],
        1_000_000,
        12 * 2**20,
        "pack_weights",
    )(w_in, b_in[:, None, :], w_exp_out)


def unpack_kernel(in_ref, first_ref, bias_ref, second_ref):
    hidden = first_ref.shape[2]
    first_ref[0] = in_ref[0, :D, :].astype(f32)
    bias_ref[0] = in_ref[0, D : D + BIAS_ROWS, :].astype(f32)[:1]
    for c in range(D // hidden):
        start = D + BIAS_ROWS + c * hidden
        second_ref[0, :, c * hidden : (c + 1) * hidden] = in_ref[
            0, start : start + hidden, :
        ].astype(f32)


def unpack_grads(packed):
    local, total, hidden = packed.shape
    first, bias, second = call(
        unpack_kernel,
        local,
        [leading(1, total, hidden)],
        [leading(1, D, hidden), leading(1, 1, hidden), leading(1, hidden, D)],
        [
            jax.ShapeDtypeStruct((local, D, hidden), f32),
            jax.ShapeDtypeStruct((local, 1, hidden), f32),
            jax.ShapeDtypeStruct((local, hidden, D), f32),
        ],
        [],
        1_000_000,
        12 * 2**20,
        "unpack_grads",
    )(packed)
    return first, bias[:, 0, :], second


def expert_kernel(rows_ref, w_ref, out_ref, active_ref, pre_grad_ref, results, mixed_grad):
    step = pl.program_id(0)
    hidden = w_ref.shape[2]
    first = w_ref[0, :D, :]
    bias = w_ref[0, D : D + BIAS_ROWS, :].astype(f32)[:1]
    pre_act = product(rows_ref[:, :D], first) + bias
    sigma = 1.0 / (1.0 + jnp.exp(-pre_act))
    active = (pre_act * sigma).astype(bf16)
    active_ref[0] = active
    hidden_grad = jnp.zeros_like(pre_act)
    parts = []
    for c in range(D // hidden):
        start = D + BIAS_ROWS + c * hidden
        second = w_ref[0, start : start + hidden, :]
        cols = slice(D + c * hidden, D + (c + 1) * hidden)
        hidden_grad = hidden_grad + against_rows(rows_ref[:, cols], second)
        parts.append(product(active, second))
    pre_grad = (
        hidden_grad.astype(bf16).astype(f32) * (sigma * (1.0 + pre_act * (1.0 - sigma)))
    ).astype(bf16)
    pre_grad_ref[0] = pre_grad
    back = against_rows(pre_grad, first)

    @pl.when(step == 0)
    def _():
        for c, part in enumerate(parts):
            results[:, c * hidden : (c + 1) * hidden] = part
        mixed_grad[...] = back

    @pl.when(step > 0)
    def _():
        for c, part in enumerate(parts):
            cols = slice(c * hidden, (c + 1) * hidden)
            results[:, cols] = results[:, cols] + part
        mixed_grad[...] = mixed_grad[...] + back

    @pl.when(step == pl.num_programs(0) - 1)
    def _():
        out_ref[:, :D] = results[...].astype(bf16)
        out_ref[:, D:] = mixed_grad[...].astype(bf16)


def expert_rows(rows, weights):
    count = rows.shape[0]
    shards, total, hidden = weights.shape
    per_shard = jax.ShapeDtypeStruct((shards, count, hidden), bf16)
    return call(
        expert_kernel,
        shards,
        [fixed(count, 2 * D), leading(1, total, hidden)],
        [fixed(count, 2 * D), leading(1, count, hidden), leading(1, count, hidden)],
        [jax.ShapeDtypeStruct((count, 2 * D), bf16), per_shard, per_shard],
        [pltpu.VMEM((count, D), f32), pltpu.VMEM((count, D), f32)],
        8 * count * D * shards * hidden,
        14 * 2**20,
        "expert_rows",
    )(rows, weights)


def expert_grad_kernel(rows_ref, active_ref, pre_grad_ref, out_ref, rows_t):
    hidden = out_ref.shape[2]

    @pl.when(pl.program_id(0) == 0)
    def _():
        rows_t[...] = rows_ref[:, :D].T

    pre_grad = pre_grad_ref[0]
    out_ref[0, :D, :] = product(rows_t[...], pre_grad).astype(bf16)
    out_ref[0, D : D + BIAS_ROWS, :] = jnp.broadcast_to(
        jnp.sum(pre_grad.astype(f32), axis=0, keepdims=True), (BIAS_ROWS, hidden)
    ).astype(bf16)
    active_t = active_ref[0].T
    for c in range(D // hidden):
        start = D + BIAS_ROWS + c * hidden
        out_ref[0, start : start + hidden, :] = product(
            active_t, rows_ref[:, D + c * hidden : D + (c + 1) * hidden]
        ).astype(bf16)


def expert_grads(rows, active, pre_grad):
    count = rows.shape[0]
    shards, _, hidden = active.shape
    total = 2 * D + BIAS_ROWS
    return call(
        expert_grad_kernel,
        shards,
        [fixed(count, 2 * D), leading(1, count, hidden), leading(1, count, hidden)],
        leading(1, total, hidden),
        jax.ShapeDtypeStruct((shards, total, hidden), bf16),
        [pltpu.VMEM((D, count), bf16)],
        4 * count * D * shards * hidden,
        14 * 2**20,
        "expert_grads",
    )(rows, active, pre_grad)


def project_kernel(tokens_ref, w_ref, ctrl_ref, qkv_ref, normed_ref):
    scaled, _ = normalise(tokens_ref[...].astype(f32))
    normed = (scaled * gain_of(ctrl_ref[...], GAIN_ONE)).astype(bf16)
    normed_ref[...] = normed
    qkv_ref[...] = product(normed, w_ref[...]).astype(bf16)


def project(tokens, small):
    length = tokens.shape[0]
    return call(
        project_kernel,
        length // CHUNK,
        [leading(CHUNK, D), small_columns(3 * D, 0), small_columns(LANES, 4 * D)],
        [leading(CHUNK, 3 * D), leading(CHUNK, D)],
        [jax.ShapeDtypeStruct((length, 3 * D), bf16), jax.ShapeDtypeStruct((length, D), bf16)],
        [],
        6 * length * D * D,
        12 * 2**20,
        "project",
    )(tokens, small, small)


def choose(probs, routes):
    columns = routes.shape[1]
    shape = (LANES, columns)
    onehot = (lax.broadcasted_iota(jnp.int32, shape, 0) == routes).astype(bf16)
    tokens = probs.shape[0]
    own = lax.broadcasted_iota(jnp.int32, (tokens, columns), 0) // GROUP == (
        lax.broadcasted_iota(jnp.int32, (tokens, columns), 1) // ROUTES
    )
    chosen = jnp.where(own, product(probs.astype(bf16), onehot), 0.0).astype(bf16)
    return chosen, onehot, own


def mix_kernel(
    attended_ref, tokens_ref, grad_ref, wo_ref, ctrl_ref, routes_ref, slots_ref,
    residual_ref, probs_ref, out_ref, rows,
):
    step = pl.program_id(0)
    residual = tokens_ref[...].astype(f32) + product(attended_ref[...], wo_ref[...])
    residual_ref[...] = residual
    scaled, _ = normalise(residual)
    normed = (scaled * gain_of(ctrl_ref[...], GAIN_TWO)).astype(bf16)
    logits = product(normed, ctrl_ref[...]).reshape(CHUNK // GROUP, GROUP, LANES)
    weights = jnp.exp(logits - jnp.max(logits, axis=1, keepdims=True))
    probs = (weights / jnp.sum(weights, axis=1, keepdims=True)).reshape(CHUNK, LANES)
    probs_ref[...] = probs
    chosen, _, _ = choose(probs, routes_ref[0])
    columns = chosen.shape[1]
    here = pl.ds(pl.multiple_of(step * columns, columns), columns)
    rows[here, :D] = transposed_product(chosen, normed).astype(bf16)
    rows[here, D:] = transposed_product(chosen, grad_ref[...]).astype(bf16)

    @pl.when(step == pl.num_programs(0) - 1)
    def _():
        shape = (out_ref.shape[0], rows.shape[0])
        dispatch = (lax.broadcasted_iota(jnp.int32, shape, 0) == slots_ref[...]).astype(bf16)
        out_ref[...] = product(dispatch, rows[...]).astype(bf16)


def mix(attended, tokens, grad_out, small, routes, slots, slot_count):
    length = tokens.shape[0]
    steps = length // CHUNK
    count = slots.shape[0]
    return call(
        mix_kernel,
        steps,
        [leading(CHUNK, D)] * 3
        + [small_columns(D, 3 * D), small_columns(LANES, 4 * D)]
        + [leading(1, 1, count // steps), fixed(1, count)],
        [leading(CHUNK, D), leading(CHUNK, LANES), fixed(slot_count, 2 * D)],
        [
            jax.ShapeDtypeStruct((length, D), f32),
            jax.ShapeDtypeStruct((length, LANES), f32),
            jax.ShapeDtypeStruct((slot_count, 2 * D), bf16),
        ],
        [pltpu.VMEM((count, 2 * D), bf16)],
        4 * length * D * D,
        14 * 2**20,
        "mix",
    )(
        attended, tokens, grad_out, small, small,
        routes.reshape(steps, 1, count // steps), slots.reshape(1, count),
    )


def combine_kernel(
    residual_ref, grad_ref, probs_ref, attended_ref, wo_ref, ctrl_ref, routes_ref,
    slots_ref, back_ref, output_ref, residual_grad_ref, attended_grad_ref, sums_ref, gain_sum,
):
    step = pl.program_id(0)
    gain = gain_of(ctrl_ref[...], GAIN_TWO)
    residual = residual_ref[...]
    scaled, inverse = normalise(residual)
    normed = (scaled * gain).astype(bf16)
    probs = probs_ref[...]
    grad = grad_ref[...]
    chosen, onehot, own = choose(probs, routes_ref[0])
    shape = (chosen.shape[1], back_ref.shape[0])
    collect = (lax.broadcasted_iota(jnp.int32, shape, 1) == slots_ref[...]).astype(bf16)
    rows = product(collect, back_ref[...]).astype(bf16)
    results = rows[:, :D]
    mixed_grad = rows[:, D:]
    output_ref[...] = (residual + product(chosen, results)).astype(bf16)
    chosen_grad = jnp.where(own, against_rows(grad, results) + against_rows(normed, mixed_grad), 0.0)
    high = chosen_grad.astype(bf16)
    low = (chosen_grad - high.astype(f32)).astype(bf16)
    prob_grad = against_rows(high, onehot) + against_rows(low, onehot)
    weighted = (probs * prob_grad).reshape(CHUNK // GROUP, GROUP, LANES)
    total = jnp.broadcast_to(jnp.sum(weighted, axis=1, keepdims=True), weighted.shape)
    logit_grad = (probs * (prob_grad - total.reshape(CHUNK, LANES))).astype(bf16)
    normed_grad = product(chosen, mixed_grad) + against_rows(logit_grad, ctrl_ref[...])
    gain_part = jnp.sum(normed_grad * scaled, axis=0, keepdims=True)
    residual_grad = grad.astype(f32) + norm_input_grad(normed_grad, scaled, inverse, gain)
    residual_grad_ref[...] = residual_grad
    branch = residual_grad.astype(bf16)
    attended_grad_ref[...] = against_rows(branch, wo_ref[...]).astype(bf16)
    wo_part = transposed_product(attended_ref[...], branch)
    ctrl_part = transposed_product(normed, logit_grad)

    @pl.when(step == 0)
    def _():
        sums_ref[:, :D] = wo_part
        sums_ref[:, D:] = ctrl_part
        gain_sum[...] = gain_part

    @pl.when(step > 0)
    def _():
        sums_ref[:, :D] = sums_ref[:, :D] + wo_part
        sums_ref[:, D:] = sums_ref[:, D:] + ctrl_part
        gain_sum[...] = gain_sum[...] + gain_part

    @pl.when(step == pl.num_programs(0) - 1)
    def _():
        column = jnp.broadcast_to(gain_sum[...], (LANES, D)).T
        lane = lax.broadcasted_iota(jnp.int32, (D, LANES), 1)
        sums_ref[:, D:] = jnp.where(lane == LANES - 1, column, sums_ref[:, D:])


def combine(residual, grad_out, probs, attended, small, routes, slots, back):
    length = residual.shape[0]
    steps = length // CHUNK
    count = slots.shape[0]
    return call(
        combine_kernel,
        steps,
        [leading(CHUNK, D), leading(CHUNK, D), leading(CHUNK, LANES), leading(CHUNK, D)]
        + [small_columns(D, 3 * D), small_columns(LANES, 4 * D), leading(1, 1, count // steps)]
        + [leading(count // steps, 1), fixed(*back.shape)],
        [leading(CHUNK, D)] * 3 + [fixed(D, D + LANES)],
        [
            jax.ShapeDtypeStruct((length, D), bf16),
            jax.ShapeDtypeStruct((length, D), f32),
            jax.ShapeDtypeStruct((length, D), bf16),
            jax.ShapeDtypeStruct((D, D + LANES), f32),
        ],
        [pltpu.VMEM((1, D), f32)],
        6 * length * D * D,
        24 * 2**20,
        "combine",
    )(
        residual, grad_out, probs, attended, small, small,
        routes.reshape(steps, 1, count // steps), slots.reshape(count, 1), back,
    )


def weight_grad_kernel(normed_ref, q_ref, k_ref, v_ref, sums_ref, out_ref):
    out_ref[:, 3 * D :] = sums_ref[...]
    normed_t = normed_ref[...].T
    for i, ref in enumerate((q_ref, k_ref, v_ref)):
        out_ref[:, i * D : (i + 1) * D] = product(normed_t, ref[...])


def weight_grads(normed, query_grad, key_grad, value_grad, sums):
    length = normed.shape[0]
    width = sums.shape[1]
    return call(
        weight_grad_kernel,
        1,
        [fixed(length, D)] * 4 + [fixed(D, width)],
        fixed(D, 3 * D + width),
        jax.ShapeDtypeStruct((D, 3 * D + width), f32),
        [],
        6 * length * D * D,
        12 * 2**20,
        "weight_grads",
    )(normed, query_grad, key_grad, value_grad, sums)


def input_grad_kernel(q_ref, k_ref, v_ref, w_ref, ctrl_ref, tokens_ref, residual_grad_ref, out_ref):
    upstream = against_rows(q_ref[...], w_ref[:, :D])
    upstream = upstream + against_rows(k_ref[...], w_ref[:, D : 2 * D])
    upstream = upstream + against_rows(v_ref[...], w_ref[:, 2 * D :])
    scaled, inverse = normalise(tokens_ref[...].astype(f32))
    gain = gain_of(ctrl_ref[...], GAIN_ONE)
    out_ref[...] = (
        residual_grad_ref[...] + norm_input_grad(upstream, scaled, inverse, gain)
    ).astype(bf16)


def input_grads(query_grad, key_grad, value_grad, small, tokens, residual_grad):
    length = tokens.shape[0]
    return call(
        input_grad_kernel,
        length // CHUNK,
        [leading(CHUNK, D)] * 3
        + [small_columns(3 * D, 0), small_columns(LANES, 4 * D)]
        + [leading(CHUNK, D), leading(CHUNK, D)],
        leading(CHUNK, D),
        jax.ShapeDtypeStruct((length, D), bf16),
        [],
        6 * length * D * D,
        18 * 2**20,
        "input_grads",
    )(query_grad, key_grad, value_grad, small, small, tokens, residual_grad)


def swap(block, axis, bits):
    size = lax.axis_size(axis)
    return lax.ppermute(block, axis, [(i, i ^ bits) for i in range(size)])


def halves(size):
    inner = 1
    while inner * inner * 4 <= size:
        inner *= 2
    return size // inner, inner


def spread(block, size, stride, place):
    held = jnp.zeros((size,) + block.shape, block.dtype)
    held = lax.dynamic_update_slice(held, block[None], (place, 0, 0))
    for k in range(1, size):
        got = swap(block, "shard", k * stride)
        held = lax.dynamic_update_slice(held, got[None], (place ^ k, 0, 0))
    return held.reshape(-1, block.shape[1])


def gather_shard(block):
    outer, inner = halves(lax.axis_size("shard"))
    here = lax.axis_index("shard")
    held = spread(block, inner, 1, here & (inner - 1))
    return spread(held, outer, inner, here >> (inner.bit_length() - 1))


def gather_expert(held):
    n_expert = lax.axis_size("expert")
    mine = lax.axis_index("expert")
    rows, width = held.shape
    bit = n_expert // 2
    steps = 0
    while bit:
        got = swap(held, "expert", bit)
        low = (mine & bit) == 0
        held = jnp.stack([jnp.where(low, held, got), jnp.where(low, got, held)])
        bit //= 2
        steps += 1
    order = tuple(range(steps - 1, -1, -1)) + (steps, steps + 1)
    return held.transpose(order).reshape(n_expert * rows, width)


def sum_expert(partial):
    n_expert = lax.axis_size("expert")
    mine = lax.axis_index("expert")
    width = partial.shape[1]
    steps = n_expert.bit_length() - 1
    held = partial.reshape((2,) * steps + (-1, width))
    for step in range(steps):
        bit = 1 << step
        axis = steps - 1 - step
        high = (mine & bit) >> step
        away = lax.dynamic_index_in_dim(held, high ^ 1, axis, keepdims=False).astype(bf16)
        kept = lax.dynamic_index_in_dim(held, high, axis, keepdims=False)
        held = kept + swap(away, "expert", bit).astype(f32)
    return held


def collect(held, size, stride, place):
    width = held.shape[1]
    pieces = held.reshape(size, -1, width)
    low = pieces.astype(bf16)
    total = lax.dynamic_index_in_dim(pieces, place, 0, keepdims=False)
    for k in range(1, size):
        away = lax.dynamic_index_in_dim(low, place ^ k, 0, keepdims=False)
        total = total + swap(away, "shard", k * stride).astype(f32)
    return total


def sum_shard(held):
    outer, inner = halves(lax.axis_size("shard"))
    here = lax.axis_index("shard")
    held = collect(held, outer, inner, here >> (inner.bit_length() - 1))
    return collect(held, inner, 1, here & (inner - 1))


def to_experts(array, copies):
    if copies > 1:
        array = jnp.repeat(array, copies, axis=0)
    return lax.all_to_all(array, "shard", split_axis=0, concat_axis=0, tiled=True)


def from_experts(array, copies):
    back = lax.all_to_all(array, "shard", split_axis=0, concat_axis=0, tiled=True)
    if copies > 1:
        back = back.astype(f32).reshape((-1, copies) + back.shape[1:]).sum(axis=1)
    return back


def exchange(rows, copies):
    n_expert = lax.axis_size("expert")
    n_shard = lax.axis_size("shard")
    groups = None
    if copies > 1:
        groups = [
            [e * n_shard + s for e in range(n_expert) for s in range(p, n_shard, copies)]
            for p in range(copies)
        ]
    return lax.all_to_all(
        rows, BOTH, split_axis=0, concat_axis=0, tiled=True, axis_index_groups=groups
    )


def slots_of(routes, experts):
    groups = routes.shape[0]
    named = (routes[:, :, None] == jnp.arange(experts, dtype=jnp.int32)[None, None, :]).astype(f32)
    earlier = jnp.tril(jnp.ones((groups, groups), f32), -1).astype(bf16)
    before = product(earlier, jnp.sum(named, axis=1).astype(bf16))
    rank = jnp.sum(named * before[:, None, :], axis=2).astype(jnp.int32)
    return (routes * CAP + rank).reshape(-1)


def body(
    tokens,
    ln1_gain,
    ln2_gain,
    w_query,
    w_key,
    w_value,
    w_attn_out,
    w_ctrl,
    w_in,
    b_in,
    w_exp_out,
    routes,
    grad_out,
):
    experts = w_ctrl.shape[1]
    copies = lax.axis_size("shard") * lax.axis_size("expert") // experts
    slots = slots_of(routes, experts)

    own = pack_small((w_query, w_key, w_value, w_attn_out), w_ctrl, ln1_gain, ln2_gain)
    packed = pack_weights(w_in, b_in, w_exp_out)
    held, packed = lax.optimization_barrier((gather_shard(own), packed))
    expert_w = to_experts(packed, copies)
    small = gather_expert(held)

    qkv, normed_one = project(tokens, small)
    attended, lse = attention_forward(qkv)
    residual, probs, outgoing = mix(
        attended, tokens, grad_out, small, routes, slots, experts * CAP
    )
    outgoing, expert_w = lax.optimization_barrier((outgoing, expert_w))
    arrived = exchange(outgoing, copies)
    results, active, pre_grad = expert_rows(arrived, expert_w)
    returned = exchange(results, copies)
    expert_sums = expert_grads(arrived, active, pre_grad)
    returned, expert_sums = lax.optimization_barrier((returned, expert_sums))
    expert_sums = from_experts(expert_sums, copies)
    output, residual_grad, attended_grad, sums = combine(
        residual, grad_out, probs, attended, small, routes, slots, returned
    )
    query_grad, key_grad, value_grad = attention_backward(qkv, attended_grad, attended, lse)
    late = sum_expert(weight_grads(normed_one, query_grad, key_grad, value_grad, sums))
    input_grad = input_grads(query_grad, key_grad, value_grad, small, tokens, residual_grad)
    late, input_grad, expert_sums = lax.optimization_barrier((late, input_grad, expert_sums))
    late = sum_shard(late)
    w_in_grad, b_in_grad, w_exp_out_grad = unpack_grads(expert_sums)
    products = late[:, : 3 * D] * own[:, : 3 * D].astype(f32)
    ln1_grad = jnp.sum(products, axis=1) / own[:, 4 * D + GAIN_ONE].astype(f32)
    return (
        output,
        input_grad,
        ln1_grad,
        late[:, 4 * D + GAIN_TWO],
        late[:, :D],
        late[:, D : 2 * D],
        late[:, 2 * D : 3 * D],
        late[:, 3 * D : 4 * D],
        late[:, 4 * D : 4 * D + experts],
        w_in_grad,
        b_in_grad,
        w_exp_out_grad,
    )


def solution(mesh):
    rows = P(BOTH, None)
    vector = P(BOTH)
    experts = (P("expert", None, "shard"), P("expert", "shard"), P("expert", "shard", None))
    in_specs = (rows, vector, vector) + (rows,) * 5 + experts + (rows, rows)
    out_specs = (rows, rows, vector, vector) + (rows,) * 5 + experts
    return jax.shard_map(body, mesh=mesh, in_specs=in_specs, out_specs=out_specs, check_vma=False)
```

```python
import jax
import jax.numpy as jnp
from jax import lax
from jax.experimental import pallas as pl
from jax.experimental.pallas import tpu as pltpu
from jax.sharding import PartitionSpec as P

D = 512
HEAD_DIM = 64
GROUP = 32
ROUTES = 8
BLOCK = 256
CAP = 24
EPSILON = 1e-05
SCALE = 0.125 * 1.4426950408889634
BOTH = ("expert", "shard")

bf16 = jnp.bfloat16
f32 = jnp.float32
VMEM = pltpu.CompilerParams(vmem_limit_bytes=56 * 2**20)


def product(left_op, right_op):
    return jnp.dot(left_op, right_op, preferred_element_type=f32)


def transposed_product(left_op, right_op):
    return lax.dot_general(left_op, right_op, (((0,), (0,)), ((), ())), preferred_element_type=f32)


def against_rows(left_op, right_op):
    return lax.dot_general(left_op, right_op, (((1,), (1,)), ((), ())), preferred_element_type=f32)


def attention_forward_kernel(q_ref, k_ref, v_ref, o_ref, lse_ref):
    length = q_ref.shape[0]
    q_t = q_ref[...].T
    v_t = v_ref[...].T
    zero = jnp.zeros((HEAD_DIM, BLOCK), bf16)
    ones = jnp.ones((16, length), bf16)
    for b in range(length // BLOCK):
        n = (b + 1) * BLOCK
        cols = slice(b * BLOCK, n)
        q_b = q_t[:, cols]
        keys = k_ref[:n, :]
        outs = []
        for h in range(2):
            half = q_b[h * HEAD_DIM : (h + 1) * HEAD_DIM]
            scores = product(keys, jnp.concatenate([half, zero] if h == 0 else [zero, half], 0))
            top = jnp.max(scores, axis=0, keepdims=True)
            weights = jnp.exp2(scores * SCALE - top * SCALE).astype(bf16)
            values = jnp.concatenate([v_t[h * HEAD_DIM : (h + 1) * HEAD_DIM, :n], ones[:, :n]], 0)
            out = product(values, weights)
            total = out[HEAD_DIM : HEAD_DIM + 1]
            outs.append(out[:HEAD_DIM] / total)
            lse_ref[0, h : h + 1, cols] = top * SCALE + jnp.log2(total)
        o_ref[cols, :] = jnp.concatenate(outs, 0).T.astype(bf16)


def attention_backward_kernel(
    q_ref, k_ref, v_ref, g_ref, o_ref, lse_ref, dq_ref, dk_ref, dv_ref, dq_t
):
    length = q_ref.shape[0]
    q = q_ref[...]
    g = g_ref[...]
    q_t = q.T
    g_t = g.T
    k_t = k_ref[...].T
    both = (g.astype(f32) * o_ref[...].astype(f32)).T
    lane = lax.broadcasted_iota(jnp.int32, (1, 2 * HEAD_DIM), 1)
    zero = jnp.zeros((HEAD_DIM, length), bf16)
    heads = []
    for h in range(2):
        rows = slice(h * HEAD_DIM, (h + 1) * HEAD_DIM)
        mine = (lane < HEAD_DIM) if h == 0 else (lane >= HEAD_DIM)
        heads.append(
            (
                rows,
                jnp.concatenate([q_t[rows], zero] if h == 0 else [zero, q_t[rows]], 0),
                jnp.concatenate([g_t[rows], zero] if h == 0 else [zero, g_t[rows]], 0),
                jnp.where(mine, q, 0).astype(bf16),
                jnp.where(mine, g, 0).astype(bf16),
                jnp.sum(both[rows], axis=0, keepdims=True),
                lse_ref[0, h : h + 1, :],
            )
        )
    for j in range(length // BLOCK):
        lo = j * BLOCK
        here = slice(lo, lo + BLOCK)
        keys = k_ref[here, :]
        values = v_ref[here, :]
        key_grad = jnp.zeros((BLOCK, 2 * HEAD_DIM), f32)
        value_grad = jnp.zeros((BLOCK, 2 * HEAD_DIM), f32)
        for rows, q_side, g_side, q_mine, g_mine, delta, lse in heads:
            shares = jnp.exp2(product(keys, q_side[:, lo:]) * SCALE - lse[:, lo:])
            share_grad = product(values, g_side[:, lo:])
            score_grad = (shares * (share_grad - delta[:, lo:])).astype(bf16)
            value_grad = value_grad + product(shares.astype(bf16), g_mine[lo:])
            key_grad = key_grad + product(score_grad, q_mine[lo:])
            query_part = product(k_t[rows, here], score_grad)
            if j == 0:
                dq_t[rows, :] = query_part
            else:
                dq_t[rows, lo:] = dq_t[rows, lo:] + query_part
        dk_ref[here, :] = (key_grad * 0.125).astype(bf16)
        dv_ref[here, :] = value_grad.astype(bf16)
    dq_ref[...] = (dq_t[...] * 0.125).T.astype(bf16)


def pair_columns(length, offset):
    return pl.BlockSpec((length, 2 * HEAD_DIM), lambda pair: (0, pair + offset))


def attention_forward(qkv):
    length = qkv.shape[0]
    pairs = D // (2 * HEAD_DIM)
    stats = pl.BlockSpec((1, 2, length), lambda pair: (pair, 0, 0))
    return pl.pallas_call(
        attention_forward_kernel,
        grid=(pairs,),
        in_specs=[pair_columns(length, i * pairs) for i in range(3)],
        out_specs=[pair_columns(length, 0), stats],
        out_shape=[
            jax.ShapeDtypeStruct((length, D), bf16),
            jax.ShapeDtypeStruct((pairs, 2, length), f32),
        ],
        compiler_params=VMEM,
        cost_estimate=pl.CostEstimate(
            flops=40_000_000_000, bytes_accessed=8 * 2**20, transcendentals=20_000_000
        ),
        name="attention_forward",
    )(qkv, qkv, qkv)


def attention_backward(qkv, grad, attended, lse):
    length = qkv.shape[0]
    pairs = D // (2 * HEAD_DIM)
    stats = pl.BlockSpec((1, 2, length), lambda pair: (pair, 0, 0))
    return pl.pallas_call(
        attention_backward_kernel,
        grid=(pairs,),
        in_specs=[pair_columns(length, i * pairs) for i in range(3)]
        + [pair_columns(length, 0), pair_columns(length, 0), stats],
        out_specs=[pair_columns(length, 0)] * 3,
        out_shape=[jax.ShapeDtypeStruct((length, D), bf16)] * 3,
        scratch_shapes=[pltpu.VMEM((2 * HEAD_DIM, length), f32)],
        compiler_params=VMEM,
        cost_estimate=pl.CostEstimate(
            flops=50_000_000_000, bytes_accessed=16 * 2**20, transcendentals=20_000_000
        ),
        name="attention_backward",
    )(qkv, qkv, qkv, grad, attended, lse)


CHUNK = 512
LANES = 128
BIAS_ROWS = 16
SHARDS_A_STEP = 2
GAIN_ONE = LANES - 2
GAIN_TWO = LANES - 1


def call(kernel, grid, in_specs, out_specs, out_shape, scratch, flops, moved, name):
    return pl.pallas_call(
        kernel,
        grid=(grid,),
        in_specs=in_specs,
        out_specs=out_specs,
        out_shape=out_shape,
        scratch_shapes=scratch,
        compiler_params=VMEM,
        cost_estimate=pl.CostEstimate(flops=flops, bytes_accessed=moved, transcendentals=0),
        name=name,
    )


def fixed(*shape):
    return pl.BlockSpec(shape, lambda i: (0,) * len(shape))


def small_columns(width, start):
    return pl.BlockSpec((D, width), lambda i: (0, start // width))


def leading(*shape):
    return pl.BlockSpec(shape, lambda i: (i,) + (0,) * (len(shape) - 1))


def normalise(matrix):
    average = jnp.mean(matrix, axis=1, keepdims=True)
    centered = matrix - average
    inverse = lax.rsqrt(jnp.mean(centered * centered, axis=1, keepdims=True) + EPSILON)
    return centered * inverse, inverse


def norm_input_grad(upstream, scaled, inverse, gain):
    adjusted = upstream * gain
    first_mean = jnp.mean(adjusted, axis=1, keepdims=True)
    second_mean = jnp.mean(adjusted * scaled, axis=1, keepdims=True)
    return inverse * (adjusted - first_mean - scaled * second_mean)


def small_kernel(q_ref, k_ref, v_ref, o_ref, ctrl_ref, one_ref, two_ref, out_ref):
    rows, experts = ctrl_ref.shape
    for i, ref in enumerate((q_ref, k_ref, v_ref, o_ref)):
        out_ref[0, :, i * D : (i + 1) * D] = ref[...].astype(bf16)
    square = (rows, rows)
    own = lax.broadcasted_iota(jnp.int32, square, 0) == lax.broadcasted_iota(jnp.int32, square, 1)
    one = jnp.sum(jnp.where(own, one_ref[...], 0.0), axis=1, keepdims=True)
    two = jnp.sum(jnp.where(own, two_ref[...], 0.0), axis=1, keepdims=True)
    lane = lax.broadcasted_iota(jnp.int32, (rows, LANES), 1)
    gains = jnp.where(lane == GAIN_ONE, one, jnp.where(lane == GAIN_TWO, two, 0.0))
    out_ref[0, :, 4 * D :] = gains.astype(bf16)
    out_ref[0, :, 4 * D : 4 * D + experts] = ctrl_ref[...].astype(bf16)
    for i in range(1, out_ref.shape[0]):
        out_ref[i] = out_ref[0]


def pack_small(weights, ctrl, gain_one, gain_two, copies):
    rows, experts = ctrl.shape
    width = 4 * D + LANES
    return call(
        small_kernel,
        1,
        [fixed(rows, D)] * 4 + [fixed(rows, experts), fixed(1, rows), fixed(1, rows)],
        fixed(copies, rows, width),
        jax.ShapeDtypeStruct((copies, rows, width), bf16),
        [],
        100_000,
        800_000,
        "pack_small",
    )(*weights, ctrl, gain_one.reshape(1, rows), gain_two.reshape(1, rows))


def gain_of(ctrl_block, lane):
    pick = (lax.broadcasted_iota(jnp.int32, (16, LANES), 1) == lane).astype(bf16)
    return against_rows(pick, ctrl_block)[:1]


def pack_kernel(first_ref, bias_ref, second_ref, out_ref):
    hidden = first_ref.shape[2]
    out_ref[0, :D, :] = first_ref[0].astype(bf16)
    out_ref[0, D : D + BIAS_ROWS, :] = jnp.broadcast_to(
        bias_ref[pl.ds(pl.program_id(0), 1), :], (BIAS_ROWS, hidden)
    ).astype(bf16)
    for c in range(D // hidden):
        start = D + BIAS_ROWS + c * hidden
        out_ref[0, start : start + hidden, :] = second_ref[
            0, :, c * hidden : (c + 1) * hidden
        ].astype(bf16)


def pack_weights(w_in, b_in, w_exp_out):
    local, _, hidden = w_in.shape
    total = 2 * D + BIAS_ROWS
    return call(
        pack_kernel,
        local,
        [leading(1, D, hidden), fixed(local, hidden), leading(1, hidden, D)],
        leading(1, total, hidden),
        jax.ShapeDtypeStruct((local, total, hidden), bf16),
        [],
        1_000_000,
        12 * 2**20,
        "pack_weights",
    )(w_in, b_in, w_exp_out)


def unpack_kernel(in_ref, first_ref, bias_ref, second_ref):
    hidden = first_ref.shape[2]
    first_ref[0] = in_ref[0, :D, :].astype(f32)
    bias_ref[pl.ds(pl.program_id(0), 1), :] = in_ref[0, D : D + BIAS_ROWS, :].astype(f32)[:1]
    for c in range(D // hidden):
        start = D + BIAS_ROWS + c * hidden
        second_ref[0, :, c * hidden : (c + 1) * hidden] = in_ref[
            0, start : start + hidden, :
        ].astype(f32)


def unpack_grads(packed):
    local, total, hidden = packed.shape
    return call(
        unpack_kernel,
        local,
        [leading(1, total, hidden)],
        [leading(1, D, hidden), fixed(local, hidden), leading(1, hidden, D)],
        [
            jax.ShapeDtypeStruct((local, D, hidden), f32),
            jax.ShapeDtypeStruct((local, hidden), f32),
            jax.ShapeDtypeStruct((local, hidden, D), f32),
        ],
        [],
        1_000_000,
        12 * 2**20,
        "unpack_grads",
    )(packed)


def expert_part(rows_ref, w_ref, i):
    hidden = w_ref.shape[2]
    first = w_ref[i, :D, :]
    bias = w_ref[i, D : D + BIAS_ROWS, :].astype(f32)[:1]
    pre_act = product(rows_ref[:, :D], first) + bias
    sigma = 0.5 + 0.5 * jnp.tanh(0.5 * pre_act)
    hidden_grad = jnp.zeros_like(pre_act)
    second = []
    for c in range(D // hidden):
        start = D + BIAS_ROWS + c * hidden
        second.append(w_ref[i, start : start + hidden, :])
        cols = slice(D + c * hidden, D + (c + 1) * hidden)
        hidden_grad = hidden_grad + against_rows(rows_ref[:, cols], second[-1])
    active = (pre_act * sigma).astype(bf16)
    pre_grad = (
        hidden_grad.astype(bf16).astype(f32) * (sigma * (1.0 + pre_act * (1.0 - sigma)))
    ).astype(bf16)
    return first, second, active, pre_grad


def expert_kernel(rows_ref, w_ref, out_ref, results, mixed_grad):
    step = pl.program_id(0)
    held, _, hidden = w_ref.shape
    chunks = D // hidden
    parts = [None] * (chunks + 1)
    for i in range(held):
        first, second, active, pre_grad = expert_part(rows_ref, w_ref, i)
        more = [product(active, block) for block in second] + [against_rows(pre_grad, first)]
        parts = more if i == 0 else [old + new for old, new in zip(parts, more)]

    @pl.when(step == 0)
    def _():
        for c in range(chunks):
            results[:, c * hidden : (c + 1) * hidden] = parts[c]
        mixed_grad[...] = parts[chunks]

    @pl.when(step > 0)
    def _():
        for c in range(chunks):
            cols = slice(c * hidden, (c + 1) * hidden)
            results[:, cols] = results[:, cols] + parts[c]
        mixed_grad[...] = mixed_grad[...] + parts[chunks]

    @pl.when(step == pl.num_programs(0) - 1)
    def _():
        out_ref[:, :D] = results[...].astype(bf16)
        out_ref[:, D:] = mixed_grad[...].astype(bf16)


def expert_rows(rows, weights):
    count = rows.shape[0]
    shards, total, hidden = weights.shape
    return call(
        expert_kernel,
        shards // SHARDS_A_STEP,
        [fixed(count, 2 * D), leading(SHARDS_A_STEP, total, hidden)],
        fixed(count, 2 * D),
        jax.ShapeDtypeStruct((count, 2 * D), bf16),
        [pltpu.VMEM((count, D), f32), pltpu.VMEM((count, D), f32)],
        8 * count * D * shards * hidden,
        8 * 2**20,
        "expert_rows",
    )(rows, weights)


def expert_grad_kernel(rows_ref, w_ref, out_ref, rows_t):
    hidden = out_ref.shape[2]

    @pl.when(pl.program_id(0) == 0)
    def _():
        rows_t[...] = rows_ref[:, :D].T

    _, _, active, pre_grad = expert_part(rows_ref, w_ref, 0)
    out_ref[0, :D, :] = product(rows_t[...], pre_grad).astype(bf16)
    out_ref[0, D : D + BIAS_ROWS, :] = jnp.broadcast_to(
        jnp.sum(pre_grad.astype(f32), axis=0, keepdims=True), (BIAS_ROWS, hidden)
    ).astype(bf16)
    active_t = active.T
    for c in range(D // hidden):
        start = D + BIAS_ROWS + c * hidden
        out_ref[0, start : start + hidden, :] = product(
            active_t, rows_ref[:, D + c * hidden : D + (c + 1) * hidden]
        ).astype(bf16)


def expert_grads(rows, weights):
    count = rows.shape[0]
    shards, total, hidden = weights.shape
    return call(
        expert_grad_kernel,
        shards,
        [fixed(count, 2 * D), leading(1, total, hidden)],
        leading(1, total, hidden),
        jax.ShapeDtypeStruct((shards, total, hidden), bf16),
        [pltpu.VMEM((D, count), bf16)],
        8 * count * D * shards * hidden,
        14 * 2**20,
        "expert_grads",
    )(rows, weights)


def project_kernel(tokens_ref, w_ref, ctrl_ref, qkv_ref, normed_ref):
    scaled, _ = normalise(tokens_ref[...].astype(f32))
    normed = (scaled * gain_of(ctrl_ref[...], GAIN_ONE)).astype(bf16)
    normed_ref[...] = normed
    qkv_ref[...] = product(normed, w_ref[...]).astype(bf16)


def project(tokens, small):
    length = tokens.shape[0]
    return call(
        project_kernel,
        length // CHUNK,
        [leading(CHUNK, D), small_columns(3 * D, 0), small_columns(LANES, 4 * D)],
        [leading(CHUNK, 3 * D), leading(CHUNK, D)],
        [jax.ShapeDtypeStruct((length, 3 * D), bf16), jax.ShapeDtypeStruct((length, D), bf16)],
        [],
        6 * length * D * D,
        12 * 2**20,
        "project",
    )(tokens, small, small)


def choose(probs, routes):
    columns = routes.shape[1]
    shape = (LANES, columns)
    onehot = (lax.broadcasted_iota(jnp.int32, shape, 0) == routes).astype(bf16)
    tokens = probs.shape[0]
    own = lax.broadcasted_iota(jnp.int32, (tokens, columns), 0) // GROUP == (
        lax.broadcasted_iota(jnp.int32, (tokens, columns), 1) // ROUTES
    )
    chosen = jnp.where(own, product(probs.astype(bf16), onehot), 0.0).astype(bf16)
    return chosen, onehot, own


def mix_kernel(
    attended_ref, tokens_ref, grad_ref, wo_ref, ctrl_ref, routes_ref, slots_ref,
    residual_ref, probs_ref, out_ref, rows,
):
    step = pl.program_id(0)
    residual = tokens_ref[...].astype(f32) + product(attended_ref[...], wo_ref[...])
    residual_ref[...] = residual
    scaled, _ = normalise(residual)
    normed = (scaled * gain_of(ctrl_ref[...], GAIN_TWO)).astype(bf16)
    logits = product(normed, ctrl_ref[...]).reshape(CHUNK // GROUP, GROUP, LANES)
    weights = jnp.exp(logits - jnp.max(logits, axis=1, keepdims=True))
    probs = (weights / jnp.sum(weights, axis=1, keepdims=True)).reshape(CHUNK, LANES)
    probs_ref[...] = probs
    chosen, _, _ = choose(probs, routes_ref[0])
    columns = chosen.shape[1]
    here = pl.ds(pl.multiple_of(step * columns, columns), columns)
    rows[here, :D] = transposed_product(chosen, normed).astype(bf16)
    rows[here, D:] = transposed_product(chosen, grad_ref[...]).astype(bf16)

    @pl.when(step == pl.num_programs(0) - 1)
    def _():
        shape = (out_ref.shape[0], rows.shape[0])
        dispatch = (lax.broadcasted_iota(jnp.int32, shape, 0) == slots_ref[...]).astype(bf16)
        out_ref[...] = product(dispatch, rows[...]).astype(bf16)


def mix(attended, tokens, grad_out, small, routes, slots, slot_count):
    length = tokens.shape[0]
    steps = length // CHUNK
    count = slots.shape[0]
    return call(
        mix_kernel,
        steps,
        [leading(CHUNK, D)] * 3
        + [small_columns(D, 3 * D), small_columns(LANES, 4 * D)]
        + [leading(1, 1, count // steps), fixed(1, count)],
        [leading(CHUNK, D), leading(CHUNK, LANES), fixed(slot_count, 2 * D)],
        [
            jax.ShapeDtypeStruct((length, D), f32),
            jax.ShapeDtypeStruct((length, LANES), f32),
            jax.ShapeDtypeStruct((slot_count, 2 * D), bf16),
        ],
        [pltpu.VMEM((count, 2 * D), bf16)],
        4 * length * D * D,
        14 * 2**20,
        "mix",
    )(
        attended, tokens, grad_out, small, small,
        routes.reshape(steps, 1, count // steps), slots.reshape(1, count),
    )


def combine_kernel(
    residual_ref, grad_ref, probs_ref, attended_ref, wo_ref, ctrl_ref, routes_ref,
    slots_ref, back_ref, output_ref, residual_grad_ref, attended_grad_ref, sums_ref, gain_sum,
):
    step = pl.program_id(0)
    gain = gain_of(ctrl_ref[...], GAIN_TWO)
    residual = residual_ref[...]
    scaled, inverse = normalise(residual)
    normed = (scaled * gain).astype(bf16)
    probs = probs_ref[...]
    grad = grad_ref[...]
    chosen, onehot, own = choose(probs, routes_ref[0])
    shape = (chosen.shape[1], back_ref.shape[0])
    collect = (lax.broadcasted_iota(jnp.int32, shape, 1) == slots_ref[...]).astype(bf16)
    rows = product(collect, back_ref[...]).astype(bf16)
    results = rows[:, :D]
    mixed_grad = rows[:, D:]
    output_ref[...] = (residual + product(chosen, results)).astype(bf16)
    chosen_grad = jnp.where(own, against_rows(grad, results) + against_rows(normed, mixed_grad), 0.0)
    high = chosen_grad.astype(bf16)
    low = (chosen_grad - high.astype(f32)).astype(bf16)
    prob_grad = against_rows(high, onehot) + against_rows(low, onehot)
    weighted = (probs * prob_grad).reshape(CHUNK // GROUP, GROUP, LANES)
    total = jnp.broadcast_to(jnp.sum(weighted, axis=1, keepdims=True), weighted.shape)
    logit_grad = (probs * (prob_grad - total.reshape(CHUNK, LANES))).astype(bf16)
    normed_grad = product(chosen, mixed_grad) + against_rows(logit_grad, ctrl_ref[...])
    gain_part = jnp.sum(normed_grad * scaled, axis=0, keepdims=True)
    residual_grad = grad.astype(f32) + norm_input_grad(normed_grad, scaled, inverse, gain)
    residual_grad_ref[...] = residual_grad
    branch = residual_grad.astype(bf16)
    attended_grad_ref[...] = against_rows(branch, wo_ref[...]).astype(bf16)
    wo_part = transposed_product(attended_ref[...], branch)
    ctrl_part = transposed_product(normed, logit_grad)

    @pl.when(step == 0)
    def _():
        sums_ref[:, :D] = wo_part
        sums_ref[:, D:] = ctrl_part
        gain_sum[...] = gain_part

    @pl.when(step > 0)
    def _():
        sums_ref[:, :D] = sums_ref[:, :D] + wo_part
        sums_ref[:, D:] = sums_ref[:, D:] + ctrl_part
        gain_sum[...] = gain_sum[...] + gain_part

    @pl.when(step == pl.num_programs(0) - 1)
    def _():
        column = jnp.broadcast_to(gain_sum[...], (LANES, D)).T
        lane = lax.broadcasted_iota(jnp.int32, (D, LANES), 1)
        sums_ref[:, D:] = jnp.where(lane == LANES - 1, column, sums_ref[:, D:])


def combine(residual, grad_out, probs, attended, small, routes, slots, back):
    length = residual.shape[0]
    steps = length // CHUNK
    count = slots.shape[0]
    return call(
        combine_kernel,
        steps,
        [leading(CHUNK, D), leading(CHUNK, D), leading(CHUNK, LANES), leading(CHUNK, D)]
        + [small_columns(D, 3 * D), small_columns(LANES, 4 * D), leading(1, 1, count // steps)]
        + [leading(count // steps, 1), fixed(*back.shape)],
        [leading(CHUNK, D)] * 3 + [fixed(D, D + LANES)],
        [
            jax.ShapeDtypeStruct((length, D), bf16),
            jax.ShapeDtypeStruct((length, D), f32),
            jax.ShapeDtypeStruct((length, D), bf16),
            jax.ShapeDtypeStruct((D, D + LANES), f32),
        ],
        [pltpu.VMEM((1, D), f32)],
        6 * length * D * D,
        24 * 2**20,
        "combine",
    )(
        residual, grad_out, probs, attended, small, small,
        routes.reshape(steps, 1, count // steps), slots.reshape(count, 1), back,
    )


def weight_grad_kernel(normed_ref, q_ref, k_ref, v_ref, sums_ref, out_ref):
    out_ref[:, 3 * D :] = sums_ref[...]
    normed_t = normed_ref[...].T
    for i, ref in enumerate((q_ref, k_ref, v_ref)):
        out_ref[:, i * D : (i + 1) * D] = product(normed_t, ref[...])


def weight_grads(normed, query_grad, key_grad, value_grad, sums):
    length = normed.shape[0]
    width = sums.shape[1]
    return call(
        weight_grad_kernel,
        1,
        [fixed(length, D)] * 4 + [fixed(D, width)],
        fixed(D, 3 * D + width),
        jax.ShapeDtypeStruct((D, 3 * D + width), f32),
        [],
        6 * length * D * D,
        12 * 2**20,
        "weight_grads",
    )(normed, query_grad, key_grad, value_grad, sums)


def input_grad_kernel(q_ref, k_ref, v_ref, w_ref, ctrl_ref, tokens_ref, residual_grad_ref, out_ref):
    upstream = against_rows(q_ref[...], w_ref[:, :D])
    upstream = upstream + against_rows(k_ref[...], w_ref[:, D : 2 * D])
    upstream = upstream + against_rows(v_ref[...], w_ref[:, 2 * D :])
    scaled, inverse = normalise(tokens_ref[...].astype(f32))
    gain = gain_of(ctrl_ref[...], GAIN_ONE)
    out_ref[...] = (
        residual_grad_ref[...] + norm_input_grad(upstream, scaled, inverse, gain)
    ).astype(bf16)


def input_grads(query_grad, key_grad, value_grad, small, tokens, residual_grad):
    length = tokens.shape[0]
    return call(
        input_grad_kernel,
        length // CHUNK,
        [leading(CHUNK, D)] * 3
        + [small_columns(3 * D, 0), small_columns(LANES, 4 * D)]
        + [leading(CHUNK, D), leading(CHUNK, D)],
        leading(CHUNK, D),
        jax.ShapeDtypeStruct((length, D), bf16),
        [],
        6 * length * D * D,
        18 * 2**20,
        "input_grads",
    )(query_grad, key_grad, value_grad, small, small, tokens, residual_grad)


def finish_kernel(pieces_ref, own_ref, q_ref, k_ref, v_ref, o_ref, ctrl_ref, one_ref, two_ref):
    rows, experts = ctrl_ref.shape
    total = jnp.sum(pieces_ref[...].astype(f32), axis=0)
    own = own_ref[0].astype(f32)
    for i, ref in enumerate((q_ref, k_ref, v_ref, o_ref)):
        ref[...] = total[:, i * D : (i + 1) * D]
    ctrl_ref[...] = total[:, 4 * D : 4 * D + experts]
    lane = lax.broadcasted_iota(jnp.int32, (rows, LANES), 1)

    def column(block, which):
        return jnp.sum(jnp.where(lane == which, block[:, 4 * D :], 0.0), axis=1, keepdims=True)

    one = jnp.sum(total[:, : 3 * D] * own[:, : 3 * D], axis=1, keepdims=True) / column(own, GAIN_ONE)
    square = (rows, rows)
    same = lax.broadcasted_iota(jnp.int32, square, 0) == lax.broadcasted_iota(jnp.int32, square, 1)
    one_ref[...] = jnp.sum(jnp.where(same, one, 0.0), axis=0, keepdims=True)
    two_ref[...] = jnp.sum(jnp.where(same, column(total, GAIN_TWO), 0.0), axis=0, keepdims=True)


def finish(pieces, own, experts):
    count, rows, width = pieces.shape
    outs = [(rows, D)] * 4 + [(rows, experts), (1, rows), (1, rows)]
    return call(
        finish_kernel,
        1,
        [fixed(count, rows, width), fixed(1, rows, width)],
        [fixed(*shape) for shape in outs],
        [jax.ShapeDtypeStruct(shape, f32) for shape in outs],
        [],
        1_000_000,
        1_000_000,
        "finish",
    )(pieces, own)


def swap(block, axis, bits):
    size = lax.axis_size(axis)
    return lax.ppermute(block, axis, [(i, i ^ bits) for i in range(size)])


def gather_expert(held):
    n_expert = lax.axis_size("expert")
    mine = lax.axis_index("expert")
    rows, width = held.shape
    bit = n_expert // 2
    steps = 0
    while bit:
        got = swap(held, "expert", bit)
        low = (mine & bit) == 0
        held = jnp.stack([jnp.where(low, held, got), jnp.where(low, got, held)])
        bit //= 2
        steps += 1
    order = tuple(range(steps - 1, -1, -1)) + (steps, steps + 1)
    return held.transpose(order).reshape(n_expert * rows, width)


def sum_expert(partial):
    n_expert = lax.axis_size("expert")
    mine = lax.axis_index("expert")
    width = partial.shape[1]
    steps = n_expert.bit_length() - 1
    held = partial.reshape((2,) * steps + (-1, width))
    for step in range(steps):
        bit = 1 << step
        axis = steps - 1 - step
        high = (mine & bit) >> step
        away = lax.dynamic_index_in_dim(held, high ^ 1, axis, keepdims=False).astype(bf16)
        kept = lax.dynamic_index_in_dim(held, high, axis, keepdims=False)
        held = kept + swap(away, "expert", bit).astype(f32)
    return held


def along_shard(blocks):
    return lax.all_to_all(blocks, "shard", split_axis=0, concat_axis=0, tiled=True)


def to_experts(array, copies):
    if copies > 1:
        array = jnp.repeat(array, copies, axis=0)
    return along_shard(array)


def from_experts(array, copies):
    back = along_shard(array)
    if copies > 1:
        back = back.astype(f32).reshape((-1, copies) + back.shape[1:]).sum(axis=1)
    return back


def exchange(rows, copies):
    n_expert = lax.axis_size("expert")
    n_shard = lax.axis_size("shard")
    groups = None
    if copies > 1:
        groups = [
            [e * n_shard + s for e in range(n_expert) for s in range(p, n_shard, copies)]
            for p in range(copies)
        ]
    return lax.all_to_all(
        rows, BOTH, split_axis=0, concat_axis=0, tiled=True, axis_index_groups=groups
    )


def slots_of(routes, experts):
    groups = routes.shape[0]
    named = (routes[:, :, None] == jnp.arange(experts, dtype=jnp.int32)[None, None, :]).astype(f32)
    earlier = jnp.tril(jnp.ones((groups, groups), f32), -1).astype(bf16)
    before = product(earlier, jnp.sum(named, axis=1).astype(bf16))
    rank = jnp.sum(named * before[:, None, :], axis=2).astype(jnp.int32)
    return (routes * CAP + rank).reshape(-1)


def body(
    tokens,
    ln1_gain,
    ln2_gain,
    w_query,
    w_key,
    w_value,
    w_attn_out,
    w_ctrl,
    w_in,
    b_in,
    w_exp_out,
    routes,
    grad_out,
):
    experts = w_ctrl.shape[1]
    n_shard = lax.axis_size("shard")
    copies = n_shard * lax.axis_size("expert") // experts
    slots = slots_of(routes, experts)

    own = pack_small(
        (w_query, w_key, w_value, w_attn_out), w_ctrl, ln1_gain, ln2_gain, n_shard
    )
    packed = pack_weights(w_in, b_in, w_exp_out)
    held, packed = lax.optimization_barrier((along_shard(own), packed))
    expert_w = to_experts(packed, copies)
    small = gather_expert(held.reshape(-1, held.shape[2]))

    qkv, normed_one = project(tokens, small)
    attended, lse = attention_forward(qkv)
    residual, probs, outgoing = mix(
        attended, tokens, grad_out, small, routes, slots, experts * CAP
    )
    outgoing, expert_w = lax.optimization_barrier((outgoing, expert_w))
    arrived = exchange(outgoing, copies)
    results = expert_rows(arrived, expert_w)
    returned = exchange(results, copies)
    expert_sums = expert_grads(arrived, expert_w)
    returned, expert_sums = lax.optimization_barrier((returned, expert_sums))
    expert_sums = from_experts(expert_sums, copies)
    output, residual_grad, attended_grad, sums = combine(
        residual, grad_out, probs, attended, small, routes, slots, returned
    )
    query_grad, key_grad, value_grad = attention_backward(qkv, attended_grad, attended, lse)
    late = sum_expert(weight_grads(normed_one, query_grad, key_grad, value_grad, sums))
    input_grad = input_grads(query_grad, key_grad, value_grad, small, tokens, residual_grad)
    late, input_grad, expert_sums = lax.optimization_barrier((late, input_grad, expert_sums))
    pieces = along_shard(late.astype(bf16).reshape(own.shape))
    w_in_grad, b_in_grad, w_exp_out_grad = unpack_grads(expert_sums)
    wq_grad, wk_grad, wv_grad, wo_grad, wc_grad, ln1_grad, ln2_grad = finish(pieces, own, experts)
    return (
        output,
        input_grad,
        ln1_grad.reshape(-1),
        ln2_grad.reshape(-1),
        wq_grad,
        wk_grad,
        wv_grad,
        wo_grad,
        wc_grad,
        w_in_grad,
        b_in_grad,
        w_exp_out_grad,
    )


def solution(mesh):
    rows = P(BOTH, None)
    vector = P(BOTH)
    experts = (P("expert", None, "shard"), P("expert", "shard"), P("expert", "shard", None))
    in_specs = (rows, vector, vector) + (rows,) * 5 + experts + (rows, rows)
    out_specs = (rows, rows, vector, vector) + (rows,) * 5 + experts
    return jax.shard_map(body, mesh=mesh, in_specs=in_specs, out_specs=out_specs, check_vma=False)
```

```python
import jax
import jax.numpy as jnp
from jax import lax
from jax.experimental import pallas as pl
from jax.experimental.pallas import tpu as pltpu
from jax.sharding import PartitionSpec as P

D = 512
HEAD_DIM = 64
GROUP = 32
ROUTES = 8
BLOCK = 256
CAP = 24
EPSILON = 1e-05
SCALE = 0.125 * 1.4426950408889634
BOTH = ("expert", "shard")

bf16 = jnp.bfloat16
f32 = jnp.float32
VMEM = pltpu.CompilerParams(vmem_limit_bytes=56 * 2**20)


def product(left_op, right_op):
    return jnp.dot(left_op, right_op, preferred_element_type=f32)


def transposed_product(left_op, right_op):
    return lax.dot_general(left_op, right_op, (((0,), (0,)), ((), ())), preferred_element_type=f32)


def against_rows(left_op, right_op):
    return lax.dot_general(left_op, right_op, (((1,), (1,)), ((), ())), preferred_element_type=f32)


def attention_forward_kernel(q_ref, k_ref, v_ref, o_ref, lse_ref):
    length = q_ref.shape[0]
    q_t = q_ref[...].T
    v_t = v_ref[...].T
    zero = jnp.zeros((HEAD_DIM, length), bf16)
    ones = jnp.ones((16, length), bf16)
    halves_q = [q_t[:HEAD_DIM], q_t[HEAD_DIM:]]
    sides = [
        jnp.concatenate([halves_q[0], zero], 0),
        jnp.concatenate([zero, halves_q[1]], 0),
    ]
    values = [
        jnp.concatenate([v_t[:HEAD_DIM], ones], 0),
        jnp.concatenate([v_t[HEAD_DIM:], ones], 0),
    ]

    def scores_of(b, h):
        n = (b + 1) * BLOCK
        return product(k_ref[:n, :], sides[h][:, b * BLOCK : n])

    items = [(b, h) for b in range(length // BLOCK) for h in range(2)]
    outs = []
    later = scores_of(*items[0])
    for i, (b, h) in enumerate(items):
        n = (b + 1) * BLOCK
        cols = slice(b * BLOCK, n)
        scores = later
        if i + 1 < len(items):
            later = scores_of(*items[i + 1])
        top = jnp.max(scores, axis=0, keepdims=True) * SCALE
        weights = jnp.exp2(scores * SCALE - top).astype(bf16)
        out = product(values[h][:, :n], weights)
        total = out[HEAD_DIM : HEAD_DIM + 1]
        outs.append(out[:HEAD_DIM] / total)
        lse_ref[0, h : h + 1, cols] = top + jnp.log2(total)
        if h == 1:
            o_ref[cols, :] = jnp.concatenate(outs, 0).T.astype(bf16)
            outs = []


def attention_backward_kernel(
    q_ref, k_ref, v_ref, g_ref, o_ref, lse_ref, dq_ref, dk_ref, dv_ref, dq_t
):
    length = q_ref.shape[0]
    q_t = q_ref[...].T
    g_t = g_ref[...].T
    k_t = k_ref[...].T
    both = (g_ref[...].astype(f32) * o_ref[...].astype(f32)).T
    zero = jnp.zeros((HEAD_DIM, length), bf16)
    heads = []
    for h in range(2):
        rows = slice(h * HEAD_DIM, (h + 1) * HEAD_DIM)
        heads.append(
            (
                rows,
                jnp.concatenate([q_t[rows], zero] if h == 0 else [zero, q_t[rows]], 0),
                jnp.concatenate([g_t[rows], zero] if h == 0 else [zero, g_t[rows]], 0),
                jnp.sum(both[rows], axis=0, keepdims=True),
                lse_ref[0, h : h + 1, :],
            )
        )

    def products_of(j, h):
        here = slice(j * BLOCK, (j + 1) * BLOCK)
        _, q_side, g_side, _, _ = heads[h]
        return (
            product(k_ref[here, :], q_side[:, j * BLOCK :]),
            product(v_ref[here, :], g_side[:, j * BLOCK :]),
        )

    items = [(j, h) for j in range(length // BLOCK) for h in range(2)]
    key_grads = []
    value_grads = []
    later = products_of(*items[0])
    for i, (j, h) in enumerate(items):
        lo = j * BLOCK
        here = slice(lo, lo + BLOCK)
        rows, _, _, delta, lse = heads[h]
        scores, share_grad = later
        if i + 1 < len(items):
            later = products_of(*items[i + 1])
        shares = jnp.exp2(scores * SCALE - lse[:, lo:])
        score_grad = (shares * (share_grad - delta[:, lo:])).astype(bf16)
        value_grads.append(against_rows(g_t[rows, lo:], shares.astype(bf16)))
        key_grads.append(against_rows(q_t[rows, lo:], score_grad))
        query_part = product(k_t[rows, here], score_grad)
        if j == 0:
            dq_t[rows, :] = query_part
        else:
            dq_t[rows, lo:] = dq_t[rows, lo:] + query_part
        if h == 1:
            dk_ref[here, :] = (jnp.concatenate(key_grads, 0) * 0.125).T.astype(bf16)
            dv_ref[here, :] = jnp.concatenate(value_grads, 0).T.astype(bf16)
            key_grads = []
            value_grads = []
    dq_ref[...] = (dq_t[...] * 0.125).T.astype(bf16)


def pair_columns(length, offset):
    return pl.BlockSpec((length, 2 * HEAD_DIM), lambda pair: (0, pair + offset))


def attention_forward(qkv):
    length = qkv.shape[0]
    pairs = D // (2 * HEAD_DIM)
    stats = pl.BlockSpec((1, 2, length), lambda pair: (pair, 0, 0))
    return pl.pallas_call(
        attention_forward_kernel,
        grid=(pairs,),
        in_specs=[pair_columns(length, i * pairs) for i in range(3)],
        out_specs=[pair_columns(length, 0), stats],
        out_shape=[
            jax.ShapeDtypeStruct((length, D), bf16),
            jax.ShapeDtypeStruct((pairs, 2, length), f32),
        ],
        compiler_params=VMEM,
        cost_estimate=pl.CostEstimate(
            flops=10_000_000_000, bytes_accessed=8 * 2**20, transcendentals=0
        ),
        name="attention_forward",
    )(qkv, qkv, qkv)


def attention_backward(qkv, grad, attended, lse):
    length = qkv.shape[0]
    pairs = D // (2 * HEAD_DIM)
    stats = pl.BlockSpec((1, 2, length), lambda pair: (pair, 0, 0))
    return pl.pallas_call(
        attention_backward_kernel,
        grid=(pairs,),
        in_specs=[pair_columns(length, i * pairs) for i in range(3)]
        + [pair_columns(length, 0), pair_columns(length, 0), stats],
        out_specs=[pair_columns(length, 0)] * 3,
        out_shape=[jax.ShapeDtypeStruct((length, D), bf16)] * 3,
        scratch_shapes=[pltpu.VMEM((2 * HEAD_DIM, length), f32)],
        compiler_params=VMEM,
        cost_estimate=pl.CostEstimate(
            flops=50_000_000_000, bytes_accessed=16 * 2**20, transcendentals=20_000_000
        ),
        name="attention_backward",
    )(qkv, qkv, qkv, grad, attended, lse)


CHUNK = 256
LANES = 128
BIAS_ROWS = 16
SHARDS_A_STEP = 2
GAIN_ONE = LANES - 2
GAIN_TWO = LANES - 1


def call(kernel, grid, in_specs, out_specs, out_shape, scratch, flops, moved, name):
    return pl.pallas_call(
        kernel,
        grid=(grid,),
        in_specs=in_specs,
        out_specs=out_specs,
        out_shape=out_shape,
        scratch_shapes=scratch,
        compiler_params=VMEM,
        cost_estimate=pl.CostEstimate(flops=flops, bytes_accessed=moved, transcendentals=0),
        name=name,
    )


def fixed(*shape):
    return pl.BlockSpec(shape, lambda i: (0,) * len(shape))


def small_columns(width, start):
    return pl.BlockSpec((D, width), lambda i: (0, start // width))


def leading(*shape):
    return pl.BlockSpec(shape, lambda i: (i,) + (0,) * (len(shape) - 1))


def normalise(matrix):
    average = jnp.mean(matrix, axis=1, keepdims=True)
    centered = matrix - average
    inverse = lax.rsqrt(jnp.mean(centered * centered, axis=1, keepdims=True) + EPSILON)
    return centered * inverse, inverse


def norm_input_grad(upstream, scaled, inverse, gain):
    adjusted = upstream * gain
    first_mean = jnp.mean(adjusted, axis=1, keepdims=True)
    second_mean = jnp.mean(adjusted * scaled, axis=1, keepdims=True)
    return inverse * (adjusted - first_mean - scaled * second_mean)


def small_kernel(q_ref, k_ref, v_ref, o_ref, ctrl_ref, one_ref, two_ref, out_ref):
    rows, experts = ctrl_ref.shape
    for i, ref in enumerate((q_ref, k_ref, v_ref, o_ref)):
        out_ref[:, i * D : (i + 1) * D] = ref[...].astype(bf16)
    square = (rows, rows)
    own = lax.broadcasted_iota(jnp.int32, square, 0) == lax.broadcasted_iota(jnp.int32, square, 1)
    one = jnp.sum(jnp.where(own, one_ref[...], 0.0), axis=1, keepdims=True)
    two = jnp.sum(jnp.where(own, two_ref[...], 0.0), axis=1, keepdims=True)
    lane = lax.broadcasted_iota(jnp.int32, (rows, LANES), 1)
    gains = jnp.where(lane == GAIN_ONE, one, jnp.where(lane == GAIN_TWO, two, 0.0))
    out_ref[:, 4 * D :] = gains.astype(bf16)
    out_ref[:, 4 * D : 4 * D + experts] = ctrl_ref[...].astype(bf16)


def pack_small(weights, ctrl, gain_one, gain_two):
    rows, experts = ctrl.shape
    width = 4 * D + LANES
    return call(
        small_kernel,
        1,
        [fixed(rows, D)] * 4 + [fixed(rows, experts), fixed(1, rows), fixed(1, rows)],
        fixed(rows, width),
        jax.ShapeDtypeStruct((rows, width), bf16),
        [],
        100_000,
        200_000,
        "pack_small",
    )(*weights, ctrl, gain_one.reshape(1, rows), gain_two.reshape(1, rows))


def gain_of(ctrl_block, lane):
    pick = (lax.broadcasted_iota(jnp.int32, (16, LANES), 1) == lane).astype(bf16)
    return against_rows(pick, ctrl_block)[:1]


def pack_kernel(first_ref, bias_ref, second_ref, out_ref):
    hidden = first_ref.shape[2]
    out_ref[0, :D, :] = first_ref[0].astype(bf16)
    out_ref[0, D : D + BIAS_ROWS, :] = jnp.broadcast_to(
        bias_ref[pl.ds(pl.program_id(0), 1), :], (BIAS_ROWS, hidden)
    ).astype(bf16)
    for c in range(D // hidden):
        start = D + BIAS_ROWS + c * hidden
        out_ref[0, start : start + hidden, :] = second_ref[
            0, :, c * hidden : (c + 1) * hidden
        ].astype(bf16)


def pack_weights(w_in, b_in, w_exp_out):
    local, _, hidden = w_in.shape
    total = 2 * D + BIAS_ROWS
    return call(
        pack_kernel,
        local,
        [leading(1, D, hidden), fixed(local, hidden), leading(1, hidden, D)],
        leading(1, total, hidden),
        jax.ShapeDtypeStruct((local, total, hidden), bf16),
        [],
        1_000_000,
        12 * 2**20,
        "pack_weights",
    )(w_in, b_in, w_exp_out)


def unpack_kernel(in_ref, first_ref, bias_ref, second_ref):
    hidden = first_ref.shape[2]
    first_ref[0] = in_ref[0, :D, :].astype(f32)
    bias_ref[pl.ds(pl.program_id(0), 1), :] = in_ref[0, D : D + BIAS_ROWS, :].astype(f32)[:1]
    for c in range(D // hidden):
        start = D + BIAS_ROWS + c * hidden
        second_ref[0, :, c * hidden : (c + 1) * hidden] = in_ref[
            0, start : start + hidden, :
        ].astype(f32)


def unpack_grads(packed):
    local, total, hidden = packed.shape
    return call(
        unpack_kernel,
        local,
        [leading(1, total, hidden)],
        [leading(1, D, hidden), fixed(local, hidden), leading(1, hidden, D)],
        [
            jax.ShapeDtypeStruct((local, D, hidden), f32),
            jax.ShapeDtypeStruct((local, hidden), f32),
            jax.ShapeDtypeStruct((local, hidden, D), f32),
        ],
        [],
        1_000_000,
        12 * 2**20,
        "unpack_grads",
    )(packed)


def expert_part(rows_ref, w_ref, i):
    hidden = w_ref.shape[2]
    first = w_ref[i, :D, :]
    bias = w_ref[i, D : D + BIAS_ROWS, :].astype(f32)[:1]
    pre_act = product(rows_ref[:, :D], first) + bias
    sigma = 0.5 + 0.5 * jnp.tanh(0.5 * pre_act)
    hidden_grad = jnp.zeros_like(pre_act)
    second = []
    for c in range(D // hidden):
        start = D + BIAS_ROWS + c * hidden
        second.append(w_ref[i, start : start + hidden, :])
        cols = slice(D + c * hidden, D + (c + 1) * hidden)
        hidden_grad = hidden_grad + against_rows(rows_ref[:, cols], second[-1])
    active = (pre_act * sigma).astype(bf16)
    pre_grad = (
        hidden_grad.astype(bf16).astype(f32) * (sigma * (1.0 + pre_act * (1.0 - sigma)))
    ).astype(bf16)
    return first, second, active, pre_grad


def expert_kernel(rows_ref, w_ref, out_ref, results, mixed_grad):
    step = pl.program_id(0)
    held, _, hidden = w_ref.shape
    chunks = D // hidden
    parts = [None] * (chunks + 1)
    for i in range(held):
        first, second, active, pre_grad = expert_part(rows_ref, w_ref, i)
        more = [product(active, block) for block in second] + [against_rows(pre_grad, first)]
        parts = more if i == 0 else [old + new for old, new in zip(parts, more)]

    @pl.when(step == 0)
    def _():
        for c in range(chunks):
            results[:, c * hidden : (c + 1) * hidden] = parts[c]
        mixed_grad[...] = parts[chunks]

    @pl.when(step > 0)
    def _():
        for c in range(chunks):
            cols = slice(c * hidden, (c + 1) * hidden)
            results[:, cols] = results[:, cols] + parts[c]
        mixed_grad[...] = mixed_grad[...] + parts[chunks]

    @pl.when(step == pl.num_programs(0) - 1)
    def _():
        out_ref[:, :D] = results[...].astype(bf16)
        out_ref[:, D:] = mixed_grad[...].astype(bf16)


def expert_rows(rows, weights):
    count = rows.shape[0]
    shards, total, hidden = weights.shape
    return call(
        expert_kernel,
        shards // SHARDS_A_STEP,
        [fixed(count, 2 * D), leading(SHARDS_A_STEP, total, hidden)],
        fixed(count, 2 * D),
        jax.ShapeDtypeStruct((count, 2 * D), bf16),
        [pltpu.VMEM((count, D), f32), pltpu.VMEM((count, D), f32)],
        8 * count * D * shards * hidden,
        8 * 2**20,
        "expert_rows",
    )(rows, weights)


def expert_grad_kernel(rows_ref, w_ref, out_ref, rows_t):
    hidden = out_ref.shape[2]

    @pl.when(pl.program_id(0) == 0)
    def _():
        rows_t[...] = rows_ref[:, :D].T

    _, _, active, pre_grad = expert_part(rows_ref, w_ref, 0)
    out_ref[0, :D, :] = product(rows_t[...], pre_grad).astype(bf16)
    out_ref[0, D : D + BIAS_ROWS, :] = jnp.broadcast_to(
        jnp.sum(pre_grad.astype(f32), axis=0, keepdims=True), (BIAS_ROWS, hidden)
    ).astype(bf16)
    active_t = active.T
    for c in range(D // hidden):
        start = D + BIAS_ROWS + c * hidden
        out_ref[0, start : start + hidden, :] = product(
            active_t, rows_ref[:, D + c * hidden : D + (c + 1) * hidden]
        ).astype(bf16)


def expert_grads(rows, weights):
    count = rows.shape[0]
    shards, total, hidden = weights.shape
    return call(
        expert_grad_kernel,
        shards,
        [fixed(count, 2 * D), leading(1, total, hidden)],
        leading(1, total, hidden),
        jax.ShapeDtypeStruct((shards, total, hidden), bf16),
        [pltpu.VMEM((D, count), bf16)],
        8 * count * D * shards * hidden,
        14 * 2**20,
        "expert_grads",
    )(rows, weights)


def project_kernel(tokens_ref, w_ref, ctrl_ref, qkv_ref, normed_ref):
    scaled, _ = normalise(tokens_ref[...].astype(f32))
    normed = (scaled * gain_of(ctrl_ref[...], GAIN_ONE)).astype(bf16)
    normed_ref[...] = normed
    qkv_ref[...] = product(normed, w_ref[...]).astype(bf16)


def project(tokens, small):
    length = tokens.shape[0]
    return call(
        project_kernel,
        length // CHUNK,
        [leading(CHUNK, D), small_columns(3 * D, 0), small_columns(LANES, 4 * D)],
        [leading(CHUNK, 3 * D), leading(CHUNK, D)],
        [jax.ShapeDtypeStruct((length, 3 * D), bf16), jax.ShapeDtypeStruct((length, D), bf16)],
        [],
        6 * length * D * D,
        12 * 2**20,
        "project",
    )(tokens, small, small)


def choose(probs, routes):
    columns = routes.shape[1]
    shape = (LANES, columns)
    onehot = (lax.broadcasted_iota(jnp.int32, shape, 0) == routes).astype(bf16)
    tokens = probs.shape[0]
    own = lax.broadcasted_iota(jnp.int32, (tokens, columns), 0) // GROUP == (
        lax.broadcasted_iota(jnp.int32, (tokens, columns), 1) // ROUTES
    )
    chosen = jnp.where(own, product(probs.astype(bf16), onehot), 0.0).astype(bf16)
    return chosen, onehot, own


def mix_kernel(
    attended_ref, tokens_ref, grad_ref, wo_ref, ctrl_ref, routes_ref, slots_ref,
    residual_ref, probs_ref, out_ref, rows,
):
    step = pl.program_id(0)
    residual = tokens_ref[...].astype(f32) + product(attended_ref[...], wo_ref[...])
    residual_ref[...] = residual
    scaled, _ = normalise(residual)
    normed = (scaled * gain_of(ctrl_ref[...], GAIN_TWO)).astype(bf16)
    logits = product(normed, ctrl_ref[...]).reshape(CHUNK // GROUP, GROUP, LANES)
    weights = jnp.exp(logits - jnp.max(logits, axis=1, keepdims=True))
    probs = (weights / jnp.sum(weights, axis=1, keepdims=True)).reshape(CHUNK, LANES)
    probs_ref[...] = probs
    chosen, _, _ = choose(probs, routes_ref[0])
    columns = chosen.shape[1]
    here = pl.ds(pl.multiple_of(step * columns, columns), columns)
    rows[here, :D] = transposed_product(chosen, normed).astype(bf16)
    rows[here, D:] = transposed_product(chosen, grad_ref[...]).astype(bf16)

    @pl.when(step == pl.num_programs(0) - 1)
    def _():
        shape = (out_ref.shape[0], rows.shape[0])
        dispatch = (lax.broadcasted_iota(jnp.int32, shape, 0) == slots_ref[...]).astype(bf16)
        out_ref[...] = product(dispatch, rows[...]).astype(bf16)


def mix(attended, tokens, grad_out, small, routes, slots, slot_count):
    length = tokens.shape[0]
    steps = length // CHUNK
    count = slots.shape[0]
    return call(
        mix_kernel,
        steps,
        [leading(CHUNK, D)] * 3
        + [small_columns(D, 3 * D), small_columns(LANES, 4 * D)]
        + [leading(1, 1, count // steps), fixed(1, count)],
        [leading(CHUNK, D), leading(CHUNK, LANES), fixed(slot_count, 2 * D)],
        [
            jax.ShapeDtypeStruct((length, D), f32),
            jax.ShapeDtypeStruct((length, LANES), f32),
            jax.ShapeDtypeStruct((slot_count, 2 * D), bf16),
        ],
        [pltpu.VMEM((count, 2 * D), bf16)],
        4 * length * D * D,
        14 * 2**20,
        "mix",
    )(
        attended, tokens, grad_out, small, small,
        routes.reshape(steps, 1, count // steps), slots.reshape(1, count),
    )


def combine_kernel(
    residual_ref, grad_ref, probs_ref, attended_ref, wo_ref, ctrl_ref, routes_ref,
    slots_ref, back_ref, output_ref, residual_grad_ref, attended_grad_ref, sums_ref, gain_sum,
):
    step = pl.program_id(0)
    gain = gain_of(ctrl_ref[...], GAIN_TWO)
    residual = residual_ref[...]
    scaled, inverse = normalise(residual)
    normed = (scaled * gain).astype(bf16)
    probs = probs_ref[...]
    grad = grad_ref[...]
    chosen, onehot, own = choose(probs, routes_ref[0])
    shape = (chosen.shape[1], back_ref.shape[0])
    collect = (lax.broadcasted_iota(jnp.int32, shape, 1) == slots_ref[...]).astype(bf16)
    rows = product(collect, back_ref[...]).astype(bf16)
    results = rows[:, :D]
    mixed_grad = rows[:, D:]
    output_ref[...] = (residual + product(chosen, results)).astype(bf16)
    chosen_grad = jnp.where(own, against_rows(grad, results) + against_rows(normed, mixed_grad), 0.0)
    high = chosen_grad.astype(bf16)
    low = (chosen_grad - high.astype(f32)).astype(bf16)
    prob_grad = against_rows(high, onehot) + against_rows(low, onehot)
    weighted = (probs * prob_grad).reshape(CHUNK // GROUP, GROUP, LANES)
    total = jnp.broadcast_to(jnp.sum(weighted, axis=1, keepdims=True), weighted.shape)
    logit_grad = (probs * (prob_grad - total.reshape(CHUNK, LANES))).astype(bf16)
    normed_grad = product(chosen, mixed_grad) + against_rows(logit_grad, ctrl_ref[...])
    gain_part = jnp.sum(normed_grad * scaled, axis=0, keepdims=True)
    residual_grad = grad.astype(f32) + norm_input_grad(normed_grad, scaled, inverse, gain)
    residual_grad_ref[...] = residual_grad
    branch = residual_grad.astype(bf16)
    attended_grad_ref[...] = against_rows(branch, wo_ref[...]).astype(bf16)
    wo_part = transposed_product(attended_ref[...], branch)
    ctrl_part = transposed_product(normed, logit_grad)

    @pl.when(step == 0)
    def _():
        sums_ref[:, :D] = wo_part
        sums_ref[:, D:] = ctrl_part
        gain_sum[...] = gain_part

    @pl.when(step > 0)
    def _():
        sums_ref[:, :D] = sums_ref[:, :D] + wo_part
        sums_ref[:, D:] = sums_ref[:, D:] + ctrl_part
        gain_sum[...] = gain_sum[...] + gain_part

    @pl.when(step == pl.num_programs(0) - 1)
    def _():
        column = jnp.broadcast_to(gain_sum[...], (LANES, D)).T
        lane = lax.broadcasted_iota(jnp.int32, (D, LANES), 1)
        sums_ref[:, D:] = jnp.where(lane == LANES - 1, column, sums_ref[:, D:])


def combine(residual, grad_out, probs, attended, small, routes, slots, back):
    length = residual.shape[0]
    steps = length // CHUNK
    count = slots.shape[0]
    return call(
        combine_kernel,
        steps,
        [leading(CHUNK, D), leading(CHUNK, D), leading(CHUNK, LANES), leading(CHUNK, D)]
        + [small_columns(D, 3 * D), small_columns(LANES, 4 * D), leading(1, 1, count // steps)]
        + [leading(count // steps, 1), fixed(*back.shape)],
        [leading(CHUNK, D)] * 3 + [fixed(D, D + LANES)],
        [
            jax.ShapeDtypeStruct((length, D), bf16),
            jax.ShapeDtypeStruct((length, D), f32),
            jax.ShapeDtypeStruct((length, D), bf16),
            jax.ShapeDtypeStruct((D, D + LANES), f32),
        ],
        [pltpu.VMEM((1, D), f32)],
        6 * length * D * D,
        24 * 2**20,
        "combine",
    )(
        residual, grad_out, probs, attended, small, small,
        routes.reshape(steps, 1, count // steps), slots.reshape(count, 1), back,
    )


def weight_grad_kernel(
    core_ref, normed_ref, q_ref, k_ref, v_ref, sums_ref, away_ref, kept_ref, total
):
    step = pl.program_id(0)
    normed_t = normed_ref[...].T

    for i, ref in enumerate((q_ref, k_ref, v_ref)):
        cols = slice(i * D, (i + 1) * D)
        part = product(normed_t, ref[...])

        @pl.when(step == 0)
        def _(cols=cols, part=part):
            total[:, cols] = part

        @pl.when(step > 0)
        def _(cols=cols, part=part):
            total[:, cols] = total[:, cols] + part

    @pl.when(step == pl.num_programs(0) - 1)
    def _():
        rows = kept_ref.shape[1]
        for x in range(kept_ref.shape[0]):
            mine = pl.ds(pl.multiple_of((2 * x + core_ref[0]) * rows, rows), rows)
            other = pl.ds(pl.multiple_of((2 * x + 1 - core_ref[0]) * rows, rows), rows)
            kept_ref[x, :, : 3 * D] = total[mine, :]
            kept_ref[x, :, 3 * D :] = sums_ref[mine, :]
            away_ref[x, :, : 3 * D] = total[other, :].astype(bf16)
            away_ref[x, :, 3 * D :] = sums_ref[other, :].astype(bf16)


def weight_grads(normed, query_grad, key_grad, value_grad, sums, core, n_expert):
    length = normed.shape[0]
    width = sums.shape[1]
    chunk = 512
    shape = (n_expert // 2, D // n_expert, 3 * D + width)
    return call(
        weight_grad_kernel,
        length // chunk,
        [pl.BlockSpec(memory_space=pltpu.SMEM)] + [leading(chunk, D)] * 4 + [fixed(D, width)],
        [fixed(*shape), fixed(*shape)],
        [jax.ShapeDtypeStruct(shape, bf16), jax.ShapeDtypeStruct(shape, f32)],
        [pltpu.VMEM((D, 3 * D), f32)],
        6 * length * D * D,
        12 * 2**20,
        "weight_grads",
    )(core, normed, query_grad, key_grad, value_grad, sums)


def input_grad_kernel(q_ref, k_ref, v_ref, w_ref, ctrl_ref, tokens_ref, residual_grad_ref, out_ref):
    upstream = against_rows(q_ref[...], w_ref[:, :D])
    upstream = upstream + against_rows(k_ref[...], w_ref[:, D : 2 * D])
    upstream = upstream + against_rows(v_ref[...], w_ref[:, 2 * D :])
    scaled, inverse = normalise(tokens_ref[...].astype(f32))
    gain = gain_of(ctrl_ref[...], GAIN_ONE)
    out_ref[...] = (
        residual_grad_ref[...] + norm_input_grad(upstream, scaled, inverse, gain)
    ).astype(bf16)


def input_grads(query_grad, key_grad, value_grad, small, tokens, residual_grad):
    length = tokens.shape[0]
    return call(
        input_grad_kernel,
        length // CHUNK,
        [leading(CHUNK, D)] * 3
        + [small_columns(3 * D, 0), small_columns(LANES, 4 * D)]
        + [leading(CHUNK, D), leading(CHUNK, D)],
        leading(CHUNK, D),
        jax.ShapeDtypeStruct((length, D), bf16),
        [],
        6 * length * D * D,
        18 * 2**20,
        "input_grads",
    )(query_grad, key_grad, value_grad, small, small, tokens, residual_grad)


def finish_kernel(pieces_ref, own_ref, q_ref, k_ref, v_ref, o_ref, ctrl_ref, one_ref, two_ref):
    rows, experts = ctrl_ref.shape
    total = jnp.sum(pieces_ref[...].astype(f32), axis=0)
    own = own_ref[...].astype(f32)
    for i, ref in enumerate((q_ref, k_ref, v_ref, o_ref)):
        ref[...] = total[:, i * D : (i + 1) * D]
    ctrl_ref[...] = total[:, 4 * D : 4 * D + experts]
    lane = lax.broadcasted_iota(jnp.int32, (rows, LANES), 1)

    def column(block, which):
        return jnp.sum(jnp.where(lane == which, block[:, 4 * D :], 0.0), axis=1, keepdims=True)

    one = jnp.sum(total[:, : 3 * D] * own[:, : 3 * D], axis=1, keepdims=True) / column(own, GAIN_ONE)
    square = (rows, rows)
    same = lax.broadcasted_iota(jnp.int32, square, 0) == lax.broadcasted_iota(jnp.int32, square, 1)
    one_ref[...] = jnp.sum(jnp.where(same, one, 0.0), axis=0, keepdims=True)
    two_ref[...] = jnp.sum(jnp.where(same, column(total, GAIN_TWO), 0.0), axis=0, keepdims=True)


def finish(pieces, own, experts):
    count, rows, width = pieces.shape
    outs = [(rows, D)] * 4 + [(rows, experts), (1, rows), (1, rows)]
    return call(
        finish_kernel,
        1,
        [fixed(count, rows, width), fixed(rows, width)],
        [fixed(*shape) for shape in outs],
        [jax.ShapeDtypeStruct(shape, f32) for shape in outs],
        [],
        1_000_000,
        1_000_000,
        "finish",
    )(pieces, own)


def swap(block, axis, bits):
    size = lax.axis_size(axis)
    return lax.ppermute(block, axis, [(i, i ^ bits) for i in range(size)])


def halves(size):
    inner = 1
    while inner * inner * 4 <= size:
        inner *= 2
    return size // inner, inner


def spread(block, size, stride, place):
    held = jnp.zeros((size,) + block.shape, block.dtype)
    held = lax.dynamic_update_slice(held, block[None], (place, 0, 0))
    for k in range(1, size):
        got = swap(block, "shard", k * stride)
        held = lax.dynamic_update_slice(held, got[None], (place ^ k, 0, 0))
    return held.reshape(-1, block.shape[1])


def gather_expert(held):
    n_expert = lax.axis_size("expert")
    mine = lax.axis_index("expert")
    rows, width = held.shape
    bit = n_expert // 2
    steps = 0
    while bit:
        got = swap(held, "expert", bit)
        low = (mine & bit) == 0
        held = jnp.stack([jnp.where(low, held, got), jnp.where(low, got, held)])
        bit //= 2
        steps += 1
    order = tuple(range(steps - 1, -1, -1)) + (steps, steps + 1)
    return held.transpose(order).reshape(n_expert * rows, width)


def sum_expert(away, kept):
    n_expert = lax.axis_size("expert")
    mine = lax.axis_index("expert")
    width = kept.shape[-1]
    steps = n_expert.bit_length() - 1
    held = kept + swap(away, "expert", 1).astype(f32)
    held = held.reshape((2,) * (steps - 1) + (-1, width))
    for step in range(1, steps):
        bit = 1 << step
        axis = steps - 1 - step
        high = (mine & bit) >> step
        away = lax.dynamic_index_in_dim(held, high ^ 1, axis, keepdims=False).astype(bf16)
        kept = lax.dynamic_index_in_dim(held, high, axis, keepdims=False)
        held = kept + swap(away, "expert", bit).astype(f32)
    return held


def along_shard(blocks):
    return lax.all_to_all(blocks, "shard", split_axis=0, concat_axis=0, tiled=True)


def to_experts(array, copies):
    if copies > 1:
        array = jnp.repeat(array, copies, axis=0)
    return along_shard(array)


def from_experts(array, copies):
    back = along_shard(array)
    if copies > 1:
        back = back.astype(f32).reshape((-1, copies) + back.shape[1:]).sum(axis=1)
    return back


def exchange(rows, copies):
    n_expert = lax.axis_size("expert")
    n_shard = lax.axis_size("shard")
    groups = None
    if copies > 1:
        groups = [
            [e * n_shard + s for e in range(n_expert) for s in range(p, n_shard, copies)]
            for p in range(copies)
        ]
    return lax.all_to_all(
        rows, BOTH, split_axis=0, concat_axis=0, tiled=True, axis_index_groups=groups
    )


def slots_of(routes, experts):
    groups = routes.shape[0]
    named = (routes[:, :, None] == jnp.arange(experts, dtype=jnp.int32)[None, None, :]).astype(f32)
    earlier = jnp.tril(jnp.ones((groups, groups), f32), -1).astype(bf16)
    before = product(earlier, jnp.sum(named, axis=1).astype(bf16))
    rank = jnp.sum(named * before[:, None, :], axis=2).astype(jnp.int32)
    return (routes * CAP + rank).reshape(-1)


def body(
    tokens,
    ln1_gain,
    ln2_gain,
    w_query,
    w_key,
    w_value,
    w_attn_out,
    w_ctrl,
    w_in,
    b_in,
    w_exp_out,
    routes,
    grad_out,
):
    experts = w_ctrl.shape[1]
    n_shard = lax.axis_size("shard")
    copies = n_shard * lax.axis_size("expert") // experts
    slots = slots_of(routes, experts)

    own = pack_small(
        (w_query, w_key, w_value, w_attn_out), w_ctrl, ln1_gain, ln2_gain
    )
    outer, inner = halves(n_shard)
    here = lax.axis_index("shard")
    held = spread(own, inner, 1, here & (inner - 1))
    held, w_in, w_exp_out = lax.optimization_barrier((held, w_in, w_exp_out))
    expert_w = to_experts(pack_weights(w_in, b_in, w_exp_out), copies)
    held = spread(held, outer, inner, here >> (inner.bit_length() - 1))
    small = gather_expert(held)

    qkv, normed_one = project(tokens, small)
    attended, lse = attention_forward(qkv)
    residual, probs, outgoing = mix(
        attended, tokens, grad_out, small, routes, slots, experts * CAP
    )
    outgoing, expert_w = lax.optimization_barrier((outgoing, expert_w))
    arrived = exchange(outgoing, copies)
    results = expert_rows(arrived, expert_w)
    returned = exchange(results, copies)
    expert_sums = expert_grads(arrived, expert_w)
    returned, expert_sums = lax.optimization_barrier((returned, expert_sums))
    expert_sums = from_experts(expert_sums, copies)
    output, residual_grad, attended_grad, sums = combine(
        residual, grad_out, probs, attended, small, routes, slots, returned
    )
    query_grad, key_grad, value_grad = attention_backward(qkv, attended_grad, attended, lse)
    core = (lax.axis_index("expert") & 1).reshape(1)
    away, kept = weight_grads(
        normed_one, query_grad, key_grad, value_grad, sums, core, lax.axis_size("expert")
    )
    late = sum_expert(away, kept)
    input_grad = input_grads(query_grad, key_grad, value_grad, small, tokens, residual_grad)
    late, input_grad, expert_sums = lax.optimization_barrier((late, input_grad, expert_sums))
    pieces = along_shard(late.astype(bf16).reshape((n_shard,) + own.shape))
    w_in_grad, b_in_grad, w_exp_out_grad = unpack_grads(expert_sums)
    wq_grad, wk_grad, wv_grad, wo_grad, wc_grad, ln1_grad, ln2_grad = finish(pieces, own, experts)
    return (
        output,
        input_grad,
        ln1_grad.reshape(-1),
        ln2_grad.reshape(-1),
        wq_grad,
        wk_grad,
        wv_grad,
        wo_grad,
        wc_grad,
        w_in_grad,
        b_in_grad,
        w_exp_out_grad,
    )


def solution(mesh):
    rows = P(BOTH, None)
    vector = P(BOTH)
    experts = (P("expert", None, "shard"), P("expert", "shard"), P("expert", "shard", None))
    in_specs = (rows, vector, vector) + (rows,) * 5 + experts + (rows, rows)
    out_specs = (rows, rows, vector, vector) + (rows,) * 5 + experts
    return jax.shard_map(body, mesh=mesh, in_specs=in_specs, out_specs=out_specs, check_vma=False)
```

```python
import jax
import jax.numpy as jnp
from jax import lax
from jax.experimental import pallas as pl
from jax.experimental.pallas import tpu as pltpu
from jax.sharding import PartitionSpec as P

D = 512
HEAD_DIM = 64
GROUP = 32
ROUTES = 8
BLOCK = 256
CAP = 24
EPSILON = 1e-05
SCALE = 0.125 * 1.4426950408889634
BOTH = ("expert", "shard")

bf16 = jnp.bfloat16
f32 = jnp.float32


def vmem(mebibytes):
    return pltpu.CompilerParams(vmem_limit_bytes=mebibytes * 2**20)


def product(left_op, right_op):
    return jnp.dot(left_op, right_op, preferred_element_type=f32)


def transposed_product(left_op, right_op):
    return lax.dot_general(left_op, right_op, (((0,), (0,)), ((), ())), preferred_element_type=f32)


def against_rows(left_op, right_op):
    return lax.dot_general(left_op, right_op, (((1,), (1,)), ((), ())), preferred_element_type=f32)


def attention_forward_kernel(q_ref, k_ref, v_ref, o_ref, lse_ref, qt_ref, kt_ref, ot_ref):
    length = q_ref.shape[0]
    q_t = q_ref[...].T
    qt_ref[...] = q_t
    kt_ref[...] = k_ref[...].T
    v_t = v_ref[...].T
    zero = jnp.zeros((HEAD_DIM, length), bf16)
    ones = jnp.ones((16, length), bf16)
    halves_q = [q_t[:HEAD_DIM], q_t[HEAD_DIM:]]
    sides = [
        jnp.concatenate([halves_q[0], zero], 0),
        jnp.concatenate([zero, halves_q[1]], 0),
    ]
    values = [
        jnp.concatenate([v_t[:HEAD_DIM], ones], 0),
        jnp.concatenate([v_t[HEAD_DIM:], ones], 0),
    ]

    def scores_of(b, h):
        n = (b + 1) * BLOCK
        return product(k_ref[:n, :], sides[h][:, b * BLOCK : n])

    items = [(b, h) for b in range(length // BLOCK) for h in range(2)]
    outs = []
    later = scores_of(*items[0])
    for i, (b, h) in enumerate(items):
        n = (b + 1) * BLOCK
        cols = slice(b * BLOCK, n)
        scores = later
        if i + 1 < len(items):
            later = scores_of(*items[i + 1])
        top = jnp.max(scores, axis=0, keepdims=True) * SCALE
        weights = jnp.exp2(scores * SCALE - top).astype(bf16)
        out = product(values[h][:, :n], weights)
        total = out[HEAD_DIM : HEAD_DIM + 1]
        outs.append(out[:HEAD_DIM] / total)
        lse_ref[0, h : h + 1, cols] = top + jnp.log2(total)
        if h == 1:
            both = jnp.concatenate(outs, 0).astype(bf16)
            ot_ref[:, cols] = both
            o_ref[cols, :] = both.T
            outs = []


def attention_backward_kernel(
    qt_ref, kt_ref, k_ref, v_ref, gt_ref, ot_ref, lse_ref, out_ref, dq_t
):
    length = k_ref.shape[0]
    q_t = qt_ref[...]
    g_t = gt_ref[...]
    k_t = kt_ref[...]
    both = g_t.astype(f32) * ot_ref[...].astype(f32)
    zero = jnp.zeros((HEAD_DIM, length), bf16)
    heads = []
    for h in range(2):
        rows = slice(h * HEAD_DIM, (h + 1) * HEAD_DIM)
        heads.append(
            (
                rows,
                jnp.concatenate([q_t[rows], zero] if h == 0 else [zero, q_t[rows]], 0),
                jnp.concatenate([g_t[rows], zero] if h == 0 else [zero, g_t[rows]], 0),
                jnp.sum(both[rows], axis=0, keepdims=True),
                lse_ref[0, h : h + 1, :],
            )
        )

    def products_of(j, h):
        here = slice(j * BLOCK, (j + 1) * BLOCK)
        _, q_side, g_side, _, _ = heads[h]
        return (
            product(k_ref[here, :], q_side[:, j * BLOCK :]),
            product(v_ref[here, :], g_side[:, j * BLOCK :]),
        )

    items = [(j, h) for j in range(length // BLOCK) for h in range(2)]
    key_grads = []
    value_grads = []
    later = products_of(*items[0])
    for i, (j, h) in enumerate(items):
        lo = j * BLOCK
        here = slice(lo, lo + BLOCK)
        rows, _, _, delta, lse = heads[h]
        scores, share_grad = later
        if i + 1 < len(items):
            later = products_of(*items[i + 1])
        shares = jnp.exp2(scores * SCALE - lse[:, lo:])
        score_grad = (shares * (share_grad - delta[:, lo:])).astype(bf16)
        value_grads.append(against_rows(g_t[rows, lo:], shares.astype(bf16)))
        key_grads.append(against_rows(q_t[rows, lo:], score_grad))
        query_part = product(k_t[rows, here], score_grad)
        if j == 0:
            dq_t[rows, :] = query_part
        else:
            dq_t[rows, lo:] = dq_t[rows, lo:] + query_part
        if h == 1:
            out_ref[1, here, :] = (jnp.concatenate(key_grads, 0) * 0.125).astype(bf16).T
            out_ref[2, here, :] = jnp.concatenate(value_grads, 0).astype(bf16).T
            key_grads = []
            value_grads = []
    out_ref[0] = (dq_t[...] * 0.125).astype(bf16).T


def pair_columns(length, offset):
    return pl.BlockSpec((length, 2 * HEAD_DIM), lambda pair: (0, pair + offset))


def pair_rows(length):
    return pl.BlockSpec((2 * HEAD_DIM, length), lambda pair: (pair, 0))


def attention_forward(qkv):
    length = qkv.shape[0]
    pairs = D // (2 * HEAD_DIM)
    stats = pl.BlockSpec((1, 2, length), lambda pair: (pair, 0, 0))
    return pl.pallas_call(
        attention_forward_kernel,
        grid=(pairs,),
        in_specs=[pair_columns(length, i * pairs) for i in range(3)],
        out_specs=[pair_columns(length, 0), stats] + [pair_rows(length)] * 3,
        out_shape=[
            jax.ShapeDtypeStruct((length, D), bf16),
            jax.ShapeDtypeStruct((pairs, 2, length), f32),
        ]
        + [jax.ShapeDtypeStruct((D, length), bf16)] * 3,
        compiler_params=vmem(56),
        cost_estimate=pl.CostEstimate(
            flops=10_000_000_000, bytes_accessed=8 * 2**20, transcendentals=0
        ),
        name="attention_forward",
    )(qkv, qkv, qkv)


def attention_backward(qkv, query_t, key_t, grad_t, attended_t, lse):
    length = qkv.shape[0]
    pairs = D // (2 * HEAD_DIM)
    stats = pl.BlockSpec((1, 2, length), lambda pair: (pair, 0, 0))
    return pl.pallas_call(
        attention_backward_kernel,
        grid=(pairs,),
        in_specs=[pair_rows(length)] * 2
        + [pair_columns(length, pairs), pair_columns(length, 2 * pairs)]
        + [pair_rows(length)] * 2
        + [stats],
        out_specs=pl.BlockSpec((3, length, 2 * HEAD_DIM), lambda pair: (0, 0, pair)),
        out_shape=jax.ShapeDtypeStruct((3, length, D), bf16),
        scratch_shapes=[pltpu.VMEM((2 * HEAD_DIM, length), f32)],
        compiler_params=vmem(56),
        cost_estimate=pl.CostEstimate(
            flops=50_000_000_000, bytes_accessed=16 * 2**20, transcendentals=20_000_000
        ),
        name="attention_backward",
    )(query_t, key_t, qkv, qkv, grad_t, attended_t, lse)


CHUNK = 256
COMBINE = 512
LANES = 128
BIAS_ROWS = 16
SHARDS_A_STEP = 4
GAIN_ONE = LANES - 2
GAIN_TWO = LANES - 1


def call(kernel, grid, in_specs, out_specs, out_shape, scratch, flops, moved, name, limit=56):
    return pl.pallas_call(
        kernel,
        grid=(grid,),
        in_specs=in_specs,
        out_specs=out_specs,
        out_shape=out_shape,
        scratch_shapes=scratch,
        compiler_params=vmem(limit),
        cost_estimate=pl.CostEstimate(flops=flops, bytes_accessed=moved, transcendentals=0),
        name=name,
    )


def fixed(*shape):
    return pl.BlockSpec(shape, lambda i: (0,) * len(shape))


def small_columns(width, start):
    return pl.BlockSpec((D, width), lambda i: (0, start // width))


def leading(*shape):
    return pl.BlockSpec(shape, lambda i: (i,) + (0,) * (len(shape) - 1))


def normalise(matrix):
    average = jnp.mean(matrix, axis=1, keepdims=True)
    centered = matrix - average
    inverse = lax.rsqrt(jnp.mean(centered * centered, axis=1, keepdims=True) + EPSILON)
    return centered * inverse, inverse


def norm_input_grad(upstream, scaled, inverse, gain):
    adjusted = upstream * gain
    first_mean = jnp.mean(adjusted, axis=1, keepdims=True)
    second_mean = jnp.mean(adjusted * scaled, axis=1, keepdims=True)
    return inverse * (adjusted - first_mean - scaled * second_mean)


def small_kernel(q_ref, k_ref, v_ref, o_ref, ctrl_ref, one_ref, two_ref, out_ref):
    rows, experts = ctrl_ref.shape
    for i, ref in enumerate((q_ref, k_ref, v_ref, o_ref)):
        out_ref[:, i * D : (i + 1) * D] = ref[...].astype(bf16)
    square = (rows, rows)
    own = lax.broadcasted_iota(jnp.int32, square, 0) == lax.broadcasted_iota(jnp.int32, square, 1)
    one = jnp.sum(jnp.where(own, one_ref[...], 0.0), axis=1, keepdims=True)
    two = jnp.sum(jnp.where(own, two_ref[...], 0.0), axis=1, keepdims=True)
    lane = lax.broadcasted_iota(jnp.int32, (rows, LANES), 1)
    gains = jnp.where(lane == GAIN_ONE, one, jnp.where(lane == GAIN_TWO, two, 0.0))
    out_ref[:, 4 * D :] = gains.astype(bf16)
    out_ref[:, 4 * D : 4 * D + experts] = ctrl_ref[...].astype(bf16)


def pack_small(weights, ctrl, gain_one, gain_two):
    rows, experts = ctrl.shape
    width = 4 * D + LANES
    return call(
        small_kernel,
        1,
        [fixed(rows, D)] * 4 + [fixed(rows, experts), fixed(1, rows), fixed(1, rows)],
        fixed(rows, width),
        jax.ShapeDtypeStruct((rows, width), bf16),
        [],
        100_000,
        200_000,
        "pack_small",
    )(*weights, ctrl, gain_one.reshape(1, rows), gain_two.reshape(1, rows))


def gain_of(ctrl_block, lane):
    pick = (lax.broadcasted_iota(jnp.int32, (16, LANES), 1) == lane).astype(bf16)
    return against_rows(pick, ctrl_block)[:1]


def pack_kernel(first_ref, bias_ref, second_ref, out_ref):
    held, _, hidden = first_ref.shape
    for i in range(held):
        out_ref[i, :D, :] = first_ref[i].astype(bf16)
        out_ref[i, D : D + BIAS_ROWS, :] = jnp.broadcast_to(
            bias_ref[pl.ds(pl.program_id(0) * held + i, 1), :], (BIAS_ROWS, hidden)
        ).astype(bf16)
        for c in range(D // hidden):
            start = D + BIAS_ROWS + c * hidden
            out_ref[i, start : start + hidden, :] = second_ref[
                i, :, c * hidden : (c + 1) * hidden
            ].astype(bf16)


def pack_weights(w_in, b_in, w_exp_out):
    local, _, hidden = w_in.shape
    total = 2 * D + BIAS_ROWS
    return call(
        pack_kernel,
        local // 2,
        [leading(2, D, hidden), fixed(local, hidden), leading(2, hidden, D)],
        leading(2, total, hidden),
        jax.ShapeDtypeStruct((local, total, hidden), bf16),
        [],
        1_000_000,
        12 * 2**20,
        "pack_weights",
    )(w_in, b_in, w_exp_out)


def unpack_kernel(in_ref, first_ref, bias_ref, second_ref):
    hidden = first_ref.shape[2]
    first_ref[0] = in_ref[0, :D, :].astype(f32)
    bias_ref[pl.ds(pl.program_id(0), 1), :] = in_ref[0, D : D + BIAS_ROWS, :].astype(f32)[:1]
    for c in range(D // hidden):
        start = D + BIAS_ROWS + c * hidden
        second_ref[0, :, c * hidden : (c + 1) * hidden] = in_ref[
            0, start : start + hidden, :
        ].astype(f32)


def unpack_grads(packed):
    local, total, hidden = packed.shape
    return call(
        unpack_kernel,
        local,
        [leading(1, total, hidden)],
        [leading(1, D, hidden), fixed(local, hidden), leading(1, hidden, D)],
        [
            jax.ShapeDtypeStruct((local, D, hidden), f32),
            jax.ShapeDtypeStruct((local, hidden), f32),
            jax.ShapeDtypeStruct((local, hidden, D), f32),
        ],
        [],
        1_000_000,
        12 * 2**20,
        "unpack_grads",
    )(packed)


def expert_products(rows_ref, w_ref, i):
    hidden = w_ref.shape[2]
    bias = w_ref[i, D : D + BIAS_ROWS, :].astype(f32)[:1]
    pre_act = product(rows_ref[:, :D], w_ref[i, :D, :]) + bias
    hidden_grad = jnp.zeros_like(pre_act)
    for c in range(D // hidden):
        start = D + BIAS_ROWS + c * hidden
        cols = slice(D + c * hidden, D + (c + 1) * hidden)
        hidden_grad = hidden_grad + against_rows(
            rows_ref[:, cols], w_ref[i, start : start + hidden, :]
        )
    return pre_act, hidden_grad


def activate(pre_act, hidden_grad):
    sigma = 0.5 + 0.5 * jnp.tanh(0.5 * pre_act)
    slope = sigma * (1.0 + pre_act * (1.0 - sigma))
    pre_grad = (hidden_grad.astype(bf16).astype(f32) * slope).astype(bf16)
    return (pre_act * sigma).astype(bf16), pre_grad


def expert_kernel(rows_ref, w_ref, out_ref, results, mixed_grad):
    step = pl.program_id(0)
    held, _, hidden = w_ref.shape
    chunks = D // hidden
    parts = [None] * (chunks + 1)
    later = expert_products(rows_ref, w_ref, 0)
    for i in range(held):
        now = later
        if i + 1 < held:
            later = expert_products(rows_ref, w_ref, i + 1)
        active, pre_grad = activate(*now)
        more = []
        for c in range(chunks):
            start = D + BIAS_ROWS + c * hidden
            more.append(product(active, w_ref[i, start : start + hidden, :]))
        more.append(against_rows(pre_grad, w_ref[i, :D, :]))
        parts = more if i == 0 else [old + new for old, new in zip(parts, more)]

    @pl.when(step == 0)
    def _():
        for c in range(chunks):
            results[:, c * hidden : (c + 1) * hidden] = parts[c]
        mixed_grad[...] = parts[chunks]

    @pl.when(step > 0)
    def _():
        for c in range(chunks):
            cols = slice(c * hidden, (c + 1) * hidden)
            results[:, cols] = results[:, cols] + parts[c]
        mixed_grad[...] = mixed_grad[...] + parts[chunks]

    @pl.when(step == pl.num_programs(0) - 1)
    def _():
        out_ref[:, :D] = results[...].astype(bf16)
        out_ref[:, D:] = mixed_grad[...].astype(bf16)


def expert_rows(rows, weights):
    count = rows.shape[0]
    shards, total, hidden = weights.shape
    return call(
        expert_kernel,
        shards // SHARDS_A_STEP,
        [fixed(count, 2 * D), leading(SHARDS_A_STEP, total, hidden)],
        fixed(count, 2 * D),
        jax.ShapeDtypeStruct((count, 2 * D), bf16),
        [pltpu.VMEM((count, D), f32), pltpu.VMEM((count, D), f32)],
        8 * count * D * shards * hidden,
        8 * 2**20,
        "expert_rows",
    )(rows, weights)


def expert_grad_kernel(rows_ref, w_ref, out_ref, rows_t):
    hidden = out_ref.shape[2]

    @pl.when(pl.program_id(0) == 0)
    def _():
        rows_t[...] = rows_ref[:, :D].T

    active, pre_grad = activate(*expert_products(rows_ref, w_ref, 0))
    out_ref[0, :D, :] = product(rows_t[...], pre_grad).astype(bf16)
    out_ref[0, D : D + BIAS_ROWS, :] = jnp.broadcast_to(
        jnp.sum(pre_grad.astype(f32), axis=0, keepdims=True), (BIAS_ROWS, hidden)
    ).astype(bf16)
    active_t = active.T
    for c in range(D // hidden):
        start = D + BIAS_ROWS + c * hidden
        out_ref[0, start : start + hidden, :] = product(
            active_t, rows_ref[:, D + c * hidden : D + (c + 1) * hidden]
        ).astype(bf16)


def expert_grads(rows, weights):
    count = rows.shape[0]
    shards, total, hidden = weights.shape
    return call(
        expert_grad_kernel,
        shards,
        [fixed(count, 2 * D), leading(1, total, hidden)],
        leading(1, total, hidden),
        jax.ShapeDtypeStruct((shards, total, hidden), bf16),
        [pltpu.VMEM((D, count), bf16)],
        8 * count * D * shards * hidden,
        14 * 2**20,
        "expert_grads",
        63,
    )(rows, weights)


def project_kernel(tokens_ref, w_ref, ctrl_ref, qkv_ref, normed_t_ref):
    scaled, _ = normalise(tokens_ref[...].astype(f32))
    normed = (scaled * gain_of(ctrl_ref[...], GAIN_ONE)).astype(bf16)
    normed_t_ref[...] = normed.T
    qkv_ref[...] = product(normed, w_ref[...]).astype(bf16)


def project(tokens, small):
    length = tokens.shape[0]
    return call(
        project_kernel,
        length // CHUNK,
        [leading(CHUNK, D), small_columns(3 * D, 0), small_columns(LANES, 4 * D)],
        [leading(CHUNK, 3 * D), pl.BlockSpec((D, CHUNK), lambda i: (0, i))],
        [jax.ShapeDtypeStruct((length, 3 * D), bf16), jax.ShapeDtypeStruct((D, length), bf16)],
        [],
        6 * length * D * D,
        12 * 2**20,
        "project",
    )(tokens, small, small)


def choose(probs, routes):
    columns = routes.shape[1]
    shape = (LANES, columns)
    onehot = (lax.broadcasted_iota(jnp.int32, shape, 0) == routes).astype(bf16)
    tokens = probs.shape[0]
    own = lax.broadcasted_iota(jnp.int32, (tokens, columns), 0) // GROUP == (
        lax.broadcasted_iota(jnp.int32, (tokens, columns), 1) // ROUTES
    )
    chosen = jnp.where(own, product(probs.astype(bf16), onehot), 0.0).astype(bf16)
    return chosen, onehot, own


def mix_kernel(
    attended_ref, tokens_ref, grad_ref, wo_ref, ctrl_ref, routes_ref, slots_ref,
    residual_ref, probs_ref, out_ref, rows,
):
    step = pl.program_id(0)
    residual = tokens_ref[...].astype(f32) + product(attended_ref[...], wo_ref[...])
    residual_ref[...] = residual
    scaled, _ = normalise(residual)
    normed = (scaled * gain_of(ctrl_ref[...], GAIN_TWO)).astype(bf16)
    logits = product(normed, ctrl_ref[...]).reshape(CHUNK // GROUP, GROUP, LANES)
    weights = jnp.exp(logits - jnp.max(logits, axis=1, keepdims=True))
    probs = (weights / jnp.sum(weights, axis=1, keepdims=True)).reshape(CHUNK, LANES)
    probs_ref[...] = probs
    chosen, _, _ = choose(probs, routes_ref[0])
    columns = chosen.shape[1]
    here = pl.ds(pl.multiple_of(step * columns, columns), columns)
    rows[here, :D] = transposed_product(chosen, normed).astype(bf16)
    rows[here, D:] = transposed_product(chosen, grad_ref[...]).astype(bf16)

    @pl.when(step == pl.num_programs(0) - 1)
    def _():
        shape = (out_ref.shape[0], rows.shape[0])
        dispatch = (lax.broadcasted_iota(jnp.int32, shape, 0) == slots_ref[...]).astype(bf16)
        out_ref[...] = product(dispatch, rows[...]).astype(bf16)


def mix(attended, tokens, grad_out, small, routes, slots, slot_count):
    length = tokens.shape[0]
    steps = length // CHUNK
    count = slots.shape[0]
    return call(
        mix_kernel,
        steps,
        [leading(CHUNK, D)] * 3
        + [small_columns(D, 3 * D), small_columns(LANES, 4 * D)]
        + [leading(1, 1, count // steps), fixed(1, count)],
        [leading(CHUNK, D), leading(CHUNK, LANES), fixed(slot_count, 2 * D)],
        [
            jax.ShapeDtypeStruct((length, D), f32),
            jax.ShapeDtypeStruct((length, LANES), f32),
            jax.ShapeDtypeStruct((slot_count, 2 * D), bf16),
        ],
        [pltpu.VMEM((count, 2 * D), bf16)],
        4 * length * D * D,
        14 * 2**20,
        "mix",
    )(
        attended, tokens, grad_out, small, small,
        routes.reshape(steps, 1, count // steps), slots.reshape(1, count),
    )


def combine_kernel(
    residual_ref, grad_ref, probs_ref, attended_ref, wo_ref, ctrl_ref, routes_ref,
    slots_ref, back_ref, output_ref, residual_grad_ref, attended_grad_ref, sums_ref, gain_sum,
):
    step = pl.program_id(0)
    gain = gain_of(ctrl_ref[...], GAIN_TWO)
    residual = residual_ref[...]
    scaled, inverse = normalise(residual)
    normed = (scaled * gain).astype(bf16)
    probs = probs_ref[...]
    grad = grad_ref[...]
    chosen, onehot, own = choose(probs, routes_ref[0])
    shape = (chosen.shape[1], back_ref.shape[0])
    collect = (lax.broadcasted_iota(jnp.int32, shape, 1) == slots_ref[...]).astype(bf16)
    rows = product(collect, back_ref[...]).astype(bf16)
    results = rows[:, :D]
    mixed_grad = rows[:, D:]
    output_ref[...] = (residual + product(chosen, results)).astype(bf16)
    chosen_grad = jnp.where(own, against_rows(grad, results) + against_rows(normed, mixed_grad), 0.0)
    high = chosen_grad.astype(bf16)
    low = (chosen_grad - high.astype(f32)).astype(bf16)
    prob_grad = against_rows(high, onehot) + against_rows(low, onehot)
    weighted = (probs * prob_grad).reshape(COMBINE // GROUP, GROUP, LANES)
    total = jnp.broadcast_to(jnp.sum(weighted, axis=1, keepdims=True), weighted.shape)
    logit_grad = (probs * (prob_grad - total.reshape(COMBINE, LANES))).astype(bf16)
    normed_grad = product(chosen, mixed_grad) + against_rows(logit_grad, ctrl_ref[...])
    gain_part = jnp.sum(normed_grad * scaled, axis=0, keepdims=True)
    residual_grad = grad.astype(f32) + norm_input_grad(normed_grad, scaled, inverse, gain)
    residual_grad_ref[...] = residual_grad
    branch = residual_grad.astype(bf16)
    attended_grad_ref[...] = against_rows(wo_ref[...], branch).astype(bf16)
    wo_part = transposed_product(attended_ref[...], branch)
    ctrl_part = transposed_product(normed, logit_grad)

    @pl.when(step == 0)
    def _():
        sums_ref[:, :D] = wo_part
        sums_ref[:, D:] = ctrl_part
        gain_sum[...] = gain_part

    @pl.when(step > 0)
    def _():
        sums_ref[:, :D] = sums_ref[:, :D] + wo_part
        sums_ref[:, D:] = sums_ref[:, D:] + ctrl_part
        gain_sum[...] = gain_sum[...] + gain_part

    @pl.when(step == pl.num_programs(0) - 1)
    def _():
        column = jnp.broadcast_to(gain_sum[...], (LANES, D)).T
        lane = lax.broadcasted_iota(jnp.int32, (D, LANES), 1)
        sums_ref[:, D:] = jnp.where(lane == LANES - 1, column, sums_ref[:, D:])


def combine(residual, grad_out, probs, attended, small, routes, slots, back):
    length = residual.shape[0]
    steps = length // COMBINE
    count = slots.shape[0]
    return call(
        combine_kernel,
        steps,
        [leading(COMBINE, D), leading(COMBINE, D), leading(COMBINE, LANES), leading(COMBINE, D)]
        + [small_columns(D, 3 * D), small_columns(LANES, 4 * D), leading(1, 1, count // steps)]
        + [leading(count // steps, 1), fixed(*back.shape)],
        [leading(COMBINE, D)] * 2
        + [pl.BlockSpec((D, COMBINE), lambda i: (0, i)), fixed(D, D + LANES)],
        [
            jax.ShapeDtypeStruct((length, D), bf16),
            jax.ShapeDtypeStruct((length, D), f32),
            jax.ShapeDtypeStruct((D, length), bf16),
            jax.ShapeDtypeStruct((D, D + LANES), f32),
        ],
        [pltpu.VMEM((1, D), f32)],
        6 * length * D * D,
        24 * 2**20,
        "combine",
        63,
    )(
        residual, grad_out, probs, attended, small, small,
        routes.reshape(steps, 1, count // steps), slots.reshape(count, 1), back,
    )


def weight_grad_kernel(core_ref, normed_t_ref, grad_ref, sums_ref, away_ref, kept_ref):
    step = pl.program_id(0)
    count, rows, _ = kept_ref.shape
    for x in range(count):
        mine = pl.ds(pl.multiple_of((2 * x + core_ref[0]) * rows, rows), rows)
        other = pl.ds(pl.multiple_of((2 * x + 1 - core_ref[0]) * rows, rows), rows)
        kept = product(normed_t_ref[mine, :], grad_ref[0])
        away = product(normed_t_ref[other, :], grad_ref[0]).astype(bf16)
        for i in range(3):

            @pl.when(step == i)
            def _(x=x, i=i, kept=kept, away=away):
                kept_ref[x, :, i * D : (i + 1) * D] = kept
                away_ref[x, :, i * D : (i + 1) * D] = away

        @pl.when(step == 0)
        def _(x=x, mine=mine, other=other):
            kept_ref[x, :, 3 * D :] = sums_ref[mine, :]
            away_ref[x, :, 3 * D :] = sums_ref[other, :].astype(bf16)


def weight_grads(normed_t, grads, sums, core, n_expert):
    length = normed_t.shape[1]
    width = sums.shape[1]
    shape = (n_expert // 2, D // n_expert, 3 * D + width)
    return call(
        weight_grad_kernel,
        3,
        [pl.BlockSpec(memory_space=pltpu.SMEM), fixed(D, length), leading(1, length, D)]
        + [fixed(D, width)],
        [fixed(*shape), fixed(*shape)],
        [jax.ShapeDtypeStruct(shape, bf16), jax.ShapeDtypeStruct(shape, f32)],
        [],
        6 * length * D * D,
        12 * 2**20,
        "weight_grads",
    )(core, normed_t, grads, sums)


def input_grad_kernel(grads_ref, w_ref, ctrl_ref, tokens_ref, residual_grad_ref, out_ref):
    upstream = against_rows(grads_ref[0], w_ref[:, :D])
    upstream = upstream + against_rows(grads_ref[1], w_ref[:, D : 2 * D])
    upstream = upstream + against_rows(grads_ref[2], w_ref[:, 2 * D :])
    scaled, inverse = normalise(tokens_ref[...].astype(f32))
    gain = gain_of(ctrl_ref[...], GAIN_ONE)
    out_ref[...] = (
        residual_grad_ref[...] + norm_input_grad(upstream, scaled, inverse, gain)
    ).astype(bf16)


def input_grads(grads, small, tokens, residual_grad):
    length = tokens.shape[0]
    return call(
        input_grad_kernel,
        length // CHUNK,
        [pl.BlockSpec((3, CHUNK, D), lambda i: (0, i, 0))]
        + [small_columns(3 * D, 0), small_columns(LANES, 4 * D)]
        + [leading(CHUNK, D), leading(CHUNK, D)],
        leading(CHUNK, D),
        jax.ShapeDtypeStruct((length, D), bf16),
        [],
        6 * length * D * D,
        18 * 2**20,
        "input_grads",
    )(grads, small, small, tokens, residual_grad)


def finish_kernel(pieces_ref, own_ref, q_ref, k_ref, v_ref, o_ref, ctrl_ref, one_ref, two_ref):
    rows, experts = ctrl_ref.shape
    total = jnp.sum(pieces_ref[...].astype(f32), axis=0)
    own = own_ref[...].astype(f32)
    for i, ref in enumerate((q_ref, k_ref, v_ref, o_ref)):
        ref[...] = total[:, i * D : (i + 1) * D]
    ctrl_ref[...] = total[:, 4 * D : 4 * D + experts]
    lane = lax.broadcasted_iota(jnp.int32, (rows, LANES), 1)

    def column(block, which):
        return jnp.sum(jnp.where(lane == which, block[:, 4 * D :], 0.0), axis=1, keepdims=True)

    one = jnp.sum(total[:, : 3 * D] * own[:, : 3 * D], axis=1, keepdims=True) / column(own, GAIN_ONE)
    square = (rows, rows)
    same = lax.broadcasted_iota(jnp.int32, square, 0) == lax.broadcasted_iota(jnp.int32, square, 1)
    one_ref[...] = jnp.sum(jnp.where(same, one, 0.0), axis=0, keepdims=True)
    two_ref[...] = jnp.sum(jnp.where(same, column(total, GAIN_TWO), 0.0), axis=0, keepdims=True)


def finish(pieces, own, experts):
    count, rows, width = pieces.shape
    outs = [(rows, D)] * 4 + [(rows, experts), (1, rows), (1, rows)]
    return call(
        finish_kernel,
        1,
        [fixed(count, rows, width), fixed(rows, width)],
        [fixed(*shape) for shape in outs],
        [jax.ShapeDtypeStruct(shape, f32) for shape in outs],
        [],
        1_000_000,
        1_000_000,
        "finish",
        8,
    )(pieces, own)


def swap(block, axis, bits):
    size = lax.axis_size(axis)
    return lax.ppermute(block, axis, [(i, i ^ bits) for i in range(size)])


def halves(size):
    inner = 1
    while inner * inner * 4 <= size:
        inner *= 2
    return size // inner, inner


def spread(block, size, stride, place):
    held = jnp.zeros((size,) + block.shape, block.dtype)
    held = lax.dynamic_update_slice(held, block[None], (place, 0, 0))
    for k in range(1, size):
        got = swap(block, "shard", k * stride)
        held = lax.dynamic_update_slice(held, got[None], (place ^ k, 0, 0))
    return held.reshape(-1, block.shape[1])


def gather_expert(held):
    n_expert = lax.axis_size("expert")
    mine = lax.axis_index("expert")
    rows, width = held.shape
    bit = n_expert // 2
    steps = 0
    while bit:
        got = swap(held, "expert", bit)
        low = (mine & bit) == 0
        held = jnp.stack([jnp.where(low, held, got), jnp.where(low, got, held)])
        bit //= 2
        steps += 1
    order = tuple(range(steps - 1, -1, -1)) + (steps, steps + 1)
    return held.transpose(order).reshape(n_expert * rows, width)


def sum_expert(away, kept):
    n_expert = lax.axis_size("expert")
    mine = lax.axis_index("expert")
    width = kept.shape[-1]
    steps = n_expert.bit_length() - 1
    held = kept + swap(away, "expert", 1).astype(f32)
    held = held.reshape((2,) * (steps - 1) + (-1, width))
    for step in range(1, steps):
        bit = 1 << step
        axis = steps - 1 - step
        high = (mine & bit) >> step
        away = lax.dynamic_index_in_dim(held, high ^ 1, axis, keepdims=False).astype(bf16)
        kept = lax.dynamic_index_in_dim(held, high, axis, keepdims=False)
        held = kept + swap(away, "expert", bit).astype(f32)
    return held


def along_shard(blocks):
    return lax.all_to_all(blocks, "shard", split_axis=0, concat_axis=0, tiled=True)


def to_experts(array, copies):
    if copies > 1:
        array = jnp.repeat(array, copies, axis=0)
    return along_shard(array)


def from_experts(array, copies):
    back = along_shard(array)
    if copies > 1:
        back = back.astype(f32).reshape((-1, copies) + back.shape[1:]).sum(axis=1)
    return back


def exchange(rows, copies):
    n_expert = lax.axis_size("expert")
    n_shard = lax.axis_size("shard")
    groups = None
    if copies > 1:
        groups = [
            [e * n_shard + s for e in range(n_expert) for s in range(p, n_shard, copies)]
            for p in range(copies)
        ]
    return lax.all_to_all(
        rows, BOTH, split_axis=0, concat_axis=0, tiled=True, axis_index_groups=groups
    )


def slots_of(routes, experts):
    groups = routes.shape[0]
    named = (routes[:, :, None] == jnp.arange(experts, dtype=jnp.int32)[None, None, :]).astype(f32)
    earlier = jnp.tril(jnp.ones((groups, groups), f32), -1).astype(bf16)
    before = product(earlier, jnp.sum(named, axis=1).astype(bf16))
    rank = jnp.sum(named * before[:, None, :], axis=2).astype(jnp.int32)
    return (routes * CAP + rank).reshape(-1)


def body(
    tokens,
    ln1_gain,
    ln2_gain,
    w_query,
    w_key,
    w_value,
    w_attn_out,
    w_ctrl,
    w_in,
    b_in,
    w_exp_out,
    routes,
    grad_out,
):
    experts = w_ctrl.shape[1]
    n_shard = lax.axis_size("shard")
    copies = n_shard * lax.axis_size("expert") // experts
    slots = slots_of(routes, experts)

    own = pack_small(
        (w_query, w_key, w_value, w_attn_out), w_ctrl, ln1_gain, ln2_gain
    )
    outer, inner = halves(n_shard)
    here = lax.axis_index("shard")
    held = spread(own, inner, 1, here & (inner - 1))
    held, w_in, w_exp_out = lax.optimization_barrier((held, w_in, w_exp_out))
    expert_w = to_experts(pack_weights(w_in, b_in, w_exp_out), copies)
    held = spread(held, outer, inner, here >> (inner.bit_length() - 1))
    small = gather_expert(held)

    qkv, normed_t = project(tokens, small)
    attended, lse, query_t, key_t, attended_t = attention_forward(qkv)
    residual, probs, outgoing = mix(
        attended, tokens, grad_out, small, routes, slots, experts * CAP
    )
    outgoing, expert_w = lax.optimization_barrier((outgoing, expert_w))
    arrived = exchange(outgoing, copies)
    results = expert_rows(arrived, expert_w)
    returned = exchange(results, copies)
    expert_sums = expert_grads(arrived, expert_w)
    returned, expert_sums = lax.optimization_barrier((returned, expert_sums))
    expert_sums = from_experts(expert_sums, copies)
    output, residual_grad, grad_t, sums = combine(
        residual, grad_out, probs, attended, small, routes, slots, returned
    )
    grads = attention_backward(qkv, query_t, key_t, grad_t, attended_t, lse)
    core = (lax.axis_index("expert") & 1).reshape(1)
    away, kept = weight_grads(normed_t, grads, sums, core, lax.axis_size("expert"))
    late = sum_expert(away, kept)
    input_grad = input_grads(grads, small, tokens, residual_grad)
    late, input_grad, expert_sums = lax.optimization_barrier((late, input_grad, expert_sums))
    pieces = along_shard(late.astype(bf16).reshape((n_shard,) + own.shape))
    w_in_grad, b_in_grad, w_exp_out_grad = unpack_grads(expert_sums)
    wq_grad, wk_grad, wv_grad, wo_grad, wc_grad, ln1_grad, ln2_grad = finish(pieces, own, experts)
    return (
        output,
        input_grad,
        ln1_grad.reshape(-1),
        ln2_grad.reshape(-1),
        wq_grad,
        wk_grad,
        wv_grad,
        wo_grad,
        wc_grad,
        w_in_grad,
        b_in_grad,
        w_exp_out_grad,
    )


def solution(mesh):
    rows = P(BOTH, None)
    vector = P(BOTH)
    experts = (P("expert", None, "shard"), P("expert", "shard"), P("expert", "shard", None))
    in_specs = (rows, vector, vector) + (rows,) * 5 + experts + (rows, rows)
    out_specs = (rows, rows, vector, vector) + (rows,) * 5 + experts
    return jax.shard_map(body, mesh=mesh, in_specs=in_specs, out_specs=out_specs, check_vma=False)
```

```python
import jax
import jax.numpy as jnp
from jax import lax
from jax.experimental import pallas as pl
from jax.experimental.pallas import tpu as pltpu
from jax.sharding import PartitionSpec as P

D = 512
HEAD_DIM = 64
GROUP = 32
ROUTES = 8
BLOCK = 256
CAP = 24
EPSILON = 1e-05
SCALE = 0.125 * 1.4426950408889634
BOTH = ("expert", "shard")

bf16 = jnp.bfloat16
f32 = jnp.float32


def vmem(mebibytes):
    return pltpu.CompilerParams(vmem_limit_bytes=mebibytes * 2**20)


def product(left_op, right_op):
    return jnp.dot(left_op, right_op, preferred_element_type=f32)


def transposed_product(left_op, right_op):
    return lax.dot_general(left_op, right_op, (((0,), (0,)), ((), ())), preferred_element_type=f32)


def against_rows(left_op, right_op):
    return lax.dot_general(left_op, right_op, (((1,), (1,)), ((), ())), preferred_element_type=f32)


def attention_forward_kernel(q_ref, k_ref, v_ref, o_ref, lse_ref, qt_ref, kt_ref, ot_ref):
    length = q_ref.shape[0]
    q_t = q_ref[...].T
    qt_ref[...] = q_t
    kt_ref[...] = k_ref[...].T
    v_t = v_ref[...].T
    zero = jnp.zeros((HEAD_DIM, length), bf16)
    ones = jnp.ones((16, length), bf16)
    halves_q = [q_t[:HEAD_DIM], q_t[HEAD_DIM:]]
    sides = [
        jnp.concatenate([halves_q[0], zero], 0),
        jnp.concatenate([zero, halves_q[1]], 0),
    ]
    values = [
        jnp.concatenate([v_t[:HEAD_DIM], ones], 0),
        jnp.concatenate([v_t[HEAD_DIM:], ones], 0),
    ]

    def scores_of(b, h):
        n = (b + 1) * BLOCK
        return product(k_ref[:n, :], sides[h][:, b * BLOCK : n])

    items = [(b, h) for b in range(length // BLOCK) for h in range(2)]
    outs = []
    later = scores_of(*items[0])
    for i, (b, h) in enumerate(items):
        n = (b + 1) * BLOCK
        cols = slice(b * BLOCK, n)
        scores = later
        if i + 1 < len(items):
            later = scores_of(*items[i + 1])
        top = jnp.max(scores, axis=0, keepdims=True) * SCALE
        weights = jnp.exp2(scores * SCALE - top).astype(bf16)
        out = product(values[h][:, :n], weights)
        total = out[HEAD_DIM : HEAD_DIM + 1]
        outs.append(out[:HEAD_DIM] / total)
        lse_ref[0, h : h + 1, cols] = top + jnp.log2(total)
        if h == 1:
            both = jnp.concatenate(outs, 0).astype(bf16)
            ot_ref[:, cols] = both
            o_ref[cols, :] = both.T
            outs = []


def attention_backward_kernel(
    q_ref, v_ref, qt_ref, kt_ref, gt_ref, ot_ref, lse_ref, out_ref, dq_t, stats
):
    length = q_ref.shape[0]
    q_t = qt_ref[...]
    k_t = kt_ref[...]
    g_t = gt_ref[...]
    q = q_ref[...]
    g = g_t.T
    v_t = v_ref[...].T
    both = g_t.astype(f32) * ot_ref[...].astype(f32)
    rows_of = [slice(0, HEAD_DIM), slice(HEAD_DIM, 2 * HEAD_DIM)]
    lines = [lse_ref[0]] + [jnp.sum(both[rows], axis=0, keepdims=True) for rows in rows_of]
    columns = jnp.concatenate(lines + [jnp.zeros((4, length), f32)], 0).T
    for i in range(4):
        stats[i] = jnp.broadcast_to(columns[:, i : i + 1], (length, 2 * HEAD_DIM))
    zero = jnp.zeros((HEAD_DIM, length), bf16)
    k_sides = [
        jnp.concatenate([k_t[:HEAD_DIM], zero], 0),
        jnp.concatenate([zero, k_t[HEAD_DIM:]], 0),
    ]
    v_sides = [
        jnp.concatenate([v_t[:HEAD_DIM], zero], 0),
        jnp.concatenate([zero, v_t[HEAD_DIM:]], 0),
    ]

    def stat(i, lo):
        half = stats[i, lo:, :]
        return jnp.concatenate([half, half], 1)

    def products_of(j, h):
        here = slice(j * BLOCK, (j + 1) * BLOCK)
        return (
            product(q[j * BLOCK :], k_sides[h][:, here]),
            product(g[j * BLOCK :], v_sides[h][:, here]),
        )

    items = [(j, h) for j in range(length // BLOCK) for h in range(2)]
    key_grads = []
    value_grads = []
    later = products_of(*items[0])
    for i, (j, h) in enumerate(items):
        lo = j * BLOCK
        here = slice(lo, lo + BLOCK)
        rows = rows_of[h]
        scores, share_grad = later
        if i + 1 < len(items):
            later = products_of(*items[i + 1])
        shares = jnp.exp2(scores * SCALE - stat(h, lo))
        score_grad = (shares * (share_grad - stat(2 + h, lo))).astype(bf16)
        value_grads.append(product(g_t[rows, lo:], shares.astype(bf16)))
        key_grads.append(product(q_t[rows, lo:], score_grad))
        query_part = against_rows(k_t[rows, here], score_grad)
        if j == 0:
            dq_t[rows, :] = query_part
        else:
            dq_t[rows, lo:] = dq_t[rows, lo:] + query_part
        if h == 1:
            out_ref[1, here, :] = (jnp.concatenate(key_grads, 0) * 0.125).astype(bf16).T
            out_ref[2, here, :] = jnp.concatenate(value_grads, 0).astype(bf16).T
            key_grads = []
            value_grads = []
    out_ref[0] = (dq_t[...] * 0.125).astype(bf16).T


def pair_columns(length, offset):
    return pl.BlockSpec((length, 2 * HEAD_DIM), lambda pair: (0, pair + offset))


def pair_rows(length):
    return pl.BlockSpec((2 * HEAD_DIM, length), lambda pair: (pair, 0))


def attention_forward(qkv):
    length = qkv.shape[0]
    pairs = D // (2 * HEAD_DIM)
    stats = pl.BlockSpec((1, 2, length), lambda pair: (pair, 0, 0))
    return pl.pallas_call(
        attention_forward_kernel,
        grid=(pairs,),
        in_specs=[pair_columns(length, i * pairs) for i in range(3)],
        out_specs=[pair_columns(length, 0), stats] + [pair_rows(length)] * 3,
        out_shape=[
            jax.ShapeDtypeStruct((length, D), bf16),
            jax.ShapeDtypeStruct((pairs, 2, length), f32),
        ]
        + [jax.ShapeDtypeStruct((D, length), bf16)] * 3,
        compiler_params=vmem(56),
        cost_estimate=pl.CostEstimate(
            flops=10_000_000_000, bytes_accessed=8 * 2**20, transcendentals=0
        ),
        name="attention_forward",
    )(qkv, qkv, qkv)


def attention_backward(qkv, query_t, key_t, grad_t, attended_t, lse):
    length = qkv.shape[0]
    pairs = D // (2 * HEAD_DIM)
    stats = pl.BlockSpec((1, 2, length), lambda pair: (pair, 0, 0))
    return pl.pallas_call(
        attention_backward_kernel,
        grid=(pairs,),
        in_specs=[pair_columns(length, 0), pair_columns(length, 2 * pairs)]
        + [pair_rows(length)] * 4
        + [stats],
        out_specs=pl.BlockSpec((3, length, 2 * HEAD_DIM), lambda pair: (0, 0, pair)),
        out_shape=jax.ShapeDtypeStruct((3, length, D), bf16),
        scratch_shapes=[
            pltpu.VMEM((2 * HEAD_DIM, length), f32),
            pltpu.VMEM((4, length, 2 * HEAD_DIM), f32),
        ],
        compiler_params=vmem(56),
        cost_estimate=pl.CostEstimate(
            flops=50_000_000_000, bytes_accessed=16 * 2**20, transcendentals=20_000_000
        ),
        name="attention_backward",
    )(qkv, qkv, query_t, key_t, grad_t, attended_t, lse)


CHUNK = 256
COMBINE = 512
LANES = 128
BIAS_ROWS = 16
SHARDS_A_STEP = 4
GAIN_ONE = LANES - 2
GAIN_TWO = LANES - 1


def call(kernel, grid, in_specs, out_specs, out_shape, scratch, flops, moved, name, limit=56):
    return pl.pallas_call(
        kernel,
        grid=(grid,),
        in_specs=in_specs,
        out_specs=out_specs,
        out_shape=out_shape,
        scratch_shapes=scratch,
        compiler_params=vmem(limit),
        cost_estimate=pl.CostEstimate(flops=flops, bytes_accessed=moved, transcendentals=0),
        name=name,
    )


def fixed(*shape):
    return pl.BlockSpec(shape, lambda i: (0,) * len(shape))


def small_columns(width, start):
    return pl.BlockSpec((D, width), lambda i: (0, start // width))


def leading(*shape):
    return pl.BlockSpec(shape, lambda i: (i,) + (0,) * (len(shape) - 1))


def normalise(matrix):
    average = jnp.mean(matrix, axis=1, keepdims=True)
    centered = matrix - average
    inverse = lax.rsqrt(jnp.mean(centered * centered, axis=1, keepdims=True) + EPSILON)
    return centered * inverse, inverse


def norm_input_grad(upstream, scaled, inverse, gain):
    adjusted = upstream * gain
    first_mean = jnp.mean(adjusted, axis=1, keepdims=True)
    second_mean = jnp.mean(adjusted * scaled, axis=1, keepdims=True)
    return inverse * (adjusted - first_mean - scaled * second_mean)


def small_kernel(q_ref, k_ref, v_ref, o_ref, ctrl_ref, one_ref, two_ref, out_ref):
    rows, experts = ctrl_ref.shape
    for i, ref in enumerate((q_ref, k_ref, v_ref, o_ref)):
        out_ref[:, i * D : (i + 1) * D] = ref[...].astype(bf16)
    square = (rows, rows)
    own = lax.broadcasted_iota(jnp.int32, square, 0) == lax.broadcasted_iota(jnp.int32, square, 1)
    one = jnp.sum(jnp.where(own, one_ref[...], 0.0), axis=1, keepdims=True)
    two = jnp.sum(jnp.where(own, two_ref[...], 0.0), axis=1, keepdims=True)
    lane = lax.broadcasted_iota(jnp.int32, (rows, LANES), 1)
    gains = jnp.where(lane == GAIN_ONE, one, jnp.where(lane == GAIN_TWO, two, 0.0))
    out_ref[:, 4 * D :] = gains.astype(bf16)
    out_ref[:, 4 * D : 4 * D + experts] = ctrl_ref[...].astype(bf16)


def pack_small(weights, ctrl, gain_one, gain_two):
    rows, experts = ctrl.shape
    width = 4 * D + LANES
    return call(
        small_kernel,
        1,
        [fixed(rows, D)] * 4 + [fixed(rows, experts), fixed(1, rows), fixed(1, rows)],
        fixed(rows, width),
        jax.ShapeDtypeStruct((rows, width), bf16),
        [],
        100_000,
        200_000,
        "pack_small",
    )(*weights, ctrl, gain_one.reshape(1, rows), gain_two.reshape(1, rows))


def gain_of(ctrl_block, lane):
    pick = (lax.broadcasted_iota(jnp.int32, (16, LANES), 1) == lane).astype(bf16)
    return against_rows(pick, ctrl_block)[:1]


def pack_kernel(first_ref, bias_ref, second_ref, out_ref):
    held, _, hidden = first_ref.shape
    for i in range(held):
        out_ref[i, :D, :] = first_ref[i].astype(bf16)
        out_ref[i, D : D + BIAS_ROWS, :] = jnp.broadcast_to(
            bias_ref[pl.ds(pl.program_id(0) * held + i, 1), :], (BIAS_ROWS, hidden)
        ).astype(bf16)
        for c in range(D // hidden):
            start = D + BIAS_ROWS + c * hidden
            out_ref[i, start : start + hidden, :] = second_ref[
                i, :, c * hidden : (c + 1) * hidden
            ].astype(bf16)


def pack_weights(w_in, b_in, w_exp_out):
    local, _, hidden = w_in.shape
    total = 2 * D + BIAS_ROWS
    return call(
        pack_kernel,
        local // 2,
        [leading(2, D, hidden), fixed(local, hidden), leading(2, hidden, D)],
        leading(2, total, hidden),
        jax.ShapeDtypeStruct((local, total, hidden), bf16),
        [],
        1_000_000,
        12 * 2**20,
        "pack_weights",
    )(w_in, b_in, w_exp_out)


def unpack_kernel(in_ref, first_ref, bias_ref, second_ref):
    hidden = first_ref.shape[2]
    first_ref[0] = in_ref[0, :D, :].astype(f32)
    bias_ref[pl.ds(pl.program_id(0), 1), :] = in_ref[0, D : D + BIAS_ROWS, :].astype(f32)[:1]
    for c in range(D // hidden):
        start = D + BIAS_ROWS + c * hidden
        second_ref[0, :, c * hidden : (c + 1) * hidden] = in_ref[
            0, start : start + hidden, :
        ].astype(f32)


def unpack_grads(packed):
    local, total, hidden = packed.shape
    return call(
        unpack_kernel,
        local,
        [leading(1, total, hidden)],
        [leading(1, D, hidden), fixed(local, hidden), leading(1, hidden, D)],
        [
            jax.ShapeDtypeStruct((local, D, hidden), f32),
            jax.ShapeDtypeStruct((local, hidden), f32),
            jax.ShapeDtypeStruct((local, hidden, D), f32),
        ],
        [],
        1_000_000,
        12 * 2**20,
        "unpack_grads",
    )(packed)


def expert_products(rows_ref, w_ref, i):
    hidden = w_ref.shape[2]
    bias = w_ref[i, D : D + BIAS_ROWS, :].astype(f32)[:1]
    pre_act = product(rows_ref[:, :D], w_ref[i, :D, :]) + bias
    hidden_grad = jnp.zeros_like(pre_act)
    for c in range(D // hidden):
        start = D + BIAS_ROWS + c * hidden
        cols = slice(D + c * hidden, D + (c + 1) * hidden)
        hidden_grad = hidden_grad + against_rows(
            rows_ref[:, cols], w_ref[i, start : start + hidden, :]
        )
    return pre_act, hidden_grad


def activate(pre_act, hidden_grad):
    sigma = 0.5 + 0.5 * jnp.tanh(0.5 * pre_act)
    slope = sigma * (1.0 + pre_act * (1.0 - sigma))
    pre_grad = (hidden_grad.astype(bf16).astype(f32) * slope).astype(bf16)
    return (pre_act * sigma).astype(bf16), pre_grad


def expert_kernel(rows_ref, w_ref, out_ref, results, mixed_grad):
    step = pl.program_id(0)
    held, _, hidden = w_ref.shape
    chunks = D // hidden
    parts = [None] * (chunks + 1)
    later = expert_products(rows_ref, w_ref, 0)
    for i in range(held):
        now = later
        if i + 1 < held:
            later = expert_products(rows_ref, w_ref, i + 1)
        active, pre_grad = activate(*now)
        more = []
        for c in range(chunks):
            start = D + BIAS_ROWS + c * hidden
            more.append(product(active, w_ref[i, start : start + hidden, :]))
        more.append(against_rows(pre_grad, w_ref[i, :D, :]))
        parts = more if i == 0 else [old + new for old, new in zip(parts, more)]

    @pl.when(step == 0)
    def _():
        for c in range(chunks):
            results[:, c * hidden : (c + 1) * hidden] = parts[c]
        mixed_grad[...] = parts[chunks]

    @pl.when(step > 0)
    def _():
        for c in range(chunks):
            cols = slice(c * hidden, (c + 1) * hidden)
            results[:, cols] = results[:, cols] + parts[c]
        mixed_grad[...] = mixed_grad[...] + parts[chunks]

    @pl.when(step == pl.num_programs(0) - 1)
    def _():
        out_ref[:, :D] = results[...].astype(bf16)
        out_ref[:, D:] = mixed_grad[...].astype(bf16)


def expert_rows(rows, weights):
    count = rows.shape[0]
    shards, total, hidden = weights.shape
    return call(
        expert_kernel,
        shards // SHARDS_A_STEP,
        [fixed(count, 2 * D), leading(SHARDS_A_STEP, total, hidden)],
        fixed(count, 2 * D),
        jax.ShapeDtypeStruct((count, 2 * D), bf16),
        [pltpu.VMEM((count, D), f32), pltpu.VMEM((count, D), f32)],
        8 * count * D * shards * hidden,
        8 * 2**20,
        "expert_rows",
    )(rows, weights)


def expert_grad_kernel(rows_ref, w_ref, out_ref, rows_t):
    hidden = out_ref.shape[2]

    @pl.when(pl.program_id(0) == 0)
    def _():
        rows_t[...] = rows_ref[:, :D].T

    active, pre_grad = activate(*expert_products(rows_ref, w_ref, 0))
    out_ref[0, :D, :] = product(rows_t[...], pre_grad).astype(bf16)
    out_ref[0, D : D + BIAS_ROWS, :] = jnp.broadcast_to(
        jnp.sum(pre_grad.astype(f32), axis=0, keepdims=True), (BIAS_ROWS, hidden)
    ).astype(bf16)
    active_t = active.T
    for c in range(D // hidden):
        start = D + BIAS_ROWS + c * hidden
        out_ref[0, start : start + hidden, :] = product(
            active_t, rows_ref[:, D + c * hidden : D + (c + 1) * hidden]
        ).astype(bf16)


def expert_grads(rows, weights):
    count = rows.shape[0]
    shards, total, hidden = weights.shape
    return call(
        expert_grad_kernel,
        shards,
        [fixed(count, 2 * D), leading(1, total, hidden)],
        leading(1, total, hidden),
        jax.ShapeDtypeStruct((shards, total, hidden), bf16),
        [pltpu.VMEM((D, count), bf16)],
        8 * count * D * shards * hidden,
        14 * 2**20,
        "expert_grads",
        63,
    )(rows, weights)


def project_kernel(tokens_ref, w_ref, ctrl_ref, qkv_ref, normed_t_ref):
    scaled, _ = normalise(tokens_ref[...].astype(f32))
    normed = (scaled * gain_of(ctrl_ref[...], GAIN_ONE)).astype(bf16)
    normed_t_ref[...] = normed.T
    qkv_ref[...] = product(normed, w_ref[...]).astype(bf16)


def project(tokens, small):
    length = tokens.shape[0]
    return call(
        project_kernel,
        length // CHUNK,
        [leading(CHUNK, D), small_columns(3 * D, 0), small_columns(LANES, 4 * D)],
        [leading(CHUNK, 3 * D), pl.BlockSpec((D, CHUNK), lambda i: (0, i))],
        [jax.ShapeDtypeStruct((length, 3 * D), bf16), jax.ShapeDtypeStruct((D, length), bf16)],
        [],
        6 * length * D * D,
        12 * 2**20,
        "project",
    )(tokens, small, small)


def choose(probs, routes):
    columns = routes.shape[1]
    shape = (LANES, columns)
    onehot = (lax.broadcasted_iota(jnp.int32, shape, 0) == routes).astype(bf16)
    tokens = probs.shape[0]
    own = lax.broadcasted_iota(jnp.int32, (tokens, columns), 0) // GROUP == (
        lax.broadcasted_iota(jnp.int32, (tokens, columns), 1) // ROUTES
    )
    chosen = jnp.where(own, product(probs.astype(bf16), onehot), 0.0).astype(bf16)
    return chosen, onehot, own


def mix_kernel(
    attended_ref, tokens_ref, grad_ref, wo_ref, ctrl_ref, routes_ref, slots_ref,
    residual_ref, probs_ref, out_ref, rows,
):
    step = pl.program_id(0)
    residual = tokens_ref[...].astype(f32) + product(attended_ref[...], wo_ref[...])
    residual_ref[...] = residual
    scaled, _ = normalise(residual)
    normed = (scaled * gain_of(ctrl_ref[...], GAIN_TWO)).astype(bf16)
    logits = product(normed, ctrl_ref[...]).reshape(CHUNK // GROUP, GROUP, LANES)
    weights = jnp.exp(logits - jnp.max(logits, axis=1, keepdims=True))
    probs = (weights / jnp.sum(weights, axis=1, keepdims=True)).reshape(CHUNK, LANES)
    probs_ref[...] = probs
    chosen, _, _ = choose(probs, routes_ref[0])
    columns = chosen.shape[1]
    here = pl.ds(pl.multiple_of(step * columns, columns), columns)
    rows[here, :D] = transposed_product(chosen, normed).astype(bf16)
    rows[here, D:] = transposed_product(chosen, grad_ref[...]).astype(bf16)

    @pl.when(step == pl.num_programs(0) - 1)
    def _():
        shape = (out_ref.shape[0], rows.shape[0])
        dispatch = (lax.broadcasted_iota(jnp.int32, shape, 0) == slots_ref[...]).astype(bf16)
        out_ref[...] = product(dispatch, rows[...]).astype(bf16)


def mix(attended, tokens, grad_out, small, routes, slots, slot_count):
    length = tokens.shape[0]
    steps = length // CHUNK
    count = slots.shape[0]
    return call(
        mix_kernel,
        steps,
        [leading(CHUNK, D)] * 3
        + [small_columns(D, 3 * D), small_columns(LANES, 4 * D)]
        + [leading(1, 1, count // steps), fixed(1, count)],
        [leading(CHUNK, D), leading(CHUNK, LANES), fixed(slot_count, 2 * D)],
        [
            jax.ShapeDtypeStruct((length, D), f32),
            jax.ShapeDtypeStruct((length, LANES), f32),
            jax.ShapeDtypeStruct((slot_count, 2 * D), bf16),
        ],
        [pltpu.VMEM((count, 2 * D), bf16)],
        4 * length * D * D,
        14 * 2**20,
        "mix",
    )(
        attended, tokens, grad_out, small, small,
        routes.reshape(steps, 1, count // steps), slots.reshape(1, count),
    )


def combine_kernel(
    residual_ref, grad_ref, probs_ref, attended_ref, wo_ref, ctrl_ref, routes_ref,
    slots_ref, back_ref, output_ref, residual_grad_ref, attended_grad_ref, sums_ref, gain_sum,
):
    step = pl.program_id(0)
    gain = gain_of(ctrl_ref[...], GAIN_TWO)
    residual = residual_ref[...]
    scaled, inverse = normalise(residual)
    normed = (scaled * gain).astype(bf16)
    probs = probs_ref[...]
    grad = grad_ref[...]
    chosen, onehot, own = choose(probs, routes_ref[0])
    shape = (chosen.shape[1], back_ref.shape[0])
    collect = (lax.broadcasted_iota(jnp.int32, shape, 1) == slots_ref[...]).astype(bf16)
    rows = product(collect, back_ref[...]).astype(bf16)
    results = rows[:, :D]
    mixed_grad = rows[:, D:]
    output_ref[...] = (residual + product(chosen, results)).astype(bf16)
    chosen_grad = jnp.where(own, against_rows(grad, results) + against_rows(normed, mixed_grad), 0.0)
    high = chosen_grad.astype(bf16)
    low = (chosen_grad - high.astype(f32)).astype(bf16)
    prob_grad = against_rows(high, onehot) + against_rows(low, onehot)
    weighted = (probs * prob_grad).reshape(COMBINE // GROUP, GROUP, LANES)
    total = jnp.broadcast_to(jnp.sum(weighted, axis=1, keepdims=True), weighted.shape)
    logit_grad = (probs * (prob_grad - total.reshape(COMBINE, LANES))).astype(bf16)
    normed_grad = product(chosen, mixed_grad) + against_rows(logit_grad, ctrl_ref[...])
    gain_part = jnp.sum(normed_grad * scaled, axis=0, keepdims=True)
    residual_grad = grad.astype(f32) + norm_input_grad(normed_grad, scaled, inverse, gain)
    residual_grad_ref[...] = residual_grad
    branch = residual_grad.astype(bf16)
    attended_grad_ref[...] = against_rows(wo_ref[...], branch).astype(bf16)
    wo_part = transposed_product(attended_ref[...], branch)
    ctrl_part = transposed_product(normed, logit_grad)

    @pl.when(step == 0)
    def _():
        sums_ref[:, :D] = wo_part
        sums_ref[:, D:] = ctrl_part
        gain_sum[...] = gain_part

    @pl.when(step > 0)
    def _():
        sums_ref[:, :D] = sums_ref[:, :D] + wo_part
        sums_ref[:, D:] = sums_ref[:, D:] + ctrl_part
        gain_sum[...] = gain_sum[...] + gain_part

    @pl.when(step == pl.num_programs(0) - 1)
    def _():
        column = jnp.broadcast_to(gain_sum[...], (LANES, D)).T
        lane = lax.broadcasted_iota(jnp.int32, (D, LANES), 1)
        sums_ref[:, D:] = jnp.where(lane == LANES - 1, column, sums_ref[:, D:])


def combine(residual, grad_out, probs, attended, small, routes, slots, back):
    length = residual.shape[0]
    steps = length // COMBINE
    count = slots.shape[0]
    return call(
        combine_kernel,
        steps,
        [leading(COMBINE, D), leading(COMBINE, D), leading(COMBINE, LANES), leading(COMBINE, D)]
        + [small_columns(D, 3 * D), small_columns(LANES, 4 * D), leading(1, 1, count // steps)]
        + [leading(count // steps, 1), fixed(*back.shape)],
        [leading(COMBINE, D)] * 2
        + [pl.BlockSpec((D, COMBINE), lambda i: (0, i)), fixed(D, D + LANES)],
        [
            jax.ShapeDtypeStruct((length, D), bf16),
            jax.ShapeDtypeStruct((length, D), f32),
            jax.ShapeDtypeStruct((D, length), bf16),
            jax.ShapeDtypeStruct((D, D + LANES), f32),
        ],
        [pltpu.VMEM((1, D), f32)],
        6 * length * D * D,
        24 * 2**20,
        "combine",
        63,
    )(
        residual, grad_out, probs, attended, small, small,
        routes.reshape(steps, 1, count // steps), slots.reshape(count, 1), back,
    )


def weight_grad_kernel(core_ref, normed_t_ref, grad_ref, sums_ref, away_ref, kept_ref):
    step = pl.program_id(0)
    count, rows, _ = kept_ref.shape
    for x in range(count):
        mine = pl.ds(pl.multiple_of((2 * x + core_ref[0]) * rows, rows), rows)
        other = pl.ds(pl.multiple_of((2 * x + 1 - core_ref[0]) * rows, rows), rows)
        kept = product(normed_t_ref[mine, :], grad_ref[0])
        away = product(normed_t_ref[other, :], grad_ref[0]).astype(bf16)
        for i in range(3):

            @pl.when(step == i)
            def _(x=x, i=i, kept=kept, away=away):
                kept_ref[x, :, i * D : (i + 1) * D] = kept
                away_ref[x, :, i * D : (i + 1) * D] = away

        @pl.when(step == 0)
        def _(x=x, mine=mine, other=other):
            kept_ref[x, :, 3 * D :] = sums_ref[mine, :]
            away_ref[x, :, 3 * D :] = sums_ref[other, :].astype(bf16)


def weight_grads(normed_t, grads, sums, core, n_expert):
    length = normed_t.shape[1]
    width = sums.shape[1]
    shape = (n_expert // 2, D // n_expert, 3 * D + width)
    return call(
        weight_grad_kernel,
        3,
        [pl.BlockSpec(memory_space=pltpu.SMEM), fixed(D, length), leading(1, length, D)]
        + [fixed(D, width)],
        [fixed(*shape), fixed(*shape)],
        [jax.ShapeDtypeStruct(shape, bf16), jax.ShapeDtypeStruct(shape, f32)],
        [],
        6 * length * D * D,
        12 * 2**20,
        "weight_grads",
    )(core, normed_t, grads, sums)


def input_grad_kernel(grads_ref, w_ref, ctrl_ref, tokens_ref, residual_grad_ref, out_ref):
    upstream = against_rows(grads_ref[0], w_ref[:, :D])
    upstream = upstream + against_rows(grads_ref[1], w_ref[:, D : 2 * D])
    upstream = upstream + against_rows(grads_ref[2], w_ref[:, 2 * D :])
    scaled, inverse = normalise(tokens_ref[...].astype(f32))
    gain = gain_of(ctrl_ref[...], GAIN_ONE)
    out_ref[...] = (
        residual_grad_ref[...] + norm_input_grad(upstream, scaled, inverse, gain)
    ).astype(bf16)


def input_grads(grads, small, tokens, residual_grad):
    length = tokens.shape[0]
    return call(
        input_grad_kernel,
        length // CHUNK,
        [pl.BlockSpec((3, CHUNK, D), lambda i: (0, i, 0))]
        + [small_columns(3 * D, 0), small_columns(LANES, 4 * D)]
        + [leading(CHUNK, D), leading(CHUNK, D)],
        leading(CHUNK, D),
        jax.ShapeDtypeStruct((length, D), bf16),
        [],
        6 * length * D * D,
        18 * 2**20,
        "input_grads",
    )(grads, small, small, tokens, residual_grad)


def finish_kernel(pieces_ref, own_ref, q_ref, k_ref, v_ref, o_ref, ctrl_ref, one_ref, two_ref):
    rows, experts = ctrl_ref.shape
    total = jnp.sum(pieces_ref[...].astype(f32), axis=0)
    own = own_ref[...].astype(f32)
    for i, ref in enumerate((q_ref, k_ref, v_ref, o_ref)):
        ref[...] = total[:, i * D : (i + 1) * D]
    ctrl_ref[...] = total[:, 4 * D : 4 * D + experts]
    lane = lax.broadcasted_iota(jnp.int32, (rows, LANES), 1)

    def column(block, which):
        return jnp.sum(jnp.where(lane == which, block[:, 4 * D :], 0.0), axis=1, keepdims=True)

    one = jnp.sum(total[:, : 3 * D] * own[:, : 3 * D], axis=1, keepdims=True) / column(own, GAIN_ONE)
    square = (rows, rows)
    same = lax.broadcasted_iota(jnp.int32, square, 0) == lax.broadcasted_iota(jnp.int32, square, 1)
    one_ref[...] = jnp.sum(jnp.where(same, one, 0.0), axis=0, keepdims=True)
    two_ref[...] = jnp.sum(jnp.where(same, column(total, GAIN_TWO), 0.0), axis=0, keepdims=True)


def finish(pieces, own, experts):
    count, rows, width = pieces.shape
    outs = [(rows, D)] * 4 + [(rows, experts), (1, rows), (1, rows)]
    return call(
        finish_kernel,
        1,
        [fixed(count, rows, width), fixed(rows, width)],
        [fixed(*shape) for shape in outs],
        [jax.ShapeDtypeStruct(shape, f32) for shape in outs],
        [],
        1_000_000,
        1_000_000,
        "finish",
        8,
    )(pieces, own)


def swap(block, axis, bits):
    size = lax.axis_size(axis)
    return lax.ppermute(block, axis, [(i, i ^ bits) for i in range(size)])


def halves(size):
    inner = 1
    while inner * inner * 4 <= size:
        inner *= 2
    return size // inner, inner


def spread(block, size, stride, place):
    held = jnp.zeros((size,) + block.shape, block.dtype)
    held = lax.dynamic_update_slice(held, block[None], (place, 0, 0))
    for k in range(1, size):
        got = swap(block, "shard", k * stride)
        held = lax.dynamic_update_slice(held, got[None], (place ^ k, 0, 0))
    return held.reshape(-1, block.shape[1])


def gather_expert(held):
    n_expert = lax.axis_size("expert")
    mine = lax.axis_index("expert")
    rows, width = held.shape
    bit = n_expert // 2
    steps = 0
    while bit:
        got = swap(held, "expert", bit)
        low = (mine & bit) == 0
        held = jnp.stack([jnp.where(low, held, got), jnp.where(low, got, held)])
        bit //= 2
        steps += 1
    order = tuple(range(steps - 1, -1, -1)) + (steps, steps + 1)
    return held.transpose(order).reshape(n_expert * rows, width)


def sum_expert(away, kept):
    n_expert = lax.axis_size("expert")
    mine = lax.axis_index("expert")
    width = kept.shape[-1]
    steps = n_expert.bit_length() - 1
    held = kept + swap(away, "expert", 1).astype(f32)
    held = held.reshape((2,) * (steps - 1) + (-1, width))
    for step in range(1, steps):
        bit = 1 << step
        axis = steps - 1 - step
        high = (mine & bit) >> step
        away = lax.dynamic_index_in_dim(held, high ^ 1, axis, keepdims=False).astype(bf16)
        kept = lax.dynamic_index_in_dim(held, high, axis, keepdims=False)
        held = kept + swap(away, "expert", bit).astype(f32)
    return held


def along_shard(blocks):
    return lax.all_to_all(blocks, "shard", split_axis=0, concat_axis=0, tiled=True)


def to_experts(array, copies):
    if copies > 1:
        array = jnp.repeat(array, copies, axis=0)
    return along_shard(array)


def from_experts(array, copies):
    back = along_shard(array)
    if copies > 1:
        back = back.astype(f32).reshape((-1, copies) + back.shape[1:]).sum(axis=1)
    return back


def exchange(rows, copies):
    n_expert = lax.axis_size("expert")
    n_shard = lax.axis_size("shard")
    groups = None
    if copies > 1:
        groups = [
            [e * n_shard + s for e in range(n_expert) for s in range(p, n_shard, copies)]
            for p in range(copies)
        ]
    return lax.all_to_all(
        rows, BOTH, split_axis=0, concat_axis=0, tiled=True, axis_index_groups=groups
    )


def slots_of(routes, experts):
    groups = routes.shape[0]
    named = (routes[:, :, None] == jnp.arange(experts, dtype=jnp.int32)[None, None, :]).astype(f32)
    earlier = jnp.tril(jnp.ones((groups, groups), f32), -1).astype(bf16)
    before = product(earlier, jnp.sum(named, axis=1).astype(bf16))
    rank = jnp.sum(named * before[:, None, :], axis=2).astype(jnp.int32)
    return (routes * CAP + rank).reshape(-1)


def body(
    tokens,
    ln1_gain,
    ln2_gain,
    w_query,
    w_key,
    w_value,
    w_attn_out,
    w_ctrl,
    w_in,
    b_in,
    w_exp_out,
    routes,
    grad_out,
):
    experts = w_ctrl.shape[1]
    n_shard = lax.axis_size("shard")
    copies = n_shard * lax.axis_size("expert") // experts
    slots = slots_of(routes, experts)

    own = pack_small(
        (w_query, w_key, w_value, w_attn_out), w_ctrl, ln1_gain, ln2_gain
    )
    outer, inner = halves(n_shard)
    here = lax.axis_index("shard")
    held = spread(own, inner, 1, here & (inner - 1))
    held, w_in, w_exp_out = lax.optimization_barrier((held, w_in, w_exp_out))
    expert_w = to_experts(pack_weights(w_in, b_in, w_exp_out), copies)
    held = spread(held, outer, inner, here >> (inner.bit_length() - 1))
    small = gather_expert(held)

    qkv, normed_t = project(tokens, small)
    attended, lse, query_t, key_t, attended_t = attention_forward(qkv)
    residual, probs, outgoing = mix(
        attended, tokens, grad_out, small, routes, slots, experts * CAP
    )
    outgoing, expert_w = lax.optimization_barrier((outgoing, expert_w))
    arrived = exchange(outgoing, copies)
    results = expert_rows(arrived, expert_w)
    returned = exchange(results, copies)
    expert_sums = expert_grads(arrived, expert_w)
    returned, expert_sums = lax.optimization_barrier((returned, expert_sums))
    expert_sums = from_experts(expert_sums, copies)
    output, residual_grad, grad_t, sums = combine(
        residual, grad_out, probs, attended, small, routes, slots, returned
    )
    grads = attention_backward(qkv, query_t, key_t, grad_t, attended_t, lse)
    core = (lax.axis_index("expert") & 1).reshape(1)
    away, kept = weight_grads(normed_t, grads, sums, core, lax.axis_size("expert"))
    late = sum_expert(away, kept)
    input_grad = input_grads(grads, small, tokens, residual_grad)
    late, input_grad, expert_sums = lax.optimization_barrier((late, input_grad, expert_sums))
    pieces = along_shard(late.astype(bf16).reshape((n_shard,) + own.shape))
    w_in_grad, b_in_grad, w_exp_out_grad = unpack_grads(expert_sums)
    wq_grad, wk_grad, wv_grad, wo_grad, wc_grad, ln1_grad, ln2_grad = finish(pieces, own, experts)
    return (
        output,
        input_grad,
        ln1_grad.reshape(-1),
        ln2_grad.reshape(-1),
        wq_grad,
        wk_grad,
        wv_grad,
        wo_grad,
        wc_grad,
        w_in_grad,
        b_in_grad,
        w_exp_out_grad,
    )


def solution(mesh):
    rows = P(BOTH, None)
    vector = P(BOTH)
    experts = (P("expert", None, "shard"), P("expert", "shard"), P("expert", "shard", None))
    in_specs = (rows, vector, vector) + (rows,) * 5 + experts + (rows, rows)
    out_specs = (rows, rows, vector, vector) + (rows,) * 5 + experts
    return jax.shard_map(body, mesh=mesh, in_specs=in_specs, out_specs=out_specs, check_vma=False)
```

```python
import jax
import jax.numpy as jnp
from jax import lax
from jax.experimental import pallas as pl
from jax.experimental.pallas import tpu as pltpu
from jax.sharding import PartitionSpec as P

D = 512
HEAD_DIM = 64
GROUP = 32
ROUTES = 8
BLOCK = 256
CAP = 24
EPSILON = 1e-05
SCALE = 0.125 * 1.4426950408889634
BOTH = ("expert", "shard")

bf16 = jnp.bfloat16
f32 = jnp.float32


def vmem(mebibytes):
    return pltpu.CompilerParams(vmem_limit_bytes=mebibytes * 2**20)


def product(left_op, right_op):
    return jnp.dot(left_op, right_op, preferred_element_type=f32)


def transposed_product(left_op, right_op):
    return lax.dot_general(left_op, right_op, (((0,), (0,)), ((), ())), preferred_element_type=f32)


def against_rows(left_op, right_op):
    return lax.dot_general(left_op, right_op, (((1,), (1,)), ((), ())), preferred_element_type=f32)


def attention_forward_kernel(q_ref, k_ref, v_ref, o_ref, lse_ref, qt_ref, kt_ref, ot_ref):
    length = q_ref.shape[0]
    q_t = q_ref[...].T
    qt_ref[...] = q_t
    kt_ref[...] = k_ref[...].T
    v_t = v_ref[...].T
    zero = jnp.zeros((HEAD_DIM, length), bf16)
    ones = jnp.ones((16, length), bf16)
    halves_q = [q_t[:HEAD_DIM], q_t[HEAD_DIM:]]
    sides = [
        jnp.concatenate([halves_q[0], zero], 0),
        jnp.concatenate([zero, halves_q[1]], 0),
    ]
    values = [
        jnp.concatenate([v_t[:HEAD_DIM], ones], 0),
        jnp.concatenate([v_t[HEAD_DIM:], ones], 0),
    ]

    def scores_of(b, h):
        n = (b + 1) * BLOCK
        return product(k_ref[:n, :], sides[h][:, b * BLOCK : n])

    items = [(b, h) for b in range(length // BLOCK) for h in range(2)]
    outs = []
    later = scores_of(*items[0])
    for i, (b, h) in enumerate(items):
        n = (b + 1) * BLOCK
        cols = slice(b * BLOCK, n)
        scores = later
        if i + 1 < len(items):
            later = scores_of(*items[i + 1])
        top = jnp.max(scores, axis=0, keepdims=True) * SCALE
        weights = jnp.exp2(scores * SCALE - top).astype(bf16)
        out = product(values[h][:, :n], weights)
        total = out[HEAD_DIM : HEAD_DIM + 1]
        outs.append(out[:HEAD_DIM] / total)
        lse_ref[0, h : h + 1, cols] = top + jnp.log2(total)
        if h == 1:
            both = jnp.concatenate(outs, 0).astype(bf16)
            ot_ref[:, cols] = both
            o_ref[cols, :] = both.T
            outs = []


def attention_backward_kernel(
    q_ref, v_ref, qt_ref, kt_ref, gt_ref, ot_ref, lse_ref, out_ref, dq_t, stats
):
    length = q_ref.shape[0]
    q_t = qt_ref[...]
    k_t = kt_ref[...]
    g_t = gt_ref[...]
    q = q_ref[...]
    g = g_t.T
    v_t = v_ref[...].T
    both = g_t.astype(f32) * ot_ref[...].astype(f32)
    rows_of = [slice(0, HEAD_DIM), slice(HEAD_DIM, 2 * HEAD_DIM)]
    lines = [lse_ref[0]] + [jnp.sum(both[rows], axis=0, keepdims=True) for rows in rows_of]
    columns = jnp.concatenate(lines + [jnp.zeros((4, length), f32)], 0).T
    for i in range(4):
        stats[i] = jnp.broadcast_to(columns[:, i : i + 1], (length, 2 * HEAD_DIM))
    zero = jnp.zeros((HEAD_DIM, length), bf16)
    k_sides = [
        jnp.concatenate([k_t[:HEAD_DIM], zero], 0),
        jnp.concatenate([zero, k_t[HEAD_DIM:]], 0),
    ]
    v_sides = [
        jnp.concatenate([v_t[:HEAD_DIM], zero], 0),
        jnp.concatenate([zero, v_t[HEAD_DIM:]], 0),
    ]

    def stat(i, lo):
        half = stats[i, lo:, :]
        return jnp.concatenate([half, half], 1)

    def products_of(j, h):
        here = slice(j * BLOCK, (j + 1) * BLOCK)
        return (
            product(q[j * BLOCK :], k_sides[h][:, here]),
            product(g[j * BLOCK :], v_sides[h][:, here]),
        )

    items = [(j, h) for j in range(length // BLOCK) for h in range(2)]
    key_grads = []
    value_grads = []
    later = products_of(*items[0])
    for i, (j, h) in enumerate(items):
        lo = j * BLOCK
        here = slice(lo, lo + BLOCK)
        rows = rows_of[h]
        scores, share_grad = later
        if i + 1 < len(items):
            later = products_of(*items[i + 1])
        shares = jnp.exp2(scores * SCALE - stat(h, lo))
        score_grad = (shares * (share_grad - stat(2 + h, lo))).astype(bf16)
        value_grads.append(product(g_t[rows, lo:], shares.astype(bf16)))
        key_grads.append(product(q_t[rows, lo:], score_grad))
        query_part = against_rows(k_t[rows, here], score_grad)
        if j == 0:
            dq_t[rows, :] = query_part
        else:
            dq_t[rows, lo:] = dq_t[rows, lo:] + query_part
        if h == 1:
            out_ref[1, here, :] = (jnp.concatenate(key_grads, 0) * 0.125).astype(bf16).T
            out_ref[2, here, :] = jnp.concatenate(value_grads, 0).astype(bf16).T
            key_grads = []
            value_grads = []
    out_ref[0] = (dq_t[...] * 0.125).astype(bf16).T


def pair_columns(length, offset):
    return pl.BlockSpec((length, 2 * HEAD_DIM), lambda pair: (0, pair + offset))


def pair_rows(length):
    return pl.BlockSpec((2 * HEAD_DIM, length), lambda pair: (pair, 0))


def attention_forward(qkv):
    length = qkv.shape[0]
    pairs = D // (2 * HEAD_DIM)
    stats = pl.BlockSpec((1, 2, length), lambda pair: (pair, 0, 0))
    return pl.pallas_call(
        attention_forward_kernel,
        grid=(pairs,),
        in_specs=[pair_columns(length, i * pairs) for i in range(3)],
        out_specs=[pair_columns(length, 0), stats] + [pair_rows(length)] * 3,
        out_shape=[
            jax.ShapeDtypeStruct((length, D), bf16),
            jax.ShapeDtypeStruct((pairs, 2, length), f32),
        ]
        + [jax.ShapeDtypeStruct((D, length), bf16)] * 3,
        compiler_params=vmem(56),
        cost_estimate=pl.CostEstimate(
            flops=10_000_000_000, bytes_accessed=8 * 2**20, transcendentals=0
        ),
        name="attention_forward",
    )(qkv, qkv, qkv)


def attention_backward(qkv, query_t, key_t, grad_t, attended_t, lse):
    length = qkv.shape[0]
    pairs = D // (2 * HEAD_DIM)
    stats = pl.BlockSpec((1, 2, length), lambda pair: (pair, 0, 0))
    return pl.pallas_call(
        attention_backward_kernel,
        grid=(pairs,),
        in_specs=[pair_columns(length, 0), pair_columns(length, 2 * pairs)]
        + [pair_rows(length)] * 4
        + [stats],
        out_specs=pl.BlockSpec((3, length, 2 * HEAD_DIM), lambda pair: (0, 0, pair)),
        out_shape=jax.ShapeDtypeStruct((3, length, D), bf16),
        scratch_shapes=[
            pltpu.VMEM((2 * HEAD_DIM, length), f32),
            pltpu.VMEM((4, length, 2 * HEAD_DIM), f32),
        ],
        compiler_params=vmem(56),
        cost_estimate=pl.CostEstimate(
            flops=50_000_000_000, bytes_accessed=16 * 2**20, transcendentals=20_000_000
        ),
        name="attention_backward",
    )(qkv, qkv, query_t, key_t, grad_t, attended_t, lse)


CHUNK = 256
COMBINE = 512
LANES = 128
BIAS_LANE = 64
SHARDS_A_STEP = 4
GAIN_ONE = LANES - 2
GAIN_TWO = LANES - 1


def call(kernel, grid, in_specs, out_specs, out_shape, scratch, flops, moved, name, limit=56):
    return pl.pallas_call(
        kernel,
        grid=(grid,),
        in_specs=in_specs,
        out_specs=out_specs,
        out_shape=out_shape,
        scratch_shapes=scratch,
        compiler_params=vmem(limit),
        cost_estimate=pl.CostEstimate(flops=flops, bytes_accessed=moved, transcendentals=0),
        name=name,
    )


def fixed(*shape):
    return pl.BlockSpec(shape, lambda i: (0,) * len(shape))


def small_columns(width, start):
    return pl.BlockSpec((D, width), lambda i: (0, start // width))


def leading(*shape):
    return pl.BlockSpec(shape, lambda i: (i,) + (0,) * (len(shape) - 1))


def normalise(matrix):
    average = jnp.mean(matrix, axis=1, keepdims=True)
    centered = matrix - average
    inverse = lax.rsqrt(jnp.mean(centered * centered, axis=1, keepdims=True) + EPSILON)
    return centered * inverse, inverse


def norm_input_grad(upstream, scaled, inverse, gain):
    adjusted = upstream * gain
    first_mean = jnp.mean(adjusted, axis=1, keepdims=True)
    second_mean = jnp.mean(adjusted * scaled, axis=1, keepdims=True)
    return inverse * (adjusted - first_mean - scaled * second_mean)


def small_kernel(q_ref, k_ref, v_ref, o_ref, ctrl_ref, one_ref, two_ref, bias_ref, out_ref):
    rows, experts = ctrl_ref.shape
    for i, ref in enumerate((q_ref, k_ref, v_ref, o_ref)):
        out_ref[:, i * D : (i + 1) * D] = ref[...].astype(bf16)
    square = (rows, rows)
    own = lax.broadcasted_iota(jnp.int32, square, 0) == lax.broadcasted_iota(jnp.int32, square, 1)
    one = jnp.sum(jnp.where(own, one_ref[...], 0.0), axis=1, keepdims=True)
    two = jnp.sum(jnp.where(own, two_ref[...], 0.0), axis=1, keepdims=True)
    lane = lax.broadcasted_iota(jnp.int32, (rows, LANES), 1)
    gains = jnp.where(lane == GAIN_ONE, one, jnp.where(lane == GAIN_TWO, two, 0.0))
    out_ref[:, 4 * D : 4 * D + LANES] = gains.astype(bf16)
    out_ref[:, 4 * D : 4 * D + experts] = ctrl_ref[...].astype(bf16)
    parts = [bias_ref[:, c : c + LANES] for c in range(0, bias_ref.shape[1], LANES)]
    out_ref[:, 4 * D + LANES :] = jnp.concatenate(parts, 0).astype(bf16)


def pack_small(weights, ctrl, gain_one, gain_two, bias):
    rows, experts = ctrl.shape
    width = 4 * D + 2 * LANES
    return call(
        small_kernel,
        1,
        [fixed(rows, D)] * 4
        + [fixed(rows, experts), fixed(1, rows), fixed(1, rows), fixed(*bias.shape)],
        fixed(rows, width),
        jax.ShapeDtypeStruct((rows, width), bf16),
        [],
        100_000,
        200_000,
        "pack_small",
    )(*weights, ctrl, gain_one.reshape(1, rows), gain_two.reshape(1, rows), bias)


def gain_of(ctrl_block, lane):
    pick = (lax.broadcasted_iota(jnp.int32, (16, LANES), 1) == lane).astype(bf16)
    return against_rows(pick, ctrl_block)[:1]


def pack_kernel(first_ref, second_ref, out_ref):
    held, _, hidden = first_ref.shape
    for i in range(held):
        out_ref[i, :D, :] = first_ref[i].astype(bf16)
        for c in range(D // hidden):
            start = D + c * hidden
            out_ref[i, start : start + hidden, :] = second_ref[
                i, :, c * hidden : (c + 1) * hidden
            ].astype(bf16)


def pack_weights(w_in, w_exp_out):
    local, _, hidden = w_in.shape
    return call(
        pack_kernel,
        local // 2,
        [leading(2, D, hidden), leading(2, hidden, D)],
        leading(2, 2 * D, hidden),
        jax.ShapeDtypeStruct((local, 2 * D, hidden), bf16),
        [],
        1_000_000,
        12 * 2**20,
        "pack_weights",
    )(w_in, w_exp_out)


def unpack_kernel(in_ref, first_ref, second_ref):
    hidden = first_ref.shape[2]
    first_ref[0] = in_ref[0, :D, :].astype(f32)
    for c in range(D // hidden):
        start = D + c * hidden
        second_ref[0, :, c * hidden : (c + 1) * hidden] = in_ref[
            0, start : start + hidden, :
        ].astype(f32)


def unpack_grads(packed):
    local, total, hidden = packed.shape
    return call(
        unpack_kernel,
        local,
        [leading(1, total, hidden)],
        [leading(1, D, hidden), leading(1, hidden, D)],
        [
            jax.ShapeDtypeStruct((local, D, hidden), f32),
            jax.ShapeDtypeStruct((local, hidden, D), f32),
        ],
        [],
        1_000_000,
        12 * 2**20,
        "unpack_grads",
    )(packed)


def expert_products(rows_ref, w_ref, bias_ref, i, shard):
    hidden = w_ref.shape[2]
    pre_act = product(rows_ref[:, :D], w_ref[i, :D, :]) + bias_ref[pl.ds(shard, 1), :]
    hidden_grad = jnp.zeros_like(pre_act)
    for c in range(D // hidden):
        start = D + c * hidden
        cols = slice(D + c * hidden, D + (c + 1) * hidden)
        hidden_grad = hidden_grad + against_rows(
            rows_ref[:, cols], w_ref[i, start : start + hidden, :]
        )
    return pre_act, hidden_grad


def activate(pre_act, hidden_grad):
    sigma = 0.5 + 0.5 * jnp.tanh(0.5 * pre_act)
    slope = sigma * (1.0 + pre_act * (1.0 - sigma))
    pre_grad = (hidden_grad.astype(bf16).astype(f32) * slope).astype(bf16)
    return (pre_act * sigma).astype(bf16), pre_grad


def expert_kernel(rows_ref, w_ref, bias_ref, out_ref, results, mixed_grad):
    step = pl.program_id(0)
    held, _, hidden = w_ref.shape
    chunks = D // hidden
    parts = [None] * (chunks + 1)
    later = expert_products(rows_ref, w_ref, bias_ref, 0, step * held)
    for i in range(held):
        now = later
        if i + 1 < held:
            later = expert_products(rows_ref, w_ref, bias_ref, i + 1, step * held + i + 1)
        active, pre_grad = activate(*now)
        more = []
        for c in range(chunks):
            start = D + c * hidden
            more.append(product(active, w_ref[i, start : start + hidden, :]))
        more.append(against_rows(pre_grad, w_ref[i, :D, :]))
        parts = more if i == 0 else [old + new for old, new in zip(parts, more)]

    @pl.when(step == 0)
    def _():
        for c in range(chunks):
            results[:, c * hidden : (c + 1) * hidden] = parts[c]
        mixed_grad[...] = parts[chunks]

    @pl.when(step > 0)
    def _():
        for c in range(chunks):
            cols = slice(c * hidden, (c + 1) * hidden)
            results[:, cols] = results[:, cols] + parts[c]
        mixed_grad[...] = mixed_grad[...] + parts[chunks]

    @pl.when(step == pl.num_programs(0) - 1)
    def _():
        out_ref[:, :D] = results[...].astype(bf16)
        out_ref[:, D:] = mixed_grad[...].astype(bf16)


def expert_rows(rows, weights, bias):
    count = rows.shape[0]
    shards, total, hidden = weights.shape
    return call(
        expert_kernel,
        shards // SHARDS_A_STEP,
        [fixed(count, 2 * D), leading(SHARDS_A_STEP, total, hidden), fixed(shards, hidden)],
        fixed(count, 2 * D),
        jax.ShapeDtypeStruct((count, 2 * D), bf16),
        [pltpu.VMEM((count, D), f32), pltpu.VMEM((count, D), f32)],
        8 * count * D * shards * hidden,
        8 * 2**20,
        "expert_rows",
        40,
    )(rows, weights, bias)


def bias_places(rows, hidden):
    each = hidden // rows
    shape = (rows, hidden)
    owner = lax.broadcasted_iota(jnp.int32, shape, 1) // each == lax.broadcasted_iota(
        jnp.int32, shape, 0
    )
    shape = (LANES, hidden)
    lane = lax.broadcasted_iota(jnp.int32, shape, 1) % each + BIAS_LANE
    return owner, (lane == lax.broadcasted_iota(jnp.int32, shape, 0)).astype(bf16)


def expert_grad_kernel(rows_ref, w_ref, bias_ref, out_ref, sums_ref, rows_t):
    hidden = out_ref.shape[2]

    @pl.when(pl.program_id(0) == 0)
    def _():
        rows_t[...] = rows_ref[:, :D].T

    shard = pl.program_id(0)
    active, pre_grad = activate(*expert_products(rows_ref, w_ref, bias_ref, 0, shard))
    out_ref[0, :D, :] = product(rows_t[...], pre_grad).astype(bf16)
    bias_grad = jnp.sum(pre_grad.astype(f32), axis=0, keepdims=True)
    rows = sums_ref.shape[1]
    owner, lanes = bias_places(rows, hidden)
    parts = jnp.where(owner, bias_grad, 0.0).astype(bf16)
    sums_ref[0] = against_rows(parts, lanes).astype(bf16)
    active_t = active.T
    for c in range(D // hidden):
        start = D + c * hidden
        out_ref[0, start : start + hidden, :] = product(
            active_t, rows_ref[:, D + c * hidden : D + (c + 1) * hidden]
        ).astype(bf16)


def expert_grads(rows, weights, bias, block):
    count = rows.shape[0]
    shards, total, hidden = weights.shape
    return call(
        expert_grad_kernel,
        shards,
        [fixed(count, 2 * D), leading(1, total, hidden), fixed(shards, hidden)],
        [leading(1, total, hidden), leading(1, block, LANES)],
        [
            jax.ShapeDtypeStruct((shards, total, hidden), bf16),
            jax.ShapeDtypeStruct((shards, block, LANES), bf16),
        ],
        [pltpu.VMEM((D, count), bf16)],
        8 * count * D * shards * hidden,
        14 * 2**20,
        "expert_grads",
        63,
    )(rows, weights, bias)


def project_kernel(tokens_ref, w_ref, ctrl_ref, qkv_ref, normed_t_ref):
    scaled, _ = normalise(tokens_ref[...].astype(f32))
    normed = (scaled * gain_of(ctrl_ref[...], GAIN_ONE)).astype(bf16)
    normed_t_ref[...] = normed.T
    qkv_ref[...] = product(normed, w_ref[...]).astype(bf16)


def project(tokens, small):
    length = tokens.shape[0]
    return call(
        project_kernel,
        length // CHUNK,
        [leading(CHUNK, D), small_columns(3 * D, 0), small_columns(LANES, 4 * D)],
        [leading(CHUNK, 3 * D), pl.BlockSpec((D, CHUNK), lambda i: (0, i))],
        [jax.ShapeDtypeStruct((length, 3 * D), bf16), jax.ShapeDtypeStruct((D, length), bf16)],
        [],
        6 * length * D * D,
        12 * 2**20,
        "project",
    )(tokens, small, small)


def choose(probs, routes):
    columns = routes.shape[1]
    shape = (LANES, columns)
    onehot = (lax.broadcasted_iota(jnp.int32, shape, 0) == routes).astype(bf16)
    tokens = probs.shape[0]
    own = lax.broadcasted_iota(jnp.int32, (tokens, columns), 0) // GROUP == (
        lax.broadcasted_iota(jnp.int32, (tokens, columns), 1) // ROUTES
    )
    chosen = jnp.where(own, product(probs.astype(bf16), onehot), 0.0).astype(bf16)
    return chosen, onehot, own


def mix_kernel(
    attended_ref, tokens_ref, grad_ref, wo_ref, ctrl_ref, routes_ref, slots_ref,
    residual_ref, probs_ref, out_ref, rows,
):
    step = pl.program_id(0)
    residual = tokens_ref[...].astype(f32) + product(attended_ref[...], wo_ref[...])
    residual_ref[...] = residual
    scaled, _ = normalise(residual)
    normed = (scaled * gain_of(ctrl_ref[...], GAIN_TWO)).astype(bf16)
    logits = product(normed, ctrl_ref[...]).reshape(CHUNK // GROUP, GROUP, LANES)
    weights = jnp.exp(logits - jnp.max(logits, axis=1, keepdims=True))
    probs = (weights / jnp.sum(weights, axis=1, keepdims=True)).reshape(CHUNK, LANES)
    probs_ref[...] = probs
    chosen, _, _ = choose(probs, routes_ref[0])
    columns = chosen.shape[1]
    here = pl.ds(pl.multiple_of(step * columns, columns), columns)
    rows[here, :D] = transposed_product(chosen, normed).astype(bf16)
    rows[here, D:] = transposed_product(chosen, grad_ref[...]).astype(bf16)

    @pl.when(step == pl.num_programs(0) - 1)
    def _():
        shape = (out_ref.shape[0], rows.shape[0])
        dispatch = (lax.broadcasted_iota(jnp.int32, shape, 0) == slots_ref[...]).astype(bf16)
        out_ref[...] = product(dispatch, rows[...]).astype(bf16)


def mix(attended, tokens, grad_out, small, routes, slots, slot_count):
    length = tokens.shape[0]
    steps = length // CHUNK
    count = slots.shape[0]
    return call(
        mix_kernel,
        steps,
        [leading(CHUNK, D)] * 3
        + [small_columns(D, 3 * D), small_columns(LANES, 4 * D)]
        + [leading(1, 1, count // steps), fixed(1, count)],
        [leading(CHUNK, D), leading(CHUNK, LANES), fixed(slot_count, 2 * D)],
        [
            jax.ShapeDtypeStruct((length, D), f32),
            jax.ShapeDtypeStruct((length, LANES), f32),
            jax.ShapeDtypeStruct((slot_count, 2 * D), bf16),
        ],
        [pltpu.VMEM((count, 2 * D), bf16)],
        4 * length * D * D,
        14 * 2**20,
        "mix",
    )(
        attended, tokens, grad_out, small, small,
        routes.reshape(steps, 1, count // steps), slots.reshape(1, count),
    )


def combine_kernel(
    residual_ref, grad_ref, probs_ref, attended_ref, wo_ref, ctrl_ref, routes_ref,
    slots_ref, back_ref, output_ref, residual_grad_ref, attended_grad_ref, sums_ref, gain_sum,
):
    step = pl.program_id(0)
    gain = gain_of(ctrl_ref[...], GAIN_TWO)
    residual = residual_ref[...]
    scaled, inverse = normalise(residual)
    normed = (scaled * gain).astype(bf16)
    probs = probs_ref[...]
    grad = grad_ref[...]
    chosen, onehot, own = choose(probs, routes_ref[0])
    shape = (chosen.shape[1], back_ref.shape[0])
    collect = (lax.broadcasted_iota(jnp.int32, shape, 1) == slots_ref[...]).astype(bf16)
    rows = product(collect, back_ref[...]).astype(bf16)
    results = rows[:, :D]
    mixed_grad = rows[:, D:]
    output_ref[...] = (residual + product(chosen, results)).astype(bf16)
    chosen_grad = jnp.where(own, against_rows(grad, results) + against_rows(normed, mixed_grad), 0.0)
    high = chosen_grad.astype(bf16)
    low = (chosen_grad - high.astype(f32)).astype(bf16)
    prob_grad = against_rows(high, onehot) + against_rows(low, onehot)
    weighted = (probs * prob_grad).reshape(COMBINE // GROUP, GROUP, LANES)
    total = jnp.broadcast_to(jnp.sum(weighted, axis=1, keepdims=True), weighted.shape)
    logit_grad = (probs * (prob_grad - total.reshape(COMBINE, LANES))).astype(bf16)
    normed_grad = product(chosen, mixed_grad) + against_rows(logit_grad, ctrl_ref[...])
    gain_part = jnp.sum(normed_grad * scaled, axis=0, keepdims=True)
    residual_grad = grad.astype(f32) + norm_input_grad(normed_grad, scaled, inverse, gain)
    residual_grad_ref[...] = residual_grad
    branch = residual_grad.astype(bf16)
    attended_grad_ref[...] = against_rows(wo_ref[...], branch).astype(bf16)
    wo_part = transposed_product(attended_ref[...], branch)
    ctrl_part = transposed_product(normed, logit_grad)

    @pl.when(step == 0)
    def _():
        sums_ref[:, :D] = wo_part
        sums_ref[:, D:] = ctrl_part
        gain_sum[...] = gain_part

    @pl.when(step > 0)
    def _():
        sums_ref[:, :D] = sums_ref[:, :D] + wo_part
        sums_ref[:, D:] = sums_ref[:, D:] + ctrl_part
        gain_sum[...] = gain_sum[...] + gain_part

    @pl.when(step == pl.num_programs(0) - 1)
    def _():
        column = jnp.broadcast_to(gain_sum[...], (LANES, D)).T
        lane = lax.broadcasted_iota(jnp.int32, (D, LANES), 1)
        sums_ref[:, D:] = jnp.where(lane == LANES - 1, column, sums_ref[:, D:])


def combine(residual, grad_out, probs, attended, small, routes, slots, back):
    length = residual.shape[0]
    steps = length // COMBINE
    count = slots.shape[0]
    return call(
        combine_kernel,
        steps,
        [leading(COMBINE, D), leading(COMBINE, D), leading(COMBINE, LANES), leading(COMBINE, D)]
        + [small_columns(D, 3 * D), small_columns(LANES, 4 * D), leading(1, 1, count // steps)]
        + [leading(count // steps, 1), fixed(*back.shape)],
        [leading(COMBINE, D)] * 2
        + [pl.BlockSpec((D, COMBINE), lambda i: (0, i)), fixed(D, D + LANES)],
        [
            jax.ShapeDtypeStruct((length, D), bf16),
            jax.ShapeDtypeStruct((length, D), f32),
            jax.ShapeDtypeStruct((D, length), bf16),
            jax.ShapeDtypeStruct((D, D + LANES), f32),
        ],
        [pltpu.VMEM((1, D), f32)],
        6 * length * D * D,
        24 * 2**20,
        "combine",
        63,
    )(
        residual, grad_out, probs, attended, small, small,
        routes.reshape(steps, 1, count // steps), slots.reshape(count, 1), back,
    )


def weight_grad_kernel(core_ref, normed_t_ref, grad_ref, sums_ref, away_ref, kept_ref):
    step = pl.program_id(0)
    count, rows, _ = kept_ref.shape
    for x in range(count):
        mine = pl.ds(pl.multiple_of((2 * x + core_ref[0]) * rows, rows), rows)
        other = pl.ds(pl.multiple_of((2 * x + 1 - core_ref[0]) * rows, rows), rows)
        kept = product(normed_t_ref[mine, :], grad_ref[0])
        away = product(normed_t_ref[other, :], grad_ref[0]).astype(bf16)
        for i in range(3):

            @pl.when(step == i)
            def _(x=x, i=i, kept=kept, away=away):
                kept_ref[x, :, i * D : (i + 1) * D] = kept
                away_ref[x, :, i * D : (i + 1) * D] = away

        @pl.when(step == 0)
        def _(x=x, mine=mine, other=other):
            kept_ref[x, :, 3 * D :] = sums_ref[mine, :]
            away_ref[x, :, 3 * D :] = sums_ref[other, :].astype(bf16)


def weight_grads(normed_t, grads, sums, core, n_expert):
    length = normed_t.shape[1]
    width = sums.shape[1]
    shape = (n_expert // 2, D // n_expert, 3 * D + width)
    return call(
        weight_grad_kernel,
        3,
        [pl.BlockSpec(memory_space=pltpu.SMEM), fixed(D, length), leading(1, length, D)]
        + [fixed(D, width)],
        [fixed(*shape), fixed(*shape)],
        [jax.ShapeDtypeStruct(shape, bf16), jax.ShapeDtypeStruct(shape, f32)],
        [],
        6 * length * D * D,
        12 * 2**20,
        "weight_grads",
        24,
    )(core, normed_t, grads, sums)


def input_grad_kernel(grads_ref, w_ref, ctrl_ref, tokens_ref, residual_grad_ref, out_ref):
    upstream = against_rows(grads_ref[0], w_ref[:, :D])
    upstream = upstream + against_rows(grads_ref[1], w_ref[:, D : 2 * D])
    upstream = upstream + against_rows(grads_ref[2], w_ref[:, 2 * D :])
    scaled, inverse = normalise(tokens_ref[...].astype(f32))
    gain = gain_of(ctrl_ref[...], GAIN_ONE)
    out_ref[...] = (
        residual_grad_ref[...] + norm_input_grad(upstream, scaled, inverse, gain)
    ).astype(bf16)


def input_grads(grads, small, tokens, residual_grad):
    length = tokens.shape[0]
    return call(
        input_grad_kernel,
        length // CHUNK,
        [pl.BlockSpec((3, CHUNK, D), lambda i: (0, i, 0))]
        + [small_columns(3 * D, 0), small_columns(LANES, 4 * D)]
        + [leading(CHUNK, D), leading(CHUNK, D)],
        leading(CHUNK, D),
        jax.ShapeDtypeStruct((length, D), bf16),
        [],
        6 * length * D * D,
        18 * 2**20,
        "input_grads",
    )(grads, small, small, tokens, residual_grad)


def finish_kernel(
    pieces_ref, own_ref, q_ref, k_ref, v_ref, o_ref, ctrl_ref, one_ref, two_ref, bias_ref
):
    rows, experts = ctrl_ref.shape
    total = jnp.sum(pieces_ref[...].astype(f32), axis=0)
    own = own_ref[...].astype(f32)
    for i, ref in enumerate((q_ref, k_ref, v_ref, o_ref)):
        ref[...] = total[:, i * D : (i + 1) * D]
    ctrl_ref[...] = total[:, 4 * D : 4 * D + experts]
    lane = lax.broadcasted_iota(jnp.int32, (rows, LANES), 1)

    def column(block, which):
        return jnp.sum(jnp.where(lane == which, block[:, 4 * D : 4 * D + LANES], 0.0), axis=1, keepdims=True)

    one = jnp.sum(total[:, : 3 * D] * own[:, : 3 * D], axis=1, keepdims=True) / column(own, GAIN_ONE)
    square = (rows, rows)
    same = lax.broadcasted_iota(jnp.int32, square, 0) == lax.broadcasted_iota(jnp.int32, square, 1)
    one_ref[...] = jnp.sum(jnp.where(same, one, 0.0), axis=0, keepdims=True)
    two_ref[...] = jnp.sum(jnp.where(same, column(total, GAIN_TWO), 0.0), axis=0, keepdims=True)
    local, hidden = bias_ref.shape
    owner, lanes = bias_places(rows, hidden)
    copies = pieces_ref.shape[0] // local
    for e in range(local):
        for i in range(copies):
            part = product(pieces_ref[e * copies + i, :, 4 * D :], lanes)
            line = jnp.sum(jnp.where(owner, part, 0.0), axis=0, keepdims=True)
            bias_ref[e : e + 1, :] = line if i == 0 else bias_ref[e : e + 1, :] + line


def finish(pieces, own, experts, bias_shape):
    count, rows, width = pieces.shape
    outs = [(rows, D)] * 4 + [(rows, experts), (1, rows), (1, rows), bias_shape]
    return call(
        finish_kernel,
        1,
        [fixed(count, rows, width), fixed(*own.shape)],
        [fixed(*shape) for shape in outs],
        [jax.ShapeDtypeStruct(shape, f32) for shape in outs],
        [],
        1_000_000,
        1_000_000,
        "finish",
        8,
    )(pieces, own)


def swap(block, axis, bits):
    size = lax.axis_size(axis)
    return lax.ppermute(block, axis, [(i, i ^ bits) for i in range(size)])


def halves(size):
    inner = 1
    while inner * inner * 4 <= size:
        inner *= 2
    return size // inner, inner


def spread(block, size, stride, place):
    held = jnp.zeros((size,) + block.shape, block.dtype)
    held = lax.dynamic_update_slice(held, block[None], (place, 0, 0))
    for k in range(1, size):
        got = swap(block, "shard", k * stride)
        held = lax.dynamic_update_slice(held, got[None], (place ^ k, 0, 0))
    return held.reshape(-1, block.shape[1])


def gather_expert(held):
    n_expert = lax.axis_size("expert")
    mine = lax.axis_index("expert")
    rows, width = held.shape
    bit = n_expert // 2
    steps = 0
    while bit:
        got = swap(held, "expert", bit)
        low = (mine & bit) == 0
        held = jnp.stack([jnp.where(low, held, got), jnp.where(low, got, held)])
        bit //= 2
        steps += 1
    order = tuple(range(steps - 1, -1, -1)) + (steps, steps + 1)
    return held.transpose(order).reshape(n_expert * rows, width)


def sum_expert(away, kept):
    n_expert = lax.axis_size("expert")
    mine = lax.axis_index("expert")
    width = kept.shape[-1]
    steps = n_expert.bit_length() - 1
    held = kept + swap(away, "expert", 1).astype(f32)
    held = held.reshape((2,) * (steps - 1) + (-1, width))
    for step in range(1, steps):
        bit = 1 << step
        axis = steps - 1 - step
        high = (mine & bit) >> step
        away = lax.dynamic_index_in_dim(held, high ^ 1, axis, keepdims=False).astype(bf16)
        kept = lax.dynamic_index_in_dim(held, high, axis, keepdims=False)
        held = kept + swap(away, "expert", bit).astype(f32)
    return held


def along_shard(blocks):
    return lax.all_to_all(blocks, "shard", split_axis=0, concat_axis=0, tiled=True)


def to_experts(array, copies):
    if copies > 1:
        array = jnp.repeat(array, copies, axis=0)
    return along_shard(array)


def from_experts(array, copies):
    back = along_shard(array)
    if copies > 1:
        back = back.astype(f32).reshape((-1, copies) + back.shape[1:]).sum(axis=1)
    return back


def exchange(rows, copies):
    n_expert = lax.axis_size("expert")
    n_shard = lax.axis_size("shard")
    groups = None
    if copies > 1:
        groups = [
            [e * n_shard + s for e in range(n_expert) for s in range(p, n_shard, copies)]
            for p in range(copies)
        ]
    return lax.all_to_all(
        rows, BOTH, split_axis=0, concat_axis=0, tiled=True, axis_index_groups=groups
    )


def slots_of(routes, experts):
    groups = routes.shape[0]
    named = (routes[:, :, None] == jnp.arange(experts, dtype=jnp.int32)[None, None, :]).astype(f32)
    earlier = jnp.tril(jnp.ones((groups, groups), f32), -1).astype(bf16)
    before = product(earlier, jnp.sum(named, axis=1).astype(bf16))
    rank = jnp.sum(named * before[:, None, :], axis=2).astype(jnp.int32)
    return (routes * CAP + rank).reshape(-1)


def body(
    tokens,
    ln1_gain,
    ln2_gain,
    w_query,
    w_key,
    w_value,
    w_attn_out,
    w_ctrl,
    w_in,
    b_in,
    w_exp_out,
    routes,
    grad_out,
):
    experts = w_ctrl.shape[1]
    n_shard = lax.axis_size("shard")
    copies = n_shard * lax.axis_size("expert") // experts
    slots = slots_of(routes, experts)

    own = pack_small(
        (w_query, w_key, w_value, w_attn_out), w_ctrl, ln1_gain, ln2_gain, b_in
    )
    outer, inner = halves(n_shard)
    here = lax.axis_index("shard")
    held = spread(own, inner, 1, here & (inner - 1))
    held, w_in, w_exp_out = lax.optimization_barrier((held, w_in, w_exp_out))
    expert_w = to_experts(pack_weights(w_in, w_exp_out), copies)
    held = spread(held, outer, inner, here >> (inner.bit_length() - 1))
    small = gather_expert(held)
    local, hidden = b_in.shape
    biases = held.reshape(n_shard, -1, held.shape[1])[:, :, 4 * D + LANES :]
    bias = jnp.concatenate(
        [
            lax.dynamic_index_in_dim(biases, c * local + here // copies, 1, keepdims=False)
            for c in range(hidden // LANES)
        ],
        axis=1,
    ).astype(f32)

    qkv, normed_t = project(tokens, small)
    attended, lse, query_t, key_t, attended_t = attention_forward(qkv)
    residual, probs, outgoing = mix(
        attended, tokens, grad_out, small, routes, slots, experts * CAP
    )
    outgoing, expert_w = lax.optimization_barrier((outgoing, expert_w))
    arrived = exchange(outgoing, copies)
    results = expert_rows(arrived, expert_w, bias)
    returned = exchange(results, copies)
    expert_sums, bias_sums = expert_grads(arrived, expert_w, bias, own.shape[0])
    returned, expert_sums = lax.optimization_barrier((returned, expert_sums))
    expert_sums = from_experts(expert_sums, copies)
    output, residual_grad, grad_t, sums = combine(
        residual, grad_out, probs, attended, small, routes, slots, returned
    )
    grads = attention_backward(qkv, query_t, key_t, grad_t, attended_t, lse)
    core = (lax.axis_index("expert") & 1).reshape(1)
    away, kept = weight_grads(normed_t, grads, sums, core, lax.axis_size("expert"))
    late = sum_expert(away, kept)
    input_grad = input_grads(grads, small, tokens, residual_grad)
    late, input_grad, expert_sums = lax.optimization_barrier((late, input_grad, expert_sums))
    late = late.reshape(n_shard, own.shape[0], -1)
    late = late + jnp.pad(bias_sums.astype(f32), ((0, 0), (0, 0), (4 * D, 0)))
    pieces = along_shard(late.astype(bf16))
    w_in_grad, w_exp_out_grad = unpack_grads(expert_sums)
    wq_grad, wk_grad, wv_grad, wo_grad, wc_grad, ln1_grad, ln2_grad, b_in_grad = finish(
        pieces, own, experts, b_in.shape
    )
    return (
        output,
        input_grad,
        ln1_grad.reshape(-1),
        ln2_grad.reshape(-1),
        wq_grad,
        wk_grad,
        wv_grad,
        wo_grad,
        wc_grad,
        w_in_grad,
        b_in_grad,
        w_exp_out_grad,
    )


def solution(mesh):
    rows = P(BOTH, None)
    vector = P(BOTH)
    experts = (P("expert", None, "shard"), P("expert", "shard"), P("expert", "shard", None))
    in_specs = (rows, vector, vector) + (rows,) * 5 + experts + (rows, rows)
    out_specs = (rows, rows, vector, vector) + (rows,) * 5 + experts
    return jax.shard_map(body, mesh=mesh, in_specs=in_specs, out_specs=out_specs, check_vma=False)
```

```python
import jax
import jax.numpy as jnp
from jax import lax
from jax.experimental import pallas as pl
from jax.experimental.pallas import tpu as pltpu
from jax.sharding import PartitionSpec as P

D = 512
HEAD_DIM = 64
GROUP = 32
ROUTES = 8
BLOCK = 256
CAP = 24
EPSILON = 1e-05
SCALE = 0.125 * 1.4426950408889634
BOTH = ("expert", "shard")

bf16 = jnp.bfloat16
f32 = jnp.float32


def vmem(mebibytes):
    return pltpu.CompilerParams(vmem_limit_bytes=mebibytes * 2**20)


def product(left_op, right_op):
    return jnp.dot(left_op, right_op, preferred_element_type=f32)


def transposed_product(left_op, right_op):
    return lax.dot_general(left_op, right_op, (((0,), (0,)), ((), ())), preferred_element_type=f32)


def against_rows(left_op, right_op):
    return lax.dot_general(left_op, right_op, (((1,), (1,)), ((), ())), preferred_element_type=f32)


def attention_forward_kernel(q_ref, k_ref, v_ref, o_ref, lse_ref, qt_ref, kt_ref, ot_ref):
    length = q_ref.shape[0]
    q_t = q_ref[...].T
    qt_ref[...] = q_t
    kt_ref[...] = k_ref[...].T
    v_t = v_ref[...].T
    zero = jnp.zeros((HEAD_DIM, length), bf16)
    ones = jnp.ones((16, length), bf16)
    halves_q = [q_t[:HEAD_DIM], q_t[HEAD_DIM:]]
    sides = [
        jnp.concatenate([halves_q[0], zero], 0),
        jnp.concatenate([zero, halves_q[1]], 0),
    ]
    values = [
        jnp.concatenate([v_t[:HEAD_DIM], ones], 0),
        jnp.concatenate([v_t[HEAD_DIM:], ones], 0),
    ]

    def scores_of(b, h):
        n = (b + 1) * BLOCK
        return product(k_ref[:n, :], sides[h][:, b * BLOCK : n])

    items = [(b, h) for b in range(length // BLOCK) for h in range(2)]
    outs = []
    later = scores_of(*items[0])
    for i, (b, h) in enumerate(items):
        n = (b + 1) * BLOCK
        cols = slice(b * BLOCK, n)
        scores = later
        if i + 1 < len(items):
            later = scores_of(*items[i + 1])
        top = jnp.max(scores, axis=0, keepdims=True) * SCALE
        weights = jnp.exp2(scores * SCALE - top).astype(bf16)
        out = product(values[h][:, :n], weights)
        total = out[HEAD_DIM : HEAD_DIM + 1]
        outs.append(out[:HEAD_DIM] / total)
        lse_ref[0, h : h + 1, cols] = top + jnp.log2(total)
        if h == 1:
            both = jnp.concatenate(outs, 0).astype(bf16)
            ot_ref[:, cols] = both
            o_ref[cols, :] = both.T
            outs = []


def attention_backward_kernel(
    q_ref, v_ref, qt_ref, kt_ref, gt_ref, ot_ref, lse_ref, out_ref, dq_t, stats
):
    length = q_ref.shape[0]
    q_t = qt_ref[...]
    k_t = kt_ref[...]
    g_t = gt_ref[...]
    q = q_ref[...]
    g = g_t.T
    v_t = v_ref[...].T
    both = g_t.astype(f32) * ot_ref[...].astype(f32)
    rows_of = [slice(0, HEAD_DIM), slice(HEAD_DIM, 2 * HEAD_DIM)]
    lines = [lse_ref[0]] + [jnp.sum(both[rows], axis=0, keepdims=True) for rows in rows_of]
    columns = jnp.concatenate(lines + [jnp.zeros((4, length), f32)], 0).T
    for i in range(4):
        stats[i] = jnp.broadcast_to(columns[:, i : i + 1], (length, 2 * HEAD_DIM))
    zero = jnp.zeros((HEAD_DIM, length), bf16)
    k_sides = [
        jnp.concatenate([k_t[:HEAD_DIM], zero], 0),
        jnp.concatenate([zero, k_t[HEAD_DIM:]], 0),
    ]
    v_sides = [
        jnp.concatenate([v_t[:HEAD_DIM], zero], 0),
        jnp.concatenate([zero, v_t[HEAD_DIM:]], 0),
    ]

    def stat(i, lo):
        half = stats[i, lo:, :]
        return jnp.concatenate([half, half], 1)

    def products_of(j, h):
        here = slice(j * BLOCK, (j + 1) * BLOCK)
        return (
            product(q[j * BLOCK :], k_sides[h][:, here]),
            product(g[j * BLOCK :], v_sides[h][:, here]),
        )

    items = [(j, h) for j in range(length // BLOCK) for h in range(2)]
    key_grads = []
    value_grads = []
    later = products_of(*items[0])
    for i, (j, h) in enumerate(items):
        lo = j * BLOCK
        here = slice(lo, lo + BLOCK)
        rows = rows_of[h]
        scores, share_grad = later
        if i + 1 < len(items):
            later = products_of(*items[i + 1])
        shares = jnp.exp2(scores * SCALE - stat(h, lo))
        score_grad = (shares * (share_grad - stat(2 + h, lo))).astype(bf16)
        value_grads.append(product(g_t[rows, lo:], shares.astype(bf16)))
        key_grads.append(product(q_t[rows, lo:], score_grad))
        query_part = against_rows(k_t[rows, here], score_grad)
        if j == 0:
            dq_t[rows, :] = query_part
        else:
            dq_t[rows, lo:] = dq_t[rows, lo:] + query_part
        if h == 1:
            out_ref[1, here, :] = (jnp.concatenate(key_grads, 0) * 0.125).astype(bf16).T
            out_ref[2, here, :] = jnp.concatenate(value_grads, 0).astype(bf16).T
            key_grads = []
            value_grads = []
    out_ref[0] = (dq_t[...] * 0.125).astype(bf16).T


def pair_columns(length, offset):
    return pl.BlockSpec((length, 2 * HEAD_DIM), lambda pair: (0, pair + offset))


def pair_rows(length):
    return pl.BlockSpec((2 * HEAD_DIM, length), lambda pair: (pair, 0))


def attention_forward(qkv):
    length = qkv.shape[0]
    pairs = D // (2 * HEAD_DIM)
    stats = pl.BlockSpec((1, 2, length), lambda pair: (pair, 0, 0))
    return pl.pallas_call(
        attention_forward_kernel,
        grid=(pairs,),
        in_specs=[pair_columns(length, i * pairs) for i in range(3)],
        out_specs=[pair_columns(length, 0), stats] + [pair_rows(length)] * 3,
        out_shape=[
            jax.ShapeDtypeStruct((length, D), bf16),
            jax.ShapeDtypeStruct((pairs, 2, length), f32),
        ]
        + [jax.ShapeDtypeStruct((D, length), bf16)] * 3,
        compiler_params=vmem(56),
        cost_estimate=pl.CostEstimate(
            flops=10_000_000_000, bytes_accessed=8 * 2**20, transcendentals=0
        ),
        name="attention_forward",
    )(qkv, qkv, qkv)


def attention_backward(qkv, query_t, key_t, grad_t, attended_t, lse):
    length = qkv.shape[0]
    pairs = D // (2 * HEAD_DIM)
    stats = pl.BlockSpec((1, 2, length), lambda pair: (pair, 0, 0))
    return pl.pallas_call(
        attention_backward_kernel,
        grid=(pairs,),
        in_specs=[pair_columns(length, 0), pair_columns(length, 2 * pairs)]
        + [pair_rows(length)] * 4
        + [stats],
        out_specs=pl.BlockSpec((3, length, 2 * HEAD_DIM), lambda pair: (0, 0, pair)),
        out_shape=jax.ShapeDtypeStruct((3, length, D), bf16),
        scratch_shapes=[
            pltpu.VMEM((2 * HEAD_DIM, length), f32),
            pltpu.VMEM((4, length, 2 * HEAD_DIM), f32),
        ],
        compiler_params=vmem(56),
        cost_estimate=pl.CostEstimate(
            flops=50_000_000_000, bytes_accessed=16 * 2**20, transcendentals=20_000_000
        ),
        name="attention_backward",
    )(qkv, qkv, query_t, key_t, grad_t, attended_t, lse)


CHUNK = 256
COMBINE = 512
LANES = 128
BIAS_LANE = 64
SHARDS_A_STEP = 4
GAIN_ONE = LANES - 2
GAIN_TWO = LANES - 1


def call(kernel, grid, in_specs, out_specs, out_shape, scratch, flops, moved, name, limit=56):
    return pl.pallas_call(
        kernel,
        grid=(grid,),
        in_specs=in_specs,
        out_specs=out_specs,
        out_shape=out_shape,
        scratch_shapes=scratch,
        compiler_params=vmem(limit),
        cost_estimate=pl.CostEstimate(flops=flops, bytes_accessed=moved, transcendentals=0),
        name=name,
    )


def fixed(*shape):
    return pl.BlockSpec(shape, lambda i: (0,) * len(shape))


def small_columns(width, start):
    return pl.BlockSpec((D, width), lambda i: (0, start // width))


def leading(*shape):
    return pl.BlockSpec(shape, lambda i: (i,) + (0,) * (len(shape) - 1))


def normalise(matrix):
    average = jnp.mean(matrix, axis=1, keepdims=True)
    centered = matrix - average
    inverse = lax.rsqrt(jnp.mean(centered * centered, axis=1, keepdims=True) + EPSILON)
    return centered * inverse, inverse


def norm_input_grad(upstream, scaled, inverse, gain):
    adjusted = upstream * gain
    first_mean = jnp.mean(adjusted, axis=1, keepdims=True)
    second_mean = jnp.mean(adjusted * scaled, axis=1, keepdims=True)
    return inverse * (adjusted - first_mean - scaled * second_mean)


def small_kernel(q_ref, k_ref, v_ref, o_ref, ctrl_ref, one_ref, two_ref, bias_ref, out_ref):
    rows, experts = ctrl_ref.shape
    for i, ref in enumerate((q_ref, k_ref, v_ref, o_ref)):
        out_ref[:, i * D : (i + 1) * D] = ref[...].astype(bf16)
    square = (rows, rows)
    own = lax.broadcasted_iota(jnp.int32, square, 0) == lax.broadcasted_iota(jnp.int32, square, 1)
    one = jnp.sum(jnp.where(own, one_ref[...], 0.0), axis=1, keepdims=True)
    two = jnp.sum(jnp.where(own, two_ref[...], 0.0), axis=1, keepdims=True)
    lane = lax.broadcasted_iota(jnp.int32, (rows, LANES), 1)
    gains = jnp.where(lane == GAIN_ONE, one, jnp.where(lane == GAIN_TWO, two, 0.0))
    out_ref[:, 4 * D : 4 * D + LANES] = gains.astype(bf16)
    out_ref[:, 4 * D : 4 * D + experts] = ctrl_ref[...].astype(bf16)
    parts = [bias_ref[:, c : c + LANES] for c in range(0, bias_ref.shape[1], LANES)]
    out_ref[:, 4 * D + LANES :] = jnp.concatenate(parts, 0).astype(bf16)


def pack_small(weights, ctrl, gain_one, gain_two, bias):
    rows, experts = ctrl.shape
    width = 4 * D + 2 * LANES
    return call(
        small_kernel,
        1,
        [fixed(rows, D)] * 4
        + [fixed(rows, experts), fixed(1, rows), fixed(1, rows), fixed(*bias.shape)],
        fixed(rows, width),
        jax.ShapeDtypeStruct((rows, width), bf16),
        [],
        100_000,
        200_000,
        "pack_small",
    )(*weights, ctrl, gain_one.reshape(1, rows), gain_two.reshape(1, rows), bias)


def gain_of(ctrl_block, lane):
    pick = (lax.broadcasted_iota(jnp.int32, (16, LANES), 1) == lane).astype(bf16)
    return against_rows(pick, ctrl_block)[:1]


def pack_kernel(first_ref, second_ref, out_ref):
    held, _, hidden = first_ref.shape
    for i in range(held):
        out_ref[i, :D, :] = first_ref[i].astype(bf16)
        for c in range(D // hidden):
            start = D + c * hidden
            out_ref[i, start : start + hidden, :] = second_ref[
                i, :, c * hidden : (c + 1) * hidden
            ].astype(bf16)


def pack_weights(w_in, w_exp_out):
    local, _, hidden = w_in.shape
    return call(
        pack_kernel,
        local // 2,
        [leading(2, D, hidden), leading(2, hidden, D)],
        leading(2, 2 * D, hidden),
        jax.ShapeDtypeStruct((local, 2 * D, hidden), bf16),
        [],
        1_000_000,
        12 * 2**20,
        "pack_weights",
    )(w_in, w_exp_out)


def unpack_kernel(in_ref, first_ref, second_ref):
    hidden = first_ref.shape[2]
    first_ref[0] = in_ref[0, :D, :].astype(f32)
    for c in range(D // hidden):
        start = D + c * hidden
        second_ref[0, :, c * hidden : (c + 1) * hidden] = in_ref[
            0, start : start + hidden, :
        ].astype(f32)


def unpack_grads(packed):
    local, total, hidden = packed.shape
    return call(
        unpack_kernel,
        local,
        [leading(1, total, hidden)],
        [leading(1, D, hidden), leading(1, hidden, D)],
        [
            jax.ShapeDtypeStruct((local, D, hidden), f32),
            jax.ShapeDtypeStruct((local, hidden, D), f32),
        ],
        [],
        1_000_000,
        12 * 2**20,
        "unpack_grads",
    )(packed)


def expert_products(rows_ref, w_ref, bias_ref, i, shard):
    hidden = w_ref.shape[2]
    pre_act = product(rows_ref[:, :D], w_ref[i, :D, :]) + bias_ref[pl.ds(shard, 1), :]
    hidden_grad = jnp.zeros_like(pre_act)
    for c in range(D // hidden):
        start = D + c * hidden
        cols = slice(D + c * hidden, D + (c + 1) * hidden)
        hidden_grad = hidden_grad + against_rows(
            rows_ref[:, cols], w_ref[i, start : start + hidden, :]
        )
    return pre_act, hidden_grad


def activate(pre_act, hidden_grad):
    sigma = 0.5 + 0.5 * jnp.tanh(0.5 * pre_act)
    slope = sigma * (1.0 + pre_act * (1.0 - sigma))
    pre_grad = (hidden_grad.astype(bf16).astype(f32) * slope).astype(bf16)
    return (pre_act * sigma).astype(bf16), pre_grad


def expert_kernel(rows_ref, w_ref, bias_ref, out_ref, results, mixed_grad):
    step = pl.program_id(0)
    held, _, hidden = w_ref.shape
    chunks = D // hidden
    parts = [None] * (chunks + 1)
    later = expert_products(rows_ref, w_ref, bias_ref, 0, step * held)
    for i in range(held):
        now = later
        if i + 1 < held:
            later = expert_products(rows_ref, w_ref, bias_ref, i + 1, step * held + i + 1)
        active, pre_grad = activate(*now)
        more = []
        for c in range(chunks):
            start = D + c * hidden
            more.append(product(active, w_ref[i, start : start + hidden, :]))
        more.append(against_rows(pre_grad, w_ref[i, :D, :]))
        parts = more if i == 0 else [old + new for old, new in zip(parts, more)]

    @pl.when(step == 0)
    def _():
        for c in range(chunks):
            results[:, c * hidden : (c + 1) * hidden] = parts[c]
        mixed_grad[...] = parts[chunks]

    @pl.when(step > 0)
    def _():
        for c in range(chunks):
            cols = slice(c * hidden, (c + 1) * hidden)
            results[:, cols] = results[:, cols] + parts[c]
        mixed_grad[...] = mixed_grad[...] + parts[chunks]

    @pl.when(step == pl.num_programs(0) - 1)
    def _():
        out_ref[:, :D] = results[...].astype(bf16)
        out_ref[:, D:] = mixed_grad[...].astype(bf16)


def expert_rows(rows, weights, bias):
    count = rows.shape[0]
    shards, total, hidden = weights.shape
    return call(
        expert_kernel,
        shards // SHARDS_A_STEP,
        [fixed(count, 2 * D), leading(SHARDS_A_STEP, total, hidden), fixed(shards, hidden)],
        fixed(count, 2 * D),
        jax.ShapeDtypeStruct((count, 2 * D), bf16),
        [pltpu.VMEM((count, D), f32), pltpu.VMEM((count, D), f32)],
        8 * count * D * shards * hidden,
        8 * 2**20,
        "expert_rows",
        40,
    )(rows, weights, bias)


def bias_places(rows, hidden):
    each = hidden // rows
    shape = (rows, hidden)
    owner = lax.broadcasted_iota(jnp.int32, shape, 1) // each == lax.broadcasted_iota(
        jnp.int32, shape, 0
    )
    shape = (LANES, hidden)
    lane = lax.broadcasted_iota(jnp.int32, shape, 1) % each + BIAS_LANE
    return owner, (lane == lax.broadcasted_iota(jnp.int32, shape, 0)).astype(bf16)


def expert_grad_kernel(rows_ref, w_ref, bias_ref, out_ref, sums_ref, rows_t):
    hidden = out_ref.shape[2]

    @pl.when(pl.program_id(0) == 0)
    def _():
        rows_t[...] = rows_ref[:, :D].T

    shard = pl.program_id(0)
    active, pre_grad = activate(*expert_products(rows_ref, w_ref, bias_ref, 0, shard))
    out_ref[0, :D, :] = product(rows_t[...], pre_grad).astype(bf16)
    bias_grad = jnp.sum(pre_grad.astype(f32), axis=0, keepdims=True)
    rows = sums_ref.shape[1]
    owner, lanes = bias_places(rows, hidden)
    parts = jnp.where(owner, bias_grad, 0.0).astype(bf16)
    sums_ref[0] = against_rows(parts, lanes).astype(bf16)
    active_t = active.T
    for c in range(D // hidden):
        start = D + c * hidden
        out_ref[0, start : start + hidden, :] = product(
            active_t, rows_ref[:, D + c * hidden : D + (c + 1) * hidden]
        ).astype(bf16)


def expert_grads(rows, weights, bias, block):
    count = rows.shape[0]
    shards, total, hidden = weights.shape
    return call(
        expert_grad_kernel,
        shards,
        [fixed(count, 2 * D), leading(1, total, hidden), fixed(shards, hidden)],
        [leading(1, total, hidden), leading(1, block, LANES)],
        [
            jax.ShapeDtypeStruct((shards, total, hidden), bf16),
            jax.ShapeDtypeStruct((shards, block, LANES), bf16),
        ],
        [pltpu.VMEM((D, count), bf16)],
        8 * count * D * shards * hidden,
        14 * 2**20,
        "expert_grads",
        63,
    )(rows, weights, bias)


def project_kernel(tokens_ref, w_ref, ctrl_ref, qkv_ref, normed_t_ref):
    scaled, _ = normalise(tokens_ref[...].astype(f32))
    normed = (scaled * gain_of(ctrl_ref[...], GAIN_ONE)).astype(bf16)
    normed_t_ref[...] = normed.T
    qkv_ref[...] = product(normed, w_ref[...]).astype(bf16)


def project(tokens, small):
    length = tokens.shape[0]
    return call(
        project_kernel,
        length // CHUNK,
        [leading(CHUNK, D), small_columns(3 * D, 0), small_columns(LANES, 4 * D)],
        [leading(CHUNK, 3 * D), pl.BlockSpec((D, CHUNK), lambda i: (0, i))],
        [jax.ShapeDtypeStruct((length, 3 * D), bf16), jax.ShapeDtypeStruct((D, length), bf16)],
        [],
        6 * length * D * D,
        12 * 2**20,
        "project",
    )(tokens, small, small)


def choose(probs, routes):
    columns = routes.shape[1]
    shape = (LANES, columns)
    onehot = (lax.broadcasted_iota(jnp.int32, shape, 0) == routes).astype(bf16)
    tokens = probs.shape[0]
    own = lax.broadcasted_iota(jnp.int32, (tokens, columns), 0) // GROUP == (
        lax.broadcasted_iota(jnp.int32, (tokens, columns), 1) // ROUTES
    )
    chosen = jnp.where(own, product(probs.astype(bf16), onehot), 0.0).astype(bf16)
    return chosen, onehot, own


def mix_kernel(
    attended_ref, tokens_ref, grad_ref, wo_ref, ctrl_ref, routes_ref, slots_ref,
    residual_ref, probs_ref, out_ref, rows,
):
    step = pl.program_id(0)
    residual = tokens_ref[...].astype(f32) + product(attended_ref[...], wo_ref[...])
    residual_ref[...] = residual
    scaled, _ = normalise(residual)
    normed = (scaled * gain_of(ctrl_ref[...], GAIN_TWO)).astype(bf16)
    logits = product(normed, ctrl_ref[...]).reshape(CHUNK // GROUP, GROUP, LANES)
    weights = jnp.exp(logits - jnp.max(logits, axis=1, keepdims=True))
    probs = (weights / jnp.sum(weights, axis=1, keepdims=True)).reshape(CHUNK, LANES)
    probs_ref[...] = probs
    chosen, _, _ = choose(probs, routes_ref[0])
    columns = chosen.shape[1]
    here = pl.ds(pl.multiple_of(step * columns, columns), columns)
    rows[here, :D] = transposed_product(chosen, normed).astype(bf16)
    rows[here, D:] = transposed_product(chosen, grad_ref[...]).astype(bf16)

    @pl.when(step == pl.num_programs(0) - 1)
    def _():
        shape = (out_ref.shape[0], rows.shape[0])
        dispatch = (lax.broadcasted_iota(jnp.int32, shape, 0) == slots_ref[...]).astype(bf16)
        out_ref[...] = product(dispatch, rows[...]).astype(bf16)


def mix(attended, tokens, grad_out, small, routes, slots, slot_count):
    length = tokens.shape[0]
    steps = length // CHUNK
    count = slots.shape[0]
    return call(
        mix_kernel,
        steps,
        [leading(CHUNK, D)] * 3
        + [small_columns(D, 3 * D), small_columns(LANES, 4 * D)]
        + [leading(1, 1, count // steps), fixed(1, count)],
        [leading(CHUNK, D), leading(CHUNK, LANES), fixed(slot_count, 2 * D)],
        [
            jax.ShapeDtypeStruct((length, D), f32),
            jax.ShapeDtypeStruct((length, LANES), f32),
            jax.ShapeDtypeStruct((slot_count, 2 * D), bf16),
        ],
        [pltpu.VMEM((count, 2 * D), bf16)],
        4 * length * D * D,
        14 * 2**20,
        "mix",
    )(
        attended, tokens, grad_out, small, small,
        routes.reshape(steps, 1, count // steps), slots.reshape(1, count),
    )


def combine_kernel(
    residual_ref, grad_ref, probs_ref, attended_ref, wo_ref, ctrl_ref, routes_ref,
    slots_ref, back_ref, output_ref, residual_grad_ref, attended_grad_ref, sums_ref, gain_sum,
):
    step = pl.program_id(0)
    gain = gain_of(ctrl_ref[...], GAIN_TWO)
    residual = residual_ref[...]
    scaled, inverse = normalise(residual)
    normed = (scaled * gain).astype(bf16)
    probs = probs_ref[...]
    grad = grad_ref[...]
    chosen, onehot, own = choose(probs, routes_ref[0])
    shape = (chosen.shape[1], back_ref.shape[0])
    collect = (lax.broadcasted_iota(jnp.int32, shape, 1) == slots_ref[...]).astype(bf16)
    rows = product(collect, back_ref[...]).astype(bf16)
    results = rows[:, :D]
    mixed_grad = rows[:, D:]
    output_ref[...] = (residual + product(chosen, results)).astype(bf16)
    chosen_grad = jnp.where(own, against_rows(grad, results) + against_rows(normed, mixed_grad), 0.0)
    high = chosen_grad.astype(bf16)
    low = (chosen_grad - high.astype(f32)).astype(bf16)
    prob_grad = against_rows(high, onehot) + against_rows(low, onehot)
    weighted = (probs * prob_grad).reshape(COMBINE // GROUP, GROUP, LANES)
    total = jnp.broadcast_to(jnp.sum(weighted, axis=1, keepdims=True), weighted.shape)
    logit_grad = (probs * (prob_grad - total.reshape(COMBINE, LANES))).astype(bf16)
    normed_grad = product(chosen, mixed_grad) + against_rows(logit_grad, ctrl_ref[...])
    gain_part = jnp.sum(normed_grad * scaled, axis=0, keepdims=True)
    residual_grad = grad.astype(f32) + norm_input_grad(normed_grad, scaled, inverse, gain)
    residual_grad_ref[...] = residual_grad
    branch = residual_grad.astype(bf16)
    attended_grad_ref[...] = against_rows(wo_ref[...], branch).astype(bf16)
    wo_part = transposed_product(attended_ref[...], branch)
    ctrl_part = transposed_product(normed, logit_grad)

    @pl.when(step == 0)
    def _():
        sums_ref[:, :D] = wo_part
        sums_ref[:, D:] = ctrl_part
        gain_sum[...] = gain_part

    @pl.when(step > 0)
    def _():
        sums_ref[:, :D] = sums_ref[:, :D] + wo_part
        sums_ref[:, D:] = sums_ref[:, D:] + ctrl_part
        gain_sum[...] = gain_sum[...] + gain_part

    @pl.when(step == pl.num_programs(0) - 1)
    def _():
        column = jnp.broadcast_to(gain_sum[...], (LANES, D)).T
        lane = lax.broadcasted_iota(jnp.int32, (D, LANES), 1)
        sums_ref[:, D:] = jnp.where(lane == LANES - 1, column, sums_ref[:, D:])


def combine(residual, grad_out, probs, attended, small, routes, slots, back):
    length = residual.shape[0]
    steps = length // COMBINE
    count = slots.shape[0]
    return call(
        combine_kernel,
        steps,
        [leading(COMBINE, D), leading(COMBINE, D), leading(COMBINE, LANES), leading(COMBINE, D)]
        + [small_columns(D, 3 * D), small_columns(LANES, 4 * D), leading(1, 1, count // steps)]
        + [leading(count // steps, 1), fixed(*back.shape)],
        [leading(COMBINE, D)] * 2
        + [pl.BlockSpec((D, COMBINE), lambda i: (0, i)), fixed(D, D + LANES)],
        [
            jax.ShapeDtypeStruct((length, D), bf16),
            jax.ShapeDtypeStruct((length, D), f32),
            jax.ShapeDtypeStruct((D, length), bf16),
            jax.ShapeDtypeStruct((D, D + LANES), f32),
        ],
        [pltpu.VMEM((1, D), f32)],
        6 * length * D * D,
        24 * 2**20,
        "combine",
        63,
    )(
        residual, grad_out, probs, attended, small, small,
        routes.reshape(steps, 1, count // steps), slots.reshape(count, 1), back,
    )


def weight_grad_kernel(core_ref, normed_t_ref, grad_ref, sums_ref, away_ref, kept_ref):
    step = pl.program_id(0)
    count, rows, _ = kept_ref.shape
    for x in range(count):
        mine = pl.ds(pl.multiple_of((2 * x + core_ref[0]) * rows, rows), rows)
        other = pl.ds(pl.multiple_of((2 * x + 1 - core_ref[0]) * rows, rows), rows)
        kept = product(normed_t_ref[mine, :], grad_ref[0])
        away = product(normed_t_ref[other, :], grad_ref[0]).astype(bf16)
        for i in range(3):

            @pl.when(step == i)
            def _(x=x, i=i, kept=kept, away=away):
                kept_ref[x, :, i * D : (i + 1) * D] = kept
                away_ref[x, :, i * D : (i + 1) * D] = away

        @pl.when(step == 0)
        def _(x=x, mine=mine, other=other):
            kept_ref[x, :, 3 * D :] = sums_ref[mine, :]
            away_ref[x, :, 3 * D :] = sums_ref[other, :].astype(bf16)


def weight_grads(normed_t, grads, sums, core, n_expert):
    length = normed_t.shape[1]
    width = sums.shape[1]
    shape = (n_expert // 2, D // n_expert, 3 * D + width)
    return call(
        weight_grad_kernel,
        3,
        [pl.BlockSpec(memory_space=pltpu.SMEM), fixed(D, length), leading(1, length, D)]
        + [fixed(D, width)],
        [fixed(*shape), fixed(*shape)],
        [jax.ShapeDtypeStruct(shape, bf16), jax.ShapeDtypeStruct(shape, f32)],
        [],
        6 * length * D * D,
        12 * 2**20,
        "weight_grads",
        24,
    )(core, normed_t, grads, sums)


def input_grad_kernel(grads_ref, w_ref, ctrl_ref, tokens_ref, residual_grad_ref, out_ref):
    upstream = against_rows(grads_ref[0], w_ref[:, :D])
    upstream = upstream + against_rows(grads_ref[1], w_ref[:, D : 2 * D])
    upstream = upstream + against_rows(grads_ref[2], w_ref[:, 2 * D :])
    scaled, inverse = normalise(tokens_ref[...].astype(f32))
    gain = gain_of(ctrl_ref[...], GAIN_ONE)
    out_ref[...] = (
        residual_grad_ref[...] + norm_input_grad(upstream, scaled, inverse, gain)
    ).astype(bf16)


def input_grads(grads, small, tokens, residual_grad):
    length = tokens.shape[0]
    return call(
        input_grad_kernel,
        length // CHUNK,
        [pl.BlockSpec((3, CHUNK, D), lambda i: (0, i, 0))]
        + [small_columns(3 * D, 0), small_columns(LANES, 4 * D)]
        + [leading(CHUNK, D), leading(CHUNK, D)],
        leading(CHUNK, D),
        jax.ShapeDtypeStruct((length, D), bf16),
        [],
        6 * length * D * D,
        18 * 2**20,
        "input_grads",
    )(grads, small, small, tokens, residual_grad)


def finish_kernel(
    pieces_ref, own_ref, q_ref, k_ref, v_ref, o_ref, ctrl_ref, one_ref, two_ref, bias_ref
):
    rows, experts = ctrl_ref.shape
    total = jnp.sum(pieces_ref[...].astype(f32), axis=0)
    own = own_ref[...].astype(f32)
    for i, ref in enumerate((q_ref, k_ref, v_ref, o_ref)):
        ref[...] = total[:, i * D : (i + 1) * D]
    ctrl_ref[...] = total[:, 4 * D : 4 * D + experts]
    lane = lax.broadcasted_iota(jnp.int32, (rows, LANES), 1)

    def column(block, which):
        return jnp.sum(jnp.where(lane == which, block[:, 4 * D : 4 * D + LANES], 0.0), axis=1, keepdims=True)

    one = jnp.sum(total[:, : 3 * D] * own[:, : 3 * D], axis=1, keepdims=True) / column(own, GAIN_ONE)
    square = (rows, rows)
    same = lax.broadcasted_iota(jnp.int32, square, 0) == lax.broadcasted_iota(jnp.int32, square, 1)
    one_ref[...] = jnp.sum(jnp.where(same, one, 0.0), axis=0, keepdims=True)
    two_ref[...] = jnp.sum(jnp.where(same, column(total, GAIN_TWO), 0.0), axis=0, keepdims=True)
    local, hidden = bias_ref.shape
    owner, lanes = bias_places(rows, hidden)
    copies = pieces_ref.shape[0] // local
    for e in range(local):
        for i in range(copies):
            part = product(pieces_ref[e * copies + i, :, 4 * D :], lanes)
            line = jnp.sum(jnp.where(owner, part, 0.0), axis=0, keepdims=True)
            bias_ref[e : e + 1, :] = line if i == 0 else bias_ref[e : e + 1, :] + line


def finish(pieces, own, experts, bias_shape):
    count, rows, width = pieces.shape
    outs = [(rows, D)] * 4 + [(rows, experts), (1, rows), (1, rows), bias_shape]
    return call(
        finish_kernel,
        1,
        [fixed(count, rows, width), fixed(*own.shape)],
        [fixed(*shape) for shape in outs],
        [jax.ShapeDtypeStruct(shape, f32) for shape in outs],
        [],
        1_000_000,
        1_000_000,
        "finish",
        8,
    )(pieces, own)


def swap(block, axis, bits):
    size = lax.axis_size(axis)
    return lax.ppermute(block, axis, [(i, i ^ bits) for i in range(size)])


def halves(size):
    inner = 1
    while inner * inner * 4 <= size:
        inner *= 2
    return size // inner, inner


def spread(block, size, stride, place):
    held = jnp.zeros((size,) + block.shape, block.dtype)
    held = lax.dynamic_update_slice(held, block[None], (place, 0, 0))
    for k in range(1, size):
        got = swap(block, "shard", k * stride)
        held = lax.dynamic_update_slice(held, got[None], (place ^ k, 0, 0))
    return held.reshape(-1, block.shape[1])


def gather_expert(held):
    n_expert = lax.axis_size("expert")
    mine = lax.axis_index("expert")
    rows, width = held.shape
    bit = n_expert // 2
    steps = 0
    while bit:
        got = swap(held, "expert", bit)
        low = (mine & bit) == 0
        held = jnp.stack([jnp.where(low, held, got), jnp.where(low, got, held)])
        bit //= 2
        steps += 1
    order = tuple(range(steps - 1, -1, -1)) + (steps, steps + 1)
    return held.transpose(order).reshape(n_expert * rows, width)


def sum_expert(away, kept):
    n_expert = lax.axis_size("expert")
    mine = lax.axis_index("expert")
    width = kept.shape[-1]
    steps = n_expert.bit_length() - 1
    shape = (2,) * (steps - 1) + (-1, width)
    terms = [kept.reshape(shape), swap(away, "expert", 1).reshape(shape)]
    for step in range(1, steps):
        bit = 1 << step
        axis = steps - 1 - step
        high = (mine & bit) >> step

        def half(which, axis=axis):
            return [lax.dynamic_index_in_dim(t, which, axis, keepdims=False) for t in terms]

        away = sum(t.astype(f32) for t in half(high ^ 1)).astype(bf16)
        terms = half(high) + [swap(away, "expert", bit)]
    return sum(t.astype(f32) for t in terms)


def along_shard(blocks):
    return lax.all_to_all(blocks, "shard", split_axis=0, concat_axis=0, tiled=True)


def to_experts(array, copies):
    if copies > 1:
        array = jnp.repeat(array, copies, axis=0)
    return along_shard(array)


def from_experts(array, copies):
    back = along_shard(array)
    if copies > 1:
        back = back.astype(f32).reshape((-1, copies) + back.shape[1:]).sum(axis=1)
    return back


def exchange(rows, copies):
    n_expert = lax.axis_size("expert")
    n_shard = lax.axis_size("shard")
    groups = None
    if copies > 1:
        groups = [
            [e * n_shard + s for e in range(n_expert) for s in range(p, n_shard, copies)]
            for p in range(copies)
        ]
    return lax.all_to_all(
        rows, BOTH, split_axis=0, concat_axis=0, tiled=True, axis_index_groups=groups
    )


def slots_of(routes, experts):
    groups = routes.shape[0]
    named = (routes[:, :, None] == jnp.arange(experts, dtype=jnp.int32)[None, None, :]).astype(f32)
    earlier = jnp.tril(jnp.ones((groups, groups), f32), -1).astype(bf16)
    before = product(earlier, jnp.sum(named, axis=1).astype(bf16))
    rank = jnp.sum(named * before[:, None, :], axis=2).astype(jnp.int32)
    return (routes * CAP + rank).reshape(-1)


def body(
    tokens,
    ln1_gain,
    ln2_gain,
    w_query,
    w_key,
    w_value,
    w_attn_out,
    w_ctrl,
    w_in,
    b_in,
    w_exp_out,
    routes,
    grad_out,
):
    experts = w_ctrl.shape[1]
    n_shard = lax.axis_size("shard")
    copies = n_shard * lax.axis_size("expert") // experts
    slots = slots_of(routes, experts)

    own = pack_small(
        (w_query, w_key, w_value, w_attn_out), w_ctrl, ln1_gain, ln2_gain, b_in
    )
    outer, inner = halves(n_shard)
    here = lax.axis_index("shard")
    held = spread(own, inner, 1, here & (inner - 1))
    held, w_in, w_exp_out = lax.optimization_barrier((held, w_in, w_exp_out))
    expert_w = to_experts(pack_weights(w_in, w_exp_out), copies)
    held = spread(held, outer, inner, here >> (inner.bit_length() - 1))
    small = gather_expert(held)
    local, hidden = b_in.shape
    biases = held.reshape(n_shard, -1, held.shape[1])[:, :, 4 * D + LANES :]
    bias = jnp.concatenate(
        [
            lax.dynamic_index_in_dim(biases, c * local + here // copies, 1, keepdims=False)
            for c in range(hidden // LANES)
        ],
        axis=1,
    ).astype(f32)

    qkv, normed_t = project(tokens, small)
    attended, lse, query_t, key_t, attended_t = attention_forward(qkv)
    residual, probs, outgoing = mix(
        attended, tokens, grad_out, small, routes, slots, experts * CAP
    )
    outgoing, expert_w = lax.optimization_barrier((outgoing, expert_w))
    arrived = exchange(outgoing, copies)
    results = expert_rows(arrived, expert_w, bias)
    returned = exchange(results, copies)
    expert_sums, bias_sums = expert_grads(arrived, expert_w, bias, own.shape[0])
    returned, expert_sums = lax.optimization_barrier((returned, expert_sums))
    expert_sums = from_experts(expert_sums, copies)
    output, residual_grad, grad_t, sums = combine(
        residual, grad_out, probs, attended, small, routes, slots, returned
    )
    grads = attention_backward(qkv, query_t, key_t, grad_t, attended_t, lse)
    core = (lax.axis_index("expert") & 1).reshape(1)
    away, kept = weight_grads(normed_t, grads, sums, core, lax.axis_size("expert"))
    late = sum_expert(away, kept).reshape(n_shard, own.shape[0], -1)
    late = late + jnp.pad(bias_sums.astype(f32), ((0, 0), (0, 0), (4 * D, 0)))
    late = late.astype(bf16)
    input_grad = input_grads(grads, small, tokens, residual_grad)
    late, input_grad, expert_sums = lax.optimization_barrier((late, input_grad, expert_sums))
    pieces = along_shard(late)
    w_in_grad, w_exp_out_grad = unpack_grads(expert_sums)
    wq_grad, wk_grad, wv_grad, wo_grad, wc_grad, ln1_grad, ln2_grad, b_in_grad = finish(
        pieces, own, experts, b_in.shape
    )
    return (
        output,
        input_grad,
        ln1_grad.reshape(-1),
        ln2_grad.reshape(-1),
        wq_grad,
        wk_grad,
        wv_grad,
        wo_grad,
        wc_grad,
        w_in_grad,
        b_in_grad,
        w_exp_out_grad,
    )


def solution(mesh):
    rows = P(BOTH, None)
    vector = P(BOTH)
    experts = (P("expert", None, "shard"), P("expert", "shard"), P("expert", "shard", None))
    in_specs = (rows, vector, vector) + (rows,) * 5 + experts + (rows, rows)
    out_specs = (rows, rows, vector, vector) + (rows,) * 5 + experts
    return jax.shard_map(body, mesh=mesh, in_specs=in_specs, out_specs=out_specs, check_vma=False)
```

```python
import jax
import jax.numpy as jnp
from jax import lax
from jax.experimental import pallas as pl
from jax.experimental.pallas import tpu as pltpu
from jax.sharding import PartitionSpec as P

D = 512
HEAD_DIM = 64
GROUP = 32
ROUTES = 8
BLOCK = 256
CAP = 24
EPSILON = 1e-05
SCALE = 0.125 * 1.4426950408889634
BOTH = ("expert", "shard")

bf16 = jnp.bfloat16
f32 = jnp.float32


def vmem(mebibytes):
    return pltpu.CompilerParams(vmem_limit_bytes=mebibytes * 2**20)


def product(left_op, right_op):
    return jnp.dot(left_op, right_op, preferred_element_type=f32)


def transposed_product(left_op, right_op):
    return lax.dot_general(left_op, right_op, (((0,), (0,)), ((), ())), preferred_element_type=f32)


def against_rows(left_op, right_op):
    return lax.dot_general(left_op, right_op, (((1,), (1,)), ((), ())), preferred_element_type=f32)


def attention_forward_kernel(q_ref, k_ref, v_ref, o_ref, lse_ref, qt_ref, kt_ref, ot_ref):
    length = q_ref.shape[0]
    q_t = q_ref[...].T
    qt_ref[...] = q_t
    kt_ref[...] = k_ref[...].T
    v_t = v_ref[...].T
    zero = jnp.zeros((HEAD_DIM, length), bf16)
    ones = jnp.ones((16, length), bf16)
    halves_q = [q_t[:HEAD_DIM], q_t[HEAD_DIM:]]
    sides = [
        jnp.concatenate([halves_q[0], zero], 0),
        jnp.concatenate([zero, halves_q[1]], 0),
    ]
    values = [
        jnp.concatenate([v_t[:HEAD_DIM], ones], 0),
        jnp.concatenate([v_t[HEAD_DIM:], ones], 0),
    ]

    def scores_of(b, h):
        n = (b + 1) * BLOCK
        return product(k_ref[:n, :], sides[h][:, b * BLOCK : n])

    items = [(b, h) for b in range(length // BLOCK) for h in range(2)]
    outs = []
    later = scores_of(*items[0])
    for i, (b, h) in enumerate(items):
        n = (b + 1) * BLOCK
        cols = slice(b * BLOCK, n)
        scores = later
        if i + 1 < len(items):
            later = scores_of(*items[i + 1])
        top = jnp.max(scores, axis=0, keepdims=True) * SCALE
        weights = jnp.exp2(scores * SCALE - top).astype(bf16)
        out = product(values[h][:, :n], weights)
        total = out[HEAD_DIM : HEAD_DIM + 1]
        outs.append(out[:HEAD_DIM] / total)
        lse_ref[0, h : h + 1, cols] = top + jnp.log2(total)
        if h == 1:
            both = jnp.concatenate(outs, 0).astype(bf16)
            ot_ref[:, cols] = both
            o_ref[cols, :] = both.T
            outs = []


def attention_backward_kernel(
    q_ref, v_ref, qt_ref, kt_ref, gt_ref, ot_ref, lse_ref, out_ref, dq_t, stats
):
    length = q_ref.shape[0]
    q_t = qt_ref[...]
    k_t = kt_ref[...]
    g_t = gt_ref[...]
    q = q_ref[...]
    g = g_t.T
    v_t = v_ref[...].T
    both = g_t.astype(f32) * ot_ref[...].astype(f32)
    rows_of = [slice(0, HEAD_DIM), slice(HEAD_DIM, 2 * HEAD_DIM)]
    lines = [lse_ref[0]] + [jnp.sum(both[rows], axis=0, keepdims=True) for rows in rows_of]
    columns = jnp.concatenate(lines + [jnp.zeros((4, length), f32)], 0).T
    for i in range(4):
        stats[i] = jnp.broadcast_to(columns[:, i : i + 1], (length, 2 * HEAD_DIM))
    zero = jnp.zeros((HEAD_DIM, length), bf16)
    k_sides = [
        jnp.concatenate([k_t[:HEAD_DIM], zero], 0),
        jnp.concatenate([zero, k_t[HEAD_DIM:]], 0),
    ]
    v_sides = [
        jnp.concatenate([v_t[:HEAD_DIM], zero], 0),
        jnp.concatenate([zero, v_t[HEAD_DIM:]], 0),
    ]

    def stat(i, lo):
        half = stats[i, lo:, :]
        return jnp.concatenate([half, half], 1)

    def products_of(j, h):
        here = slice(j * BLOCK, (j + 1) * BLOCK)
        return (
            product(q[j * BLOCK :], k_sides[h][:, here]),
            product(g[j * BLOCK :], v_sides[h][:, here]),
        )

    items = [(j, h) for j in range(length // BLOCK) for h in range(2)]
    key_grads = []
    value_grads = []
    later = products_of(*items[0])
    for i, (j, h) in enumerate(items):
        lo = j * BLOCK
        here = slice(lo, lo + BLOCK)
        rows = rows_of[h]
        scores, share_grad = later
        if i + 1 < len(items):
            later = products_of(*items[i + 1])
        shares = jnp.exp2(scores * SCALE - stat(h, lo))
        score_grad = (shares * (share_grad - stat(2 + h, lo))).astype(bf16)
        value_grads.append(product(g_t[rows, lo:], shares.astype(bf16)))
        key_grads.append(product(q_t[rows, lo:], score_grad))
        query_part = against_rows(k_t[rows, here], score_grad)
        if j == 0:
            dq_t[rows, :] = query_part
        else:
            dq_t[rows, lo:] = dq_t[rows, lo:] + query_part
        if h == 1:
            out_ref[1, here, :] = (jnp.concatenate(key_grads, 0) * 0.125).astype(bf16).T
            out_ref[2, here, :] = jnp.concatenate(value_grads, 0).astype(bf16).T
            key_grads = []
            value_grads = []
    out_ref[0] = (dq_t[...] * 0.125).astype(bf16).T


def pair_columns(length, offset):
    return pl.BlockSpec((length, 2 * HEAD_DIM), lambda pair: (0, pair + offset))


def pair_rows(length):
    return pl.BlockSpec((2 * HEAD_DIM, length), lambda pair: (pair, 0))


def attention_forward(qkv):
    length = qkv.shape[0]
    pairs = D // (2 * HEAD_DIM)
    stats = pl.BlockSpec((1, 2, length), lambda pair: (pair, 0, 0))
    return pl.pallas_call(
        attention_forward_kernel,
        grid=(pairs,),
        in_specs=[pair_columns(length, i * pairs) for i in range(3)],
        out_specs=[pair_columns(length, 0), stats] + [pair_rows(length)] * 3,
        out_shape=[
            jax.ShapeDtypeStruct((length, D), bf16),
            jax.ShapeDtypeStruct((pairs, 2, length), f32),
        ]
        + [jax.ShapeDtypeStruct((D, length), bf16)] * 3,
        compiler_params=vmem(56),
        cost_estimate=pl.CostEstimate(
            flops=10_000_000_000, bytes_accessed=8 * 2**20, transcendentals=0
        ),
        name="attention_forward",
    )(qkv, qkv, qkv)


def attention_backward(qkv, query_t, key_t, grad_t, attended_t, lse):
    length = qkv.shape[0]
    pairs = D // (2 * HEAD_DIM)
    stats = pl.BlockSpec((1, 2, length), lambda pair: (pair, 0, 0))
    return pl.pallas_call(
        attention_backward_kernel,
        grid=(pairs,),
        in_specs=[pair_columns(length, 0), pair_columns(length, 2 * pairs)]
        + [pair_rows(length)] * 4
        + [stats],
        out_specs=pl.BlockSpec((3, length, 2 * HEAD_DIM), lambda pair: (0, 0, pair)),
        out_shape=jax.ShapeDtypeStruct((3, length, D), bf16),
        scratch_shapes=[
            pltpu.VMEM((2 * HEAD_DIM, length), f32),
            pltpu.VMEM((4, length, 2 * HEAD_DIM), f32),
        ],
        compiler_params=vmem(56),
        cost_estimate=pl.CostEstimate(
            flops=50_000_000_000, bytes_accessed=16 * 2**20, transcendentals=20_000_000
        ),
        name="attention_backward",
    )(qkv, qkv, query_t, key_t, grad_t, attended_t, lse)


CHUNK = 256
COMBINE = 512
LANES = 128
BIAS_LANE = 64
SHARDS_A_STEP = 8
GAIN_ONE = LANES - 2
GAIN_TWO = LANES - 1


def call(kernel, grid, in_specs, out_specs, out_shape, scratch, flops, moved, name, limit=56):
    return pl.pallas_call(
        kernel,
        grid=(grid,),
        in_specs=in_specs,
        out_specs=out_specs,
        out_shape=out_shape,
        scratch_shapes=scratch,
        compiler_params=vmem(limit),
        cost_estimate=pl.CostEstimate(flops=flops, bytes_accessed=moved, transcendentals=0),
        name=name,
    )


def fixed(*shape):
    return pl.BlockSpec(shape, lambda i: (0,) * len(shape))


def small_columns(width, start):
    return pl.BlockSpec((D, width), lambda i: (0, start // width))


def leading(*shape):
    return pl.BlockSpec(shape, lambda i: (i,) + (0,) * (len(shape) - 1))


def normalise(matrix):
    average = jnp.mean(matrix, axis=1, keepdims=True)
    centered = matrix - average
    inverse = lax.rsqrt(jnp.mean(centered * centered, axis=1, keepdims=True) + EPSILON)
    return centered * inverse, inverse


def norm_input_grad(upstream, scaled, inverse, gain):
    adjusted = upstream * gain
    first_mean = jnp.mean(adjusted, axis=1, keepdims=True)
    second_mean = jnp.mean(adjusted * scaled, axis=1, keepdims=True)
    return inverse * (adjusted - first_mean - scaled * second_mean)


def small_kernel(q_ref, k_ref, v_ref, o_ref, ctrl_ref, one_ref, two_ref, bias_ref, out_ref):
    rows, experts = ctrl_ref.shape
    for i, ref in enumerate((q_ref, k_ref, v_ref, o_ref)):
        out_ref[:, i * D : (i + 1) * D] = ref[...].astype(bf16)
    square = (rows, rows)
    own = lax.broadcasted_iota(jnp.int32, square, 0) == lax.broadcasted_iota(jnp.int32, square, 1)
    one = jnp.sum(jnp.where(own, one_ref[...], 0.0), axis=1, keepdims=True)
    two = jnp.sum(jnp.where(own, two_ref[...], 0.0), axis=1, keepdims=True)
    lane = lax.broadcasted_iota(jnp.int32, (rows, LANES), 1)
    gains = jnp.where(lane == GAIN_ONE, one, jnp.where(lane == GAIN_TWO, two, 0.0))
    out_ref[:, 4 * D : 4 * D + LANES] = gains.astype(bf16)
    out_ref[:, 4 * D : 4 * D + experts] = ctrl_ref[...].astype(bf16)
    parts = [bias_ref[:, c : c + LANES] for c in range(0, bias_ref.shape[1], LANES)]
    out_ref[:, 4 * D + LANES :] = jnp.concatenate(parts, 0).astype(bf16)


def pack_small(weights, ctrl, gain_one, gain_two, bias):
    rows, experts = ctrl.shape
    width = 4 * D + 2 * LANES
    return call(
        small_kernel,
        1,
        [fixed(rows, D)] * 4
        + [fixed(rows, experts), fixed(1, rows), fixed(1, rows), fixed(*bias.shape)],
        fixed(rows, width),
        jax.ShapeDtypeStruct((rows, width), bf16),
        [],
        100_000,
        200_000,
        "pack_small",
    )(*weights, ctrl, gain_one.reshape(1, rows), gain_two.reshape(1, rows), bias)


def gain_of(ctrl_block, lane):
    pick = (lax.broadcasted_iota(jnp.int32, (16, LANES), 1) == lane).astype(bf16)
    return against_rows(pick, ctrl_block)[:1]


def pack_kernel(first_ref, second_ref, out_ref):
    held, _, hidden = first_ref.shape
    for i in range(held):
        out_ref[i, :D, :] = first_ref[i].astype(bf16)
        for c in range(D // hidden):
            start = D + c * hidden
            out_ref[i, start : start + hidden, :] = second_ref[
                i, :, c * hidden : (c + 1) * hidden
            ].astype(bf16)


def pack_weights(w_in, w_exp_out):
    local, _, hidden = w_in.shape
    return call(
        pack_kernel,
        local // 2,
        [leading(2, D, hidden), leading(2, hidden, D)],
        leading(2, 2 * D, hidden),
        jax.ShapeDtypeStruct((local, 2 * D, hidden), bf16),
        [],
        1_000_000,
        12 * 2**20,
        "pack_weights",
    )(w_in, w_exp_out)


def unpack_kernel(in_ref, first_ref, second_ref):
    hidden = first_ref.shape[2]
    first_ref[0] = in_ref[0, :D, :].astype(f32)
    for c in range(D // hidden):
        start = D + c * hidden
        second_ref[0, :, c * hidden : (c + 1) * hidden] = in_ref[
            0, start : start + hidden, :
        ].astype(f32)


def unpack_grads(packed):
    local, total, hidden = packed.shape
    return call(
        unpack_kernel,
        local,
        [leading(1, total, hidden)],
        [leading(1, D, hidden), leading(1, hidden, D)],
        [
            jax.ShapeDtypeStruct((local, D, hidden), f32),
            jax.ShapeDtypeStruct((local, hidden, D), f32),
        ],
        [],
        1_000_000,
        12 * 2**20,
        "unpack_grads",
    )(packed)


def expert_products(rows_ref, w_ref, bias_ref, i, shard):
    hidden = w_ref.shape[2]
    pre_act = product(rows_ref[:, :D], w_ref[i, :D, :]) + bias_ref[pl.ds(shard, 1), :]
    hidden_grad = jnp.zeros_like(pre_act)
    for c in range(D // hidden):
        start = D + c * hidden
        cols = slice(D + c * hidden, D + (c + 1) * hidden)
        hidden_grad = hidden_grad + against_rows(
            rows_ref[:, cols], w_ref[i, start : start + hidden, :]
        )
    return pre_act, hidden_grad


def activate(pre_act, hidden_grad):
    sigma = 0.5 + 0.5 * jnp.tanh(0.5 * pre_act)
    slope = sigma * (1.0 + pre_act * (1.0 - sigma))
    pre_grad = (hidden_grad.astype(bf16).astype(f32) * slope).astype(bf16)
    return (pre_act * sigma).astype(bf16), pre_grad


def expert_kernel(rows_ref, w_ref, bias_ref, out_ref, results, mixed_grad):
    step = pl.program_id(0)
    held, _, hidden = w_ref.shape
    chunks = D // hidden
    parts = [None] * (chunks + 1)
    later = expert_products(rows_ref, w_ref, bias_ref, 0, step * held)
    for i in range(held):
        now = later
        if i + 1 < held:
            later = expert_products(rows_ref, w_ref, bias_ref, i + 1, step * held + i + 1)
        active, pre_grad = activate(*now)
        more = []
        for c in range(chunks):
            start = D + c * hidden
            more.append(product(active, w_ref[i, start : start + hidden, :]))
        more.append(against_rows(pre_grad, w_ref[i, :D, :]))
        parts = more if i == 0 else [old + new for old, new in zip(parts, more)]

    @pl.when(step == 0)
    def _():
        for c in range(chunks):
            results[:, c * hidden : (c + 1) * hidden] = parts[c]
        mixed_grad[...] = parts[chunks]

    @pl.when(step > 0)
    def _():
        for c in range(chunks):
            cols = slice(c * hidden, (c + 1) * hidden)
            results[:, cols] = results[:, cols] + parts[c]
        mixed_grad[...] = mixed_grad[...] + parts[chunks]

    @pl.when(step == pl.num_programs(0) - 1)
    def _():
        out_ref[:, :D] = results[...].astype(bf16)
        out_ref[:, D:] = mixed_grad[...].astype(bf16)


def expert_rows(rows, weights, bias):
    count = rows.shape[0]
    shards, total, hidden = weights.shape
    return call(
        expert_kernel,
        shards // SHARDS_A_STEP,
        [fixed(count, 2 * D), leading(SHARDS_A_STEP, total, hidden), fixed(shards, hidden)],
        fixed(count, 2 * D),
        jax.ShapeDtypeStruct((count, 2 * D), bf16),
        [pltpu.VMEM((count, D), f32), pltpu.VMEM((count, D), f32)],
        8 * count * D * shards * hidden,
        8 * 2**20,
        "expert_rows",
        40,
    )(rows, weights, bias)


def bias_places(rows, hidden):
    each = hidden // rows
    shape = (rows, hidden)
    owner = lax.broadcasted_iota(jnp.int32, shape, 1) // each == lax.broadcasted_iota(
        jnp.int32, shape, 0
    )
    shape = (LANES, hidden)
    lane = lax.broadcasted_iota(jnp.int32, shape, 1) % each + BIAS_LANE
    return owner, (lane == lax.broadcasted_iota(jnp.int32, shape, 0)).astype(bf16)


def expert_grad_kernel(rows_ref, w_ref, bias_ref, out_ref, sums_ref, rows_t):
    hidden = out_ref.shape[2]

    @pl.when(pl.program_id(0) == 0)
    def _():
        rows_t[...] = rows_ref[:, :D].T

    shard = pl.program_id(0)
    active, pre_grad = activate(*expert_products(rows_ref, w_ref, bias_ref, 0, shard))
    out_ref[0, :D, :] = product(rows_t[...], pre_grad).astype(bf16)
    bias_grad = jnp.sum(pre_grad.astype(f32), axis=0, keepdims=True)
    rows = sums_ref.shape[1]
    owner, lanes = bias_places(rows, hidden)
    parts = jnp.where(owner, bias_grad, 0.0).astype(bf16)
    sums_ref[0] = against_rows(parts, lanes).astype(bf16)
    active_t = active.T
    for c in range(D // hidden):
        start = D + c * hidden
        out_ref[0, start : start + hidden, :] = product(
            active_t, rows_ref[:, D + c * hidden : D + (c + 1) * hidden]
        ).astype(bf16)


def expert_grads(rows, weights, bias, block):
    count = rows.shape[0]
    shards, total, hidden = weights.shape
    return call(
        expert_grad_kernel,
        shards,
        [fixed(count, 2 * D), leading(1, total, hidden), fixed(shards, hidden)],
        [leading(1, total, hidden), leading(1, block, LANES)],
        [
            jax.ShapeDtypeStruct((shards, total, hidden), bf16),
            jax.ShapeDtypeStruct((shards, block, LANES), bf16),
        ],
        [pltpu.VMEM((D, count), bf16)],
        8 * count * D * shards * hidden,
        14 * 2**20,
        "expert_grads",
        63,
    )(rows, weights, bias)


def project_kernel(tokens_ref, w_ref, ctrl_ref, qkv_ref, normed_t_ref):
    scaled, _ = normalise(tokens_ref[...].astype(f32))
    normed = (scaled * gain_of(ctrl_ref[...], GAIN_ONE)).astype(bf16)
    normed_t_ref[...] = normed.T
    qkv_ref[...] = product(normed, w_ref[...]).astype(bf16)


def project(tokens, small):
    length = tokens.shape[0]
    return call(
        project_kernel,
        length // CHUNK,
        [leading(CHUNK, D), small_columns(3 * D, 0), small_columns(LANES, 4 * D)],
        [leading(CHUNK, 3 * D), pl.BlockSpec((D, CHUNK), lambda i: (0, i))],
        [jax.ShapeDtypeStruct((length, 3 * D), bf16), jax.ShapeDtypeStruct((D, length), bf16)],
        [],
        6 * length * D * D,
        12 * 2**20,
        "project",
    )(tokens, small, small)


def choose(probs, routes):
    columns = routes.shape[1]
    shape = (LANES, columns)
    onehot = (lax.broadcasted_iota(jnp.int32, shape, 0) == routes).astype(bf16)
    tokens = probs.shape[0]
    own = lax.broadcasted_iota(jnp.int32, (tokens, columns), 0) // GROUP == (
        lax.broadcasted_iota(jnp.int32, (tokens, columns), 1) // ROUTES
    )
    chosen = jnp.where(own, product(probs.astype(bf16), onehot), 0.0).astype(bf16)
    return chosen, onehot, own


def mix_kernel(
    attended_ref, tokens_ref, grad_ref, wo_ref, ctrl_ref, routes_ref, slots_ref,
    residual_ref, probs_ref, out_ref, rows,
):
    step = pl.program_id(0)
    residual = tokens_ref[...].astype(f32) + product(attended_ref[...], wo_ref[...])
    residual_ref[...] = residual
    scaled, _ = normalise(residual)
    normed = (scaled * gain_of(ctrl_ref[...], GAIN_TWO)).astype(bf16)
    logits = product(normed, ctrl_ref[...]).reshape(CHUNK // GROUP, GROUP, LANES)
    weights = jnp.exp(logits - jnp.max(logits, axis=1, keepdims=True))
    probs = (weights / jnp.sum(weights, axis=1, keepdims=True)).reshape(CHUNK, LANES)
    probs_ref[...] = probs
    chosen, _, _ = choose(probs, routes_ref[0])
    columns = chosen.shape[1]
    here = pl.ds(pl.multiple_of(step * columns, columns), columns)
    rows[here, :D] = transposed_product(chosen, normed).astype(bf16)
    rows[here, D:] = transposed_product(chosen, grad_ref[...]).astype(bf16)

    @pl.when(step == pl.num_programs(0) - 1)
    def _():
        shape = (out_ref.shape[0], rows.shape[0])
        dispatch = (lax.broadcasted_iota(jnp.int32, shape, 0) == slots_ref[...]).astype(bf16)
        out_ref[...] = product(dispatch, rows[...]).astype(bf16)


def mix(attended, tokens, grad_out, small, routes, slots, slot_count):
    length = tokens.shape[0]
    steps = length // CHUNK
    count = slots.shape[0]
    return call(
        mix_kernel,
        steps,
        [leading(CHUNK, D)] * 3
        + [small_columns(D, 3 * D), small_columns(LANES, 4 * D)]
        + [leading(1, 1, count // steps), fixed(1, count)],
        [leading(CHUNK, D), leading(CHUNK, LANES), fixed(slot_count, 2 * D)],
        [
            jax.ShapeDtypeStruct((length, D), f32),
            jax.ShapeDtypeStruct((length, LANES), f32),
            jax.ShapeDtypeStruct((slot_count, 2 * D), bf16),
        ],
        [pltpu.VMEM((count, 2 * D), bf16)],
        4 * length * D * D,
        14 * 2**20,
        "mix",
    )(
        attended, tokens, grad_out, small, small,
        routes.reshape(steps, 1, count // steps), slots.reshape(1, count),
    )


def combine_kernel(
    residual_ref, grad_ref, probs_ref, attended_ref, wo_ref, ctrl_ref, routes_ref,
    slots_ref, back_ref, output_ref, residual_grad_ref, attended_grad_ref, sums_ref, gain_sum,
):
    step = pl.program_id(0)
    gain = gain_of(ctrl_ref[...], GAIN_TWO)
    residual = residual_ref[...]
    scaled, inverse = normalise(residual)
    normed = (scaled * gain).astype(bf16)
    probs = probs_ref[...]
    grad = grad_ref[...]
    chosen, onehot, own = choose(probs, routes_ref[0])
    shape = (chosen.shape[1], back_ref.shape[0])
    collect = (lax.broadcasted_iota(jnp.int32, shape, 1) == slots_ref[...]).astype(bf16)
    rows = product(collect, back_ref[...]).astype(bf16)
    results = rows[:, :D]
    mixed_grad = rows[:, D:]
    output_ref[...] = (residual + product(chosen, results)).astype(bf16)
    chosen_grad = jnp.where(own, against_rows(grad, results) + against_rows(normed, mixed_grad), 0.0)
    high = chosen_grad.astype(bf16)
    low = (chosen_grad - high.astype(f32)).astype(bf16)
    prob_grad = against_rows(high, onehot) + against_rows(low, onehot)
    weighted = (probs * prob_grad).reshape(COMBINE // GROUP, GROUP, LANES)
    total = jnp.broadcast_to(jnp.sum(weighted, axis=1, keepdims=True), weighted.shape)
    logit_grad = (probs * (prob_grad - total.reshape(COMBINE, LANES))).astype(bf16)
    normed_grad = product(chosen, mixed_grad) + against_rows(logit_grad, ctrl_ref[...])
    gain_part = jnp.sum(normed_grad * scaled, axis=0, keepdims=True)
    residual_grad = grad.astype(f32) + norm_input_grad(normed_grad, scaled, inverse, gain)
    residual_grad_ref[...] = residual_grad
    branch = residual_grad.astype(bf16)
    attended_grad_ref[...] = against_rows(wo_ref[...], branch).astype(bf16)
    wo_part = transposed_product(attended_ref[...], branch)
    ctrl_part = transposed_product(normed, logit_grad)

    @pl.when(step == 0)
    def _():
        sums_ref[:, :D] = wo_part
        sums_ref[:, D:] = ctrl_part
        gain_sum[...] = gain_part

    @pl.when(step > 0)
    def _():
        sums_ref[:, :D] = sums_ref[:, :D] + wo_part
        sums_ref[:, D:] = sums_ref[:, D:] + ctrl_part
        gain_sum[...] = gain_sum[...] + gain_part

    @pl.when(step == pl.num_programs(0) - 1)
    def _():
        column = jnp.broadcast_to(gain_sum[...], (LANES, D)).T
        lane = lax.broadcasted_iota(jnp.int32, (D, LANES), 1)
        sums_ref[:, D:] = jnp.where(lane == LANES - 1, column, sums_ref[:, D:])


def combine(residual, grad_out, probs, attended, small, routes, slots, back):
    length = residual.shape[0]
    steps = length // COMBINE
    count = slots.shape[0]
    return call(
        combine_kernel,
        steps,
        [leading(COMBINE, D), leading(COMBINE, D), leading(COMBINE, LANES), leading(COMBINE, D)]
        + [small_columns(D, 3 * D), small_columns(LANES, 4 * D), leading(1, 1, count // steps)]
        + [leading(count // steps, 1), fixed(*back.shape)],
        [leading(COMBINE, D)] * 2
        + [pl.BlockSpec((D, COMBINE), lambda i: (0, i)), fixed(D, D + LANES)],
        [
            jax.ShapeDtypeStruct((length, D), bf16),
            jax.ShapeDtypeStruct((length, D), f32),
            jax.ShapeDtypeStruct((D, length), bf16),
            jax.ShapeDtypeStruct((D, D + LANES), f32),
        ],
        [pltpu.VMEM((1, D), f32)],
        6 * length * D * D,
        24 * 2**20,
        "combine",
        63,
    )(
        residual, grad_out, probs, attended, small, small,
        routes.reshape(steps, 1, count // steps), slots.reshape(count, 1), back,
    )


def weight_grad_kernel(core_ref, normed_t_ref, grad_ref, sums_ref, away_ref, kept_ref):
    step = pl.program_id(0)
    count, rows, _ = kept_ref.shape
    for x in range(count):
        mine = pl.ds(pl.multiple_of((2 * x + core_ref[0]) * rows, rows), rows)
        other = pl.ds(pl.multiple_of((2 * x + 1 - core_ref[0]) * rows, rows), rows)
        kept = product(normed_t_ref[mine, :], grad_ref[0])
        away = product(normed_t_ref[other, :], grad_ref[0]).astype(bf16)
        for i in range(3):

            @pl.when(step == i)
            def _(x=x, i=i, kept=kept, away=away):
                kept_ref[x, :, i * D : (i + 1) * D] = kept
                away_ref[x, :, i * D : (i + 1) * D] = away

        @pl.when(step == 0)
        def _(x=x, mine=mine, other=other):
            kept_ref[x, :, 3 * D :] = sums_ref[mine, :]
            away_ref[x, :, 3 * D :] = sums_ref[other, :].astype(bf16)


def weight_grads(normed_t, grads, sums, core, n_expert):
    length = normed_t.shape[1]
    width = sums.shape[1]
    shape = (n_expert // 2, D // n_expert, 3 * D + width)
    return call(
        weight_grad_kernel,
        3,
        [pl.BlockSpec(memory_space=pltpu.SMEM), fixed(D, length), leading(1, length, D)]
        + [fixed(D, width)],
        [fixed(*shape), fixed(*shape)],
        [jax.ShapeDtypeStruct(shape, bf16), jax.ShapeDtypeStruct(shape, f32)],
        [],
        6 * length * D * D,
        12 * 2**20,
        "weight_grads",
        24,
    )(core, normed_t, grads, sums)


def input_grad_kernel(grads_ref, w_ref, ctrl_ref, tokens_ref, residual_grad_ref, out_ref):
    upstream = against_rows(grads_ref[0], w_ref[:, :D])
    upstream = upstream + against_rows(grads_ref[1], w_ref[:, D : 2 * D])
    upstream = upstream + against_rows(grads_ref[2], w_ref[:, 2 * D :])
    scaled, inverse = normalise(tokens_ref[...].astype(f32))
    gain = gain_of(ctrl_ref[...], GAIN_ONE)
    out_ref[...] = (
        residual_grad_ref[...] + norm_input_grad(upstream, scaled, inverse, gain)
    ).astype(bf16)


def input_grads(grads, small, tokens, residual_grad):
    length = tokens.shape[0]
    return call(
        input_grad_kernel,
        length // CHUNK,
        [pl.BlockSpec((3, CHUNK, D), lambda i: (0, i, 0))]
        + [small_columns(3 * D, 0), small_columns(LANES, 4 * D)]
        + [leading(CHUNK, D), leading(CHUNK, D)],
        leading(CHUNK, D),
        jax.ShapeDtypeStruct((length, D), bf16),
        [],
        6 * length * D * D,
        18 * 2**20,
        "input_grads",
    )(grads, small, small, tokens, residual_grad)


def finish_kernel(
    pieces_ref, own_ref, q_ref, k_ref, v_ref, o_ref, ctrl_ref, one_ref, two_ref, bias_ref
):
    rows, experts = ctrl_ref.shape
    total = jnp.sum(pieces_ref[...].astype(f32), axis=0)
    own = own_ref[...].astype(f32)
    for i, ref in enumerate((q_ref, k_ref, v_ref, o_ref)):
        ref[...] = total[:, i * D : (i + 1) * D]
    ctrl_ref[...] = total[:, 4 * D : 4 * D + experts]
    lane = lax.broadcasted_iota(jnp.int32, (rows, LANES), 1)

    def column(block, which):
        return jnp.sum(jnp.where(lane == which, block[:, 4 * D : 4 * D + LANES], 0.0), axis=1, keepdims=True)

    one = jnp.sum(total[:, : 3 * D] * own[:, : 3 * D], axis=1, keepdims=True) / column(own, GAIN_ONE)
    square = (rows, rows)
    same = lax.broadcasted_iota(jnp.int32, square, 0) == lax.broadcasted_iota(jnp.int32, square, 1)
    one_ref[...] = jnp.sum(jnp.where(same, one, 0.0), axis=0, keepdims=True)
    two_ref[...] = jnp.sum(jnp.where(same, column(total, GAIN_TWO), 0.0), axis=0, keepdims=True)
    local, hidden = bias_ref.shape
    owner, lanes = bias_places(rows, hidden)
    copies = pieces_ref.shape[0] // local
    for e in range(local):
        for i in range(copies):
            part = product(pieces_ref[e * copies + i, :, 4 * D :], lanes)
            line = jnp.sum(jnp.where(owner, part, 0.0), axis=0, keepdims=True)
            bias_ref[e : e + 1, :] = line if i == 0 else bias_ref[e : e + 1, :] + line


def finish(pieces, own, experts, bias_shape):
    count, rows, width = pieces.shape
    outs = [(rows, D)] * 4 + [(rows, experts), (1, rows), (1, rows), bias_shape]
    return call(
        finish_kernel,
        1,
        [fixed(count, rows, width), fixed(*own.shape)],
        [fixed(*shape) for shape in outs],
        [jax.ShapeDtypeStruct(shape, f32) for shape in outs],
        [],
        1_000_000,
        1_000_000,
        "finish",
        8,
    )(pieces, own)


def swap(block, axis, bits):
    size = lax.axis_size(axis)
    return lax.ppermute(block, axis, [(i, i ^ bits) for i in range(size)])


def halves(size):
    inner = 1
    while inner * inner * 4 <= size:
        inner *= 2
    return size // inner, inner


def spread(block, size, stride, place):
    held = jnp.zeros((size,) + block.shape, block.dtype)
    held = lax.dynamic_update_slice(held, block[None], (place, 0, 0))
    for k in range(1, size):
        got = swap(block, "shard", k * stride)
        held = lax.dynamic_update_slice(held, got[None], (place ^ k, 0, 0))
    return held.reshape(-1, block.shape[1])


def gather_expert(held):
    n_expert = lax.axis_size("expert")
    mine = lax.axis_index("expert")
    rows, width = held.shape
    bit = n_expert // 2
    steps = 0
    while bit:
        got = swap(held, "expert", bit)
        low = (mine & bit) == 0
        held = jnp.stack([jnp.where(low, held, got), jnp.where(low, got, held)])
        bit //= 2
        steps += 1
    order = tuple(range(steps - 1, -1, -1)) + (steps, steps + 1)
    return held.transpose(order).reshape(n_expert * rows, width)


def sum_expert(away, kept):
    n_expert = lax.axis_size("expert")
    mine = lax.axis_index("expert")
    width = kept.shape[-1]
    steps = n_expert.bit_length() - 1
    shape = (2,) * (steps - 1) + (-1, width)
    terms = [kept.reshape(shape), swap(away, "expert", 1).reshape(shape)]
    for step in range(1, steps):
        bit = 1 << step
        axis = steps - 1 - step
        high = (mine & bit) >> step

        def half(which, axis=axis):
            return [lax.dynamic_index_in_dim(t, which, axis, keepdims=False) for t in terms]

        away = sum(t.astype(f32) for t in half(high ^ 1)).astype(bf16)
        terms = half(high) + [swap(away, "expert", bit)]
    return sum(t.astype(f32) for t in terms)


def along_shard(blocks):
    return lax.all_to_all(blocks, "shard", split_axis=0, concat_axis=0, tiled=True)


def to_experts(array, copies):
    if copies > 1:
        array = jnp.repeat(array, copies, axis=0)
    return along_shard(array)


def from_experts(array, copies):
    back = along_shard(array)
    if copies > 1:
        back = back.astype(f32).reshape((-1, copies) + back.shape[1:]).sum(axis=1)
    return back


def exchange(rows, copies):
    n_expert = lax.axis_size("expert")
    n_shard = lax.axis_size("shard")
    groups = None
    if copies > 1:
        groups = [
            [e * n_shard + s for e in range(n_expert) for s in range(p, n_shard, copies)]
            for p in range(copies)
        ]
    return lax.all_to_all(
        rows, BOTH, split_axis=0, concat_axis=0, tiled=True, axis_index_groups=groups
    )


def slots_of(routes, experts):
    groups = routes.shape[0]
    named = (routes[:, :, None] == jnp.arange(experts, dtype=jnp.int32)[None, None, :]).astype(f32)
    earlier = jnp.tril(jnp.ones((groups, groups), f32), -1).astype(bf16)
    before = product(earlier, jnp.sum(named, axis=1).astype(bf16))
    rank = jnp.sum(named * before[:, None, :], axis=2).astype(jnp.int32)
    return (routes * CAP + rank).reshape(-1)


def body(
    tokens,
    ln1_gain,
    ln2_gain,
    w_query,
    w_key,
    w_value,
    w_attn_out,
    w_ctrl,
    w_in,
    b_in,
    w_exp_out,
    routes,
    grad_out,
):
    experts = w_ctrl.shape[1]
    n_shard = lax.axis_size("shard")
    copies = n_shard * lax.axis_size("expert") // experts
    slots = slots_of(routes, experts)

    own = pack_small(
        (w_query, w_key, w_value, w_attn_out), w_ctrl, ln1_gain, ln2_gain, b_in
    )
    outer, inner = halves(n_shard)
    here = lax.axis_index("shard")
    held = spread(own, inner, 1, here & (inner - 1))
    held, w_in, w_exp_out = lax.optimization_barrier((held, w_in, w_exp_out))
    expert_w = to_experts(pack_weights(w_in, w_exp_out), copies)
    held = spread(held, outer, inner, here >> (inner.bit_length() - 1))
    small = gather_expert(held)
    local, hidden = b_in.shape
    biases = held.reshape(n_shard, -1, held.shape[1])[:, :, 4 * D + LANES :]
    bias = jnp.concatenate(
        [
            lax.dynamic_index_in_dim(biases, c * local + here // copies, 1, keepdims=False)
            for c in range(hidden // LANES)
        ],
        axis=1,
    ).astype(f32)

    qkv, normed_t = project(tokens, small)
    attended, lse, query_t, key_t, attended_t = attention_forward(qkv)
    residual, probs, outgoing = mix(
        attended, tokens, grad_out, small, routes, slots, experts * CAP
    )
    outgoing, expert_w = lax.optimization_barrier((outgoing, expert_w))
    arrived = exchange(outgoing, copies)
    results = expert_rows(arrived, expert_w, bias)
    returned = exchange(results, copies)
    expert_sums, bias_sums = expert_grads(arrived, expert_w, bias, own.shape[0])
    returned, expert_sums = lax.optimization_barrier((returned, expert_sums))
    expert_sums = from_experts(expert_sums, copies)
    output, residual_grad, grad_t, sums = combine(
        residual, grad_out, probs, attended, small, routes, slots, returned
    )
    grads = attention_backward(qkv, query_t, key_t, grad_t, attended_t, lse)
    core = (lax.axis_index("expert") & 1).reshape(1)
    away, kept = weight_grads(normed_t, grads, sums, core, lax.axis_size("expert"))
    late = sum_expert(away, kept).reshape(n_shard, own.shape[0], -1)
    late = late + jnp.pad(bias_sums.astype(f32), ((0, 0), (0, 0), (4 * D, 0)))
    late = late.astype(bf16)
    input_grad = input_grads(grads, small, tokens, residual_grad)
    late, input_grad, expert_sums = lax.optimization_barrier((late, input_grad, expert_sums))
    pieces = along_shard(late)
    w_in_grad, w_exp_out_grad = unpack_grads(expert_sums)
    wq_grad, wk_grad, wv_grad, wo_grad, wc_grad, ln1_grad, ln2_grad, b_in_grad = finish(
        pieces, own, experts, b_in.shape
    )
    return (
        output,
        input_grad,
        ln1_grad.reshape(-1),
        ln2_grad.reshape(-1),
        wq_grad,
        wk_grad,
        wv_grad,
        wo_grad,
        wc_grad,
        w_in_grad,
        b_in_grad,
        w_exp_out_grad,
    )


def solution(mesh):
    rows = P(BOTH, None)
    vector = P(BOTH)
    experts = (P("expert", None, "shard"), P("expert", "shard"), P("expert", "shard", None))
    in_specs = (rows, vector, vector) + (rows,) * 5 + experts + (rows, rows)
    out_specs = (rows, rows, vector, vector) + (rows,) * 5 + experts
    return jax.shard_map(body, mesh=mesh, in_specs=in_specs, out_specs=out_specs, check_vma=False)
```

```python
import jax
import jax.numpy as jnp
from jax import lax
from jax.experimental import pallas as pl
from jax.experimental.pallas import tpu as pltpu
from jax.sharding import PartitionSpec as P

D = 512
HEAD_DIM = 64
GROUP = 32
ROUTES = 8
BLOCK = 256
CAP = 24
EPSILON = 1e-05
SCALE = 0.125 * 1.4426950408889634
BOTH = ("expert", "shard")

bf16 = jnp.bfloat16
f32 = jnp.float32


def vmem(mebibytes):
    return pltpu.CompilerParams(vmem_limit_bytes=mebibytes * 2**20)


def product(left_op, right_op):
    return jnp.dot(left_op, right_op, preferred_element_type=f32)


def transposed_product(left_op, right_op):
    return lax.dot_general(left_op, right_op, (((0,), (0,)), ((), ())), preferred_element_type=f32)


def against_rows(left_op, right_op):
    return lax.dot_general(left_op, right_op, (((1,), (1,)), ((), ())), preferred_element_type=f32)


def attention_forward_kernel(q_ref, k_ref, v_ref, o_ref, lse_ref, qt_ref, kt_ref, ot_ref):
    length = q_ref.shape[0]
    q_t = q_ref[...].T
    qt_ref[...] = q_t
    kt_ref[...] = k_ref[...].T
    v_t = v_ref[...].T
    zero = jnp.zeros((HEAD_DIM, length), bf16)
    ones = jnp.ones((16, length), bf16)
    halves_q = [q_t[:HEAD_DIM], q_t[HEAD_DIM:]]
    sides = [
        jnp.concatenate([halves_q[0], zero], 0),
        jnp.concatenate([zero, halves_q[1]], 0),
    ]
    values = [
        jnp.concatenate([v_t[:HEAD_DIM], ones], 0),
        jnp.concatenate([v_t[HEAD_DIM:], ones], 0),
    ]

    def scores_of(b, h):
        n = (b + 1) * BLOCK
        return product(k_ref[:n, :], sides[h][:, b * BLOCK : n])

    items = [(b, h) for b in range(length // BLOCK) for h in range(2)]
    outs = []
    later = scores_of(*items[0])
    for i, (b, h) in enumerate(items):
        n = (b + 1) * BLOCK
        cols = slice(b * BLOCK, n)
        scores = later
        if i + 1 < len(items):
            later = scores_of(*items[i + 1])
        top = jnp.max(scores, axis=0, keepdims=True) * SCALE
        weights = jnp.exp2(scores * SCALE - top).astype(bf16)
        out = product(values[h][:, :n], weights)
        total = out[HEAD_DIM : HEAD_DIM + 1]
        outs.append(out[:HEAD_DIM] / total)
        lse_ref[0, h : h + 1, cols] = top + jnp.log2(total)
        if h == 1:
            both = jnp.concatenate(outs, 0).astype(bf16)
            ot_ref[:, cols] = both
            o_ref[cols, :] = both.T
            outs = []


def attention_backward_kernel(
    q_ref, v_ref, qt_ref, kt_ref, gt_ref, ot_ref, lse_ref, out_ref, dq_t, stats
):
    length = q_ref.shape[0]
    q_t = qt_ref[...]
    k_t = kt_ref[...]
    g_t = gt_ref[...]
    q = q_ref[...]
    g = g_t.T
    v_t = v_ref[...].T
    both = g_t.astype(f32) * ot_ref[...].astype(f32)
    rows_of = [slice(0, HEAD_DIM), slice(HEAD_DIM, 2 * HEAD_DIM)]
    lines = [lse_ref[0]] + [jnp.sum(both[rows], axis=0, keepdims=True) for rows in rows_of]
    columns = jnp.concatenate(lines + [jnp.zeros((4, length), f32)], 0).T
    for i in range(4):
        stats[i] = jnp.broadcast_to(columns[:, i : i + 1], (length, 2 * HEAD_DIM))
    zero = jnp.zeros((HEAD_DIM, length), bf16)
    k_sides = [
        jnp.concatenate([k_t[:HEAD_DIM], zero], 0),
        jnp.concatenate([zero, k_t[HEAD_DIM:]], 0),
    ]
    v_sides = [
        jnp.concatenate([v_t[:HEAD_DIM], zero], 0),
        jnp.concatenate([zero, v_t[HEAD_DIM:]], 0),
    ]

    def stat(i, lo):
        half = stats[i, lo:, :]
        return jnp.concatenate([half, half], 1)

    def products_of(j, h):
        here = slice(j * BLOCK, (j + 1) * BLOCK)
        return (
            product(q[j * BLOCK :], k_sides[h][:, here]),
            product(g[j * BLOCK :], v_sides[h][:, here]),
        )

    items = [(j, h) for j in range(length // BLOCK) for h in range(2)]
    key_grads = []
    value_grads = []
    later = products_of(*items[0])
    for i, (j, h) in enumerate(items):
        lo = j * BLOCK
        here = slice(lo, lo + BLOCK)
        rows = rows_of[h]
        scores, share_grad = later
        if i + 1 < len(items):
            later = products_of(*items[i + 1])
        shares = jnp.exp2(scores * SCALE - stat(h, lo))
        score_grad = (shares * (share_grad - stat(2 + h, lo))).astype(bf16)
        value_grads.append(product(g_t[rows, lo:], shares.astype(bf16)))
        key_grads.append(product(q_t[rows, lo:], score_grad))
        query_part = against_rows(k_t[rows, here], score_grad)
        if j == 0:
            dq_t[rows, :] = query_part
        else:
            dq_t[rows, lo:] = dq_t[rows, lo:] + query_part
        if h == 1:
            out_ref[1, here, :] = (jnp.concatenate(key_grads, 0) * 0.125).astype(bf16).T
            out_ref[2, here, :] = jnp.concatenate(value_grads, 0).astype(bf16).T
            key_grads = []
            value_grads = []
    out_ref[0] = (dq_t[...] * 0.125).astype(bf16).T


def pair_columns(length, offset):
    return pl.BlockSpec((length, 2 * HEAD_DIM), lambda pair: (0, pair + offset))


def pair_rows(length):
    return pl.BlockSpec((2 * HEAD_DIM, length), lambda pair: (pair, 0))


def attention_forward(qkv):
    length = qkv.shape[0]
    pairs = D // (2 * HEAD_DIM)
    stats = pl.BlockSpec((1, 2, length), lambda pair: (pair, 0, 0))
    return pl.pallas_call(
        attention_forward_kernel,
        grid=(pairs,),
        in_specs=[pair_columns(length, i * pairs) for i in range(3)],
        out_specs=[pair_columns(length, 0), stats] + [pair_rows(length)] * 3,
        out_shape=[
            jax.ShapeDtypeStruct((length, D), bf16),
            jax.ShapeDtypeStruct((pairs, 2, length), f32),
        ]
        + [jax.ShapeDtypeStruct((D, length), bf16)] * 3,
        compiler_params=vmem(56),
        cost_estimate=pl.CostEstimate(
            flops=10_000_000_000, bytes_accessed=8 * 2**20, transcendentals=0
        ),
        name="attention_forward",
    )(qkv, qkv, qkv)


def attention_backward(qkv, query_t, key_t, grad_t, attended_t, lse):
    length = qkv.shape[0]
    pairs = D // (2 * HEAD_DIM)
    stats = pl.BlockSpec((1, 2, length), lambda pair: (pair, 0, 0))
    return pl.pallas_call(
        attention_backward_kernel,
        grid=(pairs,),
        in_specs=[pair_columns(length, 0), pair_columns(length, 2 * pairs)]
        + [pair_rows(length)] * 4
        + [stats],
        out_specs=pl.BlockSpec((3, length, 2 * HEAD_DIM), lambda pair: (0, 0, pair)),
        out_shape=jax.ShapeDtypeStruct((3, length, D), bf16),
        scratch_shapes=[
            pltpu.VMEM((2 * HEAD_DIM, length), f32),
            pltpu.VMEM((4, length, 2 * HEAD_DIM), f32),
        ],
        compiler_params=vmem(56),
        cost_estimate=pl.CostEstimate(
            flops=50_000_000_000, bytes_accessed=16 * 2**20, transcendentals=20_000_000
        ),
        name="attention_backward",
    )(qkv, qkv, query_t, key_t, grad_t, attended_t, lse)


CHUNK = 256
COMBINE = 512
LANES = 128
BIAS_LANE = 64
SHARDS_A_STEP = 4
GAIN_ONE = LANES - 2
GAIN_TWO = LANES - 1


def call(kernel, grid, in_specs, out_specs, out_shape, scratch, flops, moved, name, limit=56):
    return pl.pallas_call(
        kernel,
        grid=(grid,),
        in_specs=in_specs,
        out_specs=out_specs,
        out_shape=out_shape,
        scratch_shapes=scratch,
        compiler_params=vmem(limit),
        cost_estimate=pl.CostEstimate(flops=flops, bytes_accessed=moved, transcendentals=0),
        name=name,
    )


def fixed(*shape):
    return pl.BlockSpec(shape, lambda i: (0,) * len(shape))


def small_columns(width, start):
    return pl.BlockSpec((D, width), lambda i: (0, start // width))


def leading(*shape):
    return pl.BlockSpec(shape, lambda i: (i,) + (0,) * (len(shape) - 1))


def normalise(matrix):
    average = jnp.mean(matrix, axis=1, keepdims=True)
    centered = matrix - average
    inverse = lax.rsqrt(jnp.mean(centered * centered, axis=1, keepdims=True) + EPSILON)
    return centered * inverse, inverse


def norm_input_grad(upstream, scaled, inverse, gain):
    adjusted = upstream * gain
    first_mean = jnp.mean(adjusted, axis=1, keepdims=True)
    second_mean = jnp.mean(adjusted * scaled, axis=1, keepdims=True)
    return inverse * (adjusted - first_mean - scaled * second_mean)


def small_kernel(q_ref, k_ref, v_ref, o_ref, ctrl_ref, one_ref, two_ref, bias_ref, out_ref):
    rows, experts = ctrl_ref.shape
    for i, ref in enumerate((q_ref, k_ref, v_ref, o_ref)):
        out_ref[:, i * D : (i + 1) * D] = ref[...].astype(bf16)
    square = (rows, rows)
    own = lax.broadcasted_iota(jnp.int32, square, 0) == lax.broadcasted_iota(jnp.int32, square, 1)
    one = jnp.sum(jnp.where(own, one_ref[...], 0.0), axis=1, keepdims=True)
    two = jnp.sum(jnp.where(own, two_ref[...], 0.0), axis=1, keepdims=True)
    lane = lax.broadcasted_iota(jnp.int32, (rows, LANES), 1)
    gains = jnp.where(lane == GAIN_ONE, one, jnp.where(lane == GAIN_TWO, two, 0.0))
    out_ref[:, 4 * D : 4 * D + LANES] = gains.astype(bf16)
    out_ref[:, 4 * D : 4 * D + experts] = ctrl_ref[...].astype(bf16)
    parts = [bias_ref[:, c : c + LANES] for c in range(0, bias_ref.shape[1], LANES)]
    out_ref[:, 4 * D + LANES :] = jnp.concatenate(parts, 0).astype(bf16)


def pack_small(weights, ctrl, gain_one, gain_two, bias):
    rows, experts = ctrl.shape
    width = 4 * D + 2 * LANES
    return call(
        small_kernel,
        1,
        [fixed(rows, D)] * 4
        + [fixed(rows, experts), fixed(1, rows), fixed(1, rows), fixed(*bias.shape)],
        fixed(rows, width),
        jax.ShapeDtypeStruct((rows, width), bf16),
        [],
        100_000,
        200_000,
        "pack_small",
    )(*weights, ctrl, gain_one.reshape(1, rows), gain_two.reshape(1, rows), bias)


def gain_of(ctrl_block, lane):
    pick = (lax.broadcasted_iota(jnp.int32, (16, LANES), 1) == lane).astype(bf16)
    return against_rows(pick, ctrl_block)[:1]


def pack_kernel(first_ref, second_ref, out_ref):
    held, _, hidden = first_ref.shape
    for i in range(held):
        out_ref[i, :D, :] = first_ref[i].astype(bf16)
        for c in range(D // hidden):
            start = D + c * hidden
            out_ref[i, start : start + hidden, :] = second_ref[
                i, :, c * hidden : (c + 1) * hidden
            ].astype(bf16)


def pack_weights(w_in, w_exp_out):
    local, _, hidden = w_in.shape
    return call(
        pack_kernel,
        local // 2,
        [leading(2, D, hidden), leading(2, hidden, D)],
        leading(2, 2 * D, hidden),
        jax.ShapeDtypeStruct((local, 2 * D, hidden), bf16),
        [],
        1_000_000,
        12 * 2**20,
        "pack_weights",
    )(w_in, w_exp_out)


def unpack_kernel(in_ref, first_ref, second_ref):
    hidden = first_ref.shape[2]
    first_ref[0] = in_ref[0, :D, :].astype(f32)
    for c in range(D // hidden):
        start = D + c * hidden
        second_ref[0, :, c * hidden : (c + 1) * hidden] = in_ref[
            0, start : start + hidden, :
        ].astype(f32)


def unpack_grads(packed):
    local, total, hidden = packed.shape
    return call(
        unpack_kernel,
        local,
        [leading(1, total, hidden)],
        [leading(1, D, hidden), leading(1, hidden, D)],
        [
            jax.ShapeDtypeStruct((local, D, hidden), f32),
            jax.ShapeDtypeStruct((local, hidden, D), f32),
        ],
        [],
        1_000_000,
        12 * 2**20,
        "unpack_grads",
    )(packed)


def expert_products(rows_ref, w_ref, bias_ref, i, shard):
    hidden = w_ref.shape[2]
    pre_act = product(rows_ref[:, :D], w_ref[i, :D, :]) + bias_ref[pl.ds(shard, 1), :]
    hidden_grad = jnp.zeros_like(pre_act)
    for c in range(D // hidden):
        start = D + c * hidden
        cols = slice(D + c * hidden, D + (c + 1) * hidden)
        hidden_grad = hidden_grad + against_rows(
            rows_ref[:, cols], w_ref[i, start : start + hidden, :]
        )
    return pre_act, hidden_grad


def activate(pre_act, hidden_grad):
    sigma = 0.5 + 0.5 * jnp.tanh(0.5 * pre_act)
    slope = sigma * (1.0 + pre_act * (1.0 - sigma))
    pre_grad = (hidden_grad.astype(bf16).astype(f32) * slope).astype(bf16)
    return (pre_act * sigma).astype(bf16), pre_grad


def expert_kernel(rows_ref, w_ref, bias_ref, out_ref, results, mixed_grad):
    step = pl.program_id(0)
    held, _, hidden = w_ref.shape
    chunks = D // hidden
    parts = [None] * (chunks + 1)
    later = expert_products(rows_ref, w_ref, bias_ref, 0, step * held)
    for i in range(held):
        now = later
        if i + 1 < held:
            later = expert_products(rows_ref, w_ref, bias_ref, i + 1, step * held + i + 1)
        active, pre_grad = activate(*now)
        more = []
        for c in range(chunks):
            start = D + c * hidden
            more.append(product(active, w_ref[i, start : start + hidden, :]))
        more.append(against_rows(pre_grad, w_ref[i, :D, :]))
        parts = more if i == 0 else [old + new for old, new in zip(parts, more)]

    @pl.when(step == 0)
    def _():
        for c in range(chunks):
            results[:, c * hidden : (c + 1) * hidden] = parts[c]
        mixed_grad[...] = parts[chunks]

    @pl.when(step > 0)
    def _():
        for c in range(chunks):
            cols = slice(c * hidden, (c + 1) * hidden)
            results[:, cols] = results[:, cols] + parts[c]
        mixed_grad[...] = mixed_grad[...] + parts[chunks]

    @pl.when(step == pl.num_programs(0) - 1)
    def _():
        out_ref[:, :D] = results[...].astype(bf16)
        out_ref[:, D:] = mixed_grad[...].astype(bf16)


def expert_rows(rows, weights, bias):
    count = rows.shape[0]
    shards, total, hidden = weights.shape
    return call(
        expert_kernel,
        shards // SHARDS_A_STEP,
        [fixed(count, 2 * D), leading(SHARDS_A_STEP, total, hidden), fixed(shards, hidden)],
        fixed(count, 2 * D),
        jax.ShapeDtypeStruct((count, 2 * D), bf16),
        [pltpu.VMEM((count, D), f32), pltpu.VMEM((count, D), f32)],
        8 * count * D * shards * hidden,
        8 * 2**20,
        "expert_rows",
        40,
    )(rows, weights, bias)


def bias_places(rows, hidden):
    each = hidden // rows
    shape = (rows, hidden)
    owner = lax.broadcasted_iota(jnp.int32, shape, 1) // each == lax.broadcasted_iota(
        jnp.int32, shape, 0
    )
    shape = (LANES, hidden)
    lane = lax.broadcasted_iota(jnp.int32, shape, 1) % each + BIAS_LANE
    return owner, (lane == lax.broadcasted_iota(jnp.int32, shape, 0)).astype(bf16)


def expert_grad_kernel(rows_ref, w_ref, bias_ref, out_ref, sums_ref, rows_t):
    hidden = out_ref.shape[2]

    @pl.when(pl.program_id(0) == 0)
    def _():
        rows_t[...] = rows_ref[:, :D].T

    shard = pl.program_id(0)
    active, pre_grad = activate(*expert_products(rows_ref, w_ref, bias_ref, 0, shard))
    out_ref[0, :D, :] = product(rows_t[...], pre_grad).astype(bf16)
    bias_grad = jnp.sum(pre_grad.astype(f32), axis=0, keepdims=True)
    rows = sums_ref.shape[1]
    owner, lanes = bias_places(rows, hidden)
    parts = jnp.where(owner, bias_grad, 0.0).astype(bf16)
    sums_ref[0] = against_rows(parts, lanes).astype(bf16)
    active_t = active.T
    for c in range(D // hidden):
        start = D + c * hidden
        out_ref[0, start : start + hidden, :] = product(
            active_t, rows_ref[:, D + c * hidden : D + (c + 1) * hidden]
        ).astype(bf16)


def expert_grads(rows, weights, bias, block):
    count = rows.shape[0]
    shards, total, hidden = weights.shape
    return call(
        expert_grad_kernel,
        shards,
        [fixed(count, 2 * D), leading(1, total, hidden), fixed(shards, hidden)],
        [leading(1, total, hidden), leading(1, block, LANES)],
        [
            jax.ShapeDtypeStruct((shards, total, hidden), bf16),
            jax.ShapeDtypeStruct((shards, block, LANES), bf16),
        ],
        [pltpu.VMEM((D, count), bf16)],
        8 * count * D * shards * hidden,
        14 * 2**20,
        "expert_grads",
        63,
    )(rows, weights, bias)


def project_kernel(tokens_ref, w_ref, ctrl_ref, qkv_ref, normed_t_ref):
    scaled, _ = normalise(tokens_ref[...].astype(f32))
    normed = (scaled * gain_of(ctrl_ref[...], GAIN_ONE)).astype(bf16)
    normed_t_ref[...] = normed.T
    qkv_ref[...] = product(normed, w_ref[...]).astype(bf16)


def project(tokens, small):
    length = tokens.shape[0]
    return call(
        project_kernel,
        length // CHUNK,
        [leading(CHUNK, D), small_columns(3 * D, 0), small_columns(LANES, 4 * D)],
        [leading(CHUNK, 3 * D), pl.BlockSpec((D, CHUNK), lambda i: (0, i))],
        [jax.ShapeDtypeStruct((length, 3 * D), bf16), jax.ShapeDtypeStruct((D, length), bf16)],
        [],
        6 * length * D * D,
        12 * 2**20,
        "project",
    )(tokens, small, small)


def choose(probs, routes):
    columns = routes.shape[1]
    shape = (LANES, columns)
    onehot = (lax.broadcasted_iota(jnp.int32, shape, 0) == routes).astype(bf16)
    tokens = probs.shape[0]
    own = lax.broadcasted_iota(jnp.int32, (tokens, columns), 0) // GROUP == (
        lax.broadcasted_iota(jnp.int32, (tokens, columns), 1) // ROUTES
    )
    chosen = jnp.where(own, product(probs.astype(bf16), onehot), 0.0).astype(bf16)
    return chosen, onehot, own


def mix_kernel(
    attended_ref, tokens_ref, grad_ref, wo_ref, ctrl_ref, routes_ref, slots_ref,
    residual_ref, probs_ref, out_ref, rows,
):
    step = pl.program_id(0)
    residual = tokens_ref[...].astype(f32) + product(attended_ref[...], wo_ref[...])
    residual_ref[...] = residual
    scaled, _ = normalise(residual)
    normed = (scaled * gain_of(ctrl_ref[...], GAIN_TWO)).astype(bf16)
    logits = product(normed, ctrl_ref[...]).reshape(CHUNK // GROUP, GROUP, LANES)
    weights = jnp.exp(logits - jnp.max(logits, axis=1, keepdims=True))
    probs = (weights / jnp.sum(weights, axis=1, keepdims=True)).reshape(CHUNK, LANES)
    probs_ref[...] = probs
    chosen, _, _ = choose(probs, routes_ref[0])
    columns = chosen.shape[1]
    here = pl.ds(pl.multiple_of(step * columns, columns), columns)
    rows[here, :D] = transposed_product(chosen, normed).astype(bf16)
    rows[here, D:] = transposed_product(chosen, grad_ref[...]).astype(bf16)

    @pl.when(step == pl.num_programs(0) - 1)
    def _():
        shape = (out_ref.shape[0], rows.shape[0])
        dispatch = (lax.broadcasted_iota(jnp.int32, shape, 0) == slots_ref[...]).astype(bf16)
        out_ref[...] = product(dispatch, rows[...]).astype(bf16)


def mix(attended, tokens, grad_out, small, routes, slots, slot_count):
    length = tokens.shape[0]
    steps = length // CHUNK
    count = slots.shape[0]
    return call(
        mix_kernel,
        steps,
        [leading(CHUNK, D)] * 3
        + [small_columns(D, 3 * D), small_columns(LANES, 4 * D)]
        + [leading(1, 1, count // steps), fixed(1, count)],
        [leading(CHUNK, D), leading(CHUNK, LANES), fixed(slot_count, 2 * D)],
        [
            jax.ShapeDtypeStruct((length, D), f32),
            jax.ShapeDtypeStruct((length, LANES), f32),
            jax.ShapeDtypeStruct((slot_count, 2 * D), bf16),
        ],
        [pltpu.VMEM((count, 2 * D), bf16)],
        4 * length * D * D,
        14 * 2**20,
        "mix",
    )(
        attended, tokens, grad_out, small, small,
        routes.reshape(steps, 1, count // steps), slots.reshape(1, count),
    )


def combine_kernel(
    residual_ref, grad_ref, probs_ref, attended_ref, wo_ref, ctrl_ref, routes_ref,
    slots_ref, back_ref, output_ref, residual_grad_ref, attended_grad_ref, sums_ref, gain_sum,
):
    step = pl.program_id(0)
    gain = gain_of(ctrl_ref[...], GAIN_TWO)
    residual = residual_ref[...]
    scaled, inverse = normalise(residual)
    normed = (scaled * gain).astype(bf16)
    probs = probs_ref[...]
    grad = grad_ref[...]
    chosen, onehot, own = choose(probs, routes_ref[0])
    shape = (chosen.shape[1], back_ref.shape[0])
    collect = (lax.broadcasted_iota(jnp.int32, shape, 1) == slots_ref[...]).astype(bf16)
    rows = product(collect, back_ref[...]).astype(bf16)
    results = rows[:, :D]
    mixed_grad = rows[:, D:]
    output_ref[...] = (residual + product(chosen, results)).astype(bf16)
    chosen_grad = jnp.where(own, against_rows(grad, results) + against_rows(normed, mixed_grad), 0.0)
    high = chosen_grad.astype(bf16)
    low = (chosen_grad - high.astype(f32)).astype(bf16)
    prob_grad = against_rows(high, onehot) + against_rows(low, onehot)
    weighted = (probs * prob_grad).reshape(COMBINE // GROUP, GROUP, LANES)
    total = jnp.broadcast_to(jnp.sum(weighted, axis=1, keepdims=True), weighted.shape)
    logit_grad = (probs * (prob_grad - total.reshape(COMBINE, LANES))).astype(bf16)
    normed_grad = product(chosen, mixed_grad) + against_rows(logit_grad, ctrl_ref[...])
    gain_part = jnp.sum(normed_grad * scaled, axis=0, keepdims=True)
    residual_grad = grad.astype(f32) + norm_input_grad(normed_grad, scaled, inverse, gain)
    residual_grad_ref[...] = residual_grad
    branch = residual_grad.astype(bf16)
    attended_grad_ref[...] = against_rows(wo_ref[...], branch).astype(bf16)
    wo_part = transposed_product(attended_ref[...], branch)
    ctrl_part = transposed_product(normed, logit_grad)

    @pl.when(step == 0)
    def _():
        sums_ref[:, :D] = wo_part
        sums_ref[:, D:] = ctrl_part
        gain_sum[...] = gain_part

    @pl.when(step > 0)
    def _():
        sums_ref[:, :D] = sums_ref[:, :D] + wo_part
        sums_ref[:, D:] = sums_ref[:, D:] + ctrl_part
        gain_sum[...] = gain_sum[...] + gain_part

    @pl.when(step == pl.num_programs(0) - 1)
    def _():
        column = jnp.broadcast_to(gain_sum[...], (LANES, D)).T
        lane = lax.broadcasted_iota(jnp.int32, (D, LANES), 1)
        sums_ref[:, D:] = jnp.where(lane == LANES - 1, column, sums_ref[:, D:])


def combine(residual, grad_out, probs, attended, small, routes, slots, back):
    length = residual.shape[0]
    steps = length // COMBINE
    count = slots.shape[0]
    return call(
        combine_kernel,
        steps,
        [leading(COMBINE, D), leading(COMBINE, D), leading(COMBINE, LANES), leading(COMBINE, D)]
        + [small_columns(D, 3 * D), small_columns(LANES, 4 * D), leading(1, 1, count // steps)]
        + [leading(count // steps, 1), fixed(*back.shape)],
        [leading(COMBINE, D)] * 2
        + [pl.BlockSpec((D, COMBINE), lambda i: (0, i)), fixed(D, D + LANES)],
        [
            jax.ShapeDtypeStruct((length, D), bf16),
            jax.ShapeDtypeStruct((length, D), f32),
            jax.ShapeDtypeStruct((D, length), bf16),
            jax.ShapeDtypeStruct((D, D + LANES), f32),
        ],
        [pltpu.VMEM((1, D), f32)],
        6 * length * D * D,
        24 * 2**20,
        "combine",
        63,
    )(
        residual, grad_out, probs, attended, small, small,
        routes.reshape(steps, 1, count // steps), slots.reshape(count, 1), back,
    )


def weight_grad_kernel(core_ref, normed_t_ref, grad_ref, sums_ref, away_ref, kept_ref):
    step = pl.program_id(0)
    count, rows, _ = kept_ref.shape
    for x in range(count):
        mine = pl.ds(pl.multiple_of((2 * x + core_ref[0]) * rows, rows), rows)
        other = pl.ds(pl.multiple_of((2 * x + 1 - core_ref[0]) * rows, rows), rows)
        kept = product(normed_t_ref[mine, :], grad_ref[0])
        away = product(normed_t_ref[other, :], grad_ref[0]).astype(bf16)
        for i in range(3):

            @pl.when(step == i)
            def _(x=x, i=i, kept=kept, away=away):
                kept_ref[x, :, i * D : (i + 1) * D] = kept
                away_ref[x, :, i * D : (i + 1) * D] = away

        @pl.when(step == 0)
        def _(x=x, mine=mine, other=other):
            kept_ref[x, :, 3 * D :] = sums_ref[mine, :]
            away_ref[x, :, 3 * D :] = sums_ref[other, :].astype(bf16)


def weight_grads(normed_t, grads, sums, core, n_expert):
    length = normed_t.shape[1]
    width = sums.shape[1]
    shape = (n_expert // 2, D // n_expert, 3 * D + width)
    return call(
        weight_grad_kernel,
        3,
        [pl.BlockSpec(memory_space=pltpu.SMEM), fixed(D, length), leading(1, length, D)]
        + [fixed(D, width)],
        [fixed(*shape), fixed(*shape)],
        [jax.ShapeDtypeStruct(shape, bf16), jax.ShapeDtypeStruct(shape, f32)],
        [],
        6 * length * D * D,
        12 * 2**20,
        "weight_grads",
    )(core, normed_t, grads, sums)


def input_grad_kernel(grads_ref, w_ref, ctrl_ref, tokens_ref, residual_grad_ref, out_ref):
    upstream = against_rows(grads_ref[0], w_ref[:, :D])
    upstream = upstream + against_rows(grads_ref[1], w_ref[:, D : 2 * D])
    upstream = upstream + against_rows(grads_ref[2], w_ref[:, 2 * D :])
    scaled, inverse = normalise(tokens_ref[...].astype(f32))
    gain = gain_of(ctrl_ref[...], GAIN_ONE)
    out_ref[...] = (
        residual_grad_ref[...] + norm_input_grad(upstream, scaled, inverse, gain)
    ).astype(bf16)


def input_grads(grads, small, tokens, residual_grad):
    length = tokens.shape[0]
    return call(
        input_grad_kernel,
        length // CHUNK,
        [pl.BlockSpec((3, CHUNK, D), lambda i: (0, i, 0))]
        + [small_columns(3 * D, 0), small_columns(LANES, 4 * D)]
        + [leading(CHUNK, D), leading(CHUNK, D)],
        leading(CHUNK, D),
        jax.ShapeDtypeStruct((length, D), bf16),
        [],
        6 * length * D * D,
        18 * 2**20,
        "input_grads",
    )(grads, small, small, tokens, residual_grad)


def finish_kernel(
    pieces_ref, own_ref, q_ref, k_ref, v_ref, o_ref, ctrl_ref, one_ref, two_ref, bias_ref
):
    rows, experts = ctrl_ref.shape
    total = jnp.sum(pieces_ref[...].astype(f32), axis=0)
    own = own_ref[...].astype(f32)
    for i, ref in enumerate((q_ref, k_ref, v_ref, o_ref)):
        ref[...] = total[:, i * D : (i + 1) * D]
    ctrl_ref[...] = total[:, 4 * D : 4 * D + experts]
    lane = lax.broadcasted_iota(jnp.int32, (rows, LANES), 1)

    def column(block, which):
        return jnp.sum(jnp.where(lane == which, block[:, 4 * D : 4 * D + LANES], 0.0), axis=1, keepdims=True)

    one = jnp.sum(total[:, : 3 * D] * own[:, : 3 * D], axis=1, keepdims=True) / column(own, GAIN_ONE)
    square = (rows, rows)
    same = lax.broadcasted_iota(jnp.int32, square, 0) == lax.broadcasted_iota(jnp.int32, square, 1)
    one_ref[...] = jnp.sum(jnp.where(same, one, 0.0), axis=0, keepdims=True)
    two_ref[...] = jnp.sum(jnp.where(same, column(total, GAIN_TWO), 0.0), axis=0, keepdims=True)
    local, hidden = bias_ref.shape
    owner, lanes = bias_places(rows, hidden)
    copies = pieces_ref.shape[0] // local
    for e in range(local):
        for i in range(copies):
            part = product(pieces_ref[e * copies + i, :, 4 * D :], lanes)
            line = jnp.sum(jnp.where(owner, part, 0.0), axis=0, keepdims=True)
            bias_ref[e : e + 1, :] = line if i == 0 else bias_ref[e : e + 1, :] + line


def finish(pieces, own, experts, bias_shape):
    count, rows, width = pieces.shape
    outs = [(rows, D)] * 4 + [(rows, experts), (1, rows), (1, rows), bias_shape]
    return call(
        finish_kernel,
        1,
        [fixed(count, rows, width), fixed(*own.shape)],
        [fixed(*shape) for shape in outs],
        [jax.ShapeDtypeStruct(shape, f32) for shape in outs],
        [],
        1_000_000,
        1_000_000,
        "finish",
        8,
    )(pieces, own)


def swap(block, axis, bits):
    size = lax.axis_size(axis)
    return lax.ppermute(block, axis, [(i, i ^ bits) for i in range(size)])


def halves(size):
    inner = 1
    while inner * inner * 4 <= size:
        inner *= 2
    return size // inner, inner


def spread(block, size, stride, place):
    held = jnp.zeros((size,) + block.shape, block.dtype)
    held = lax.dynamic_update_slice(held, block[None], (place, 0, 0))
    for k in range(1, size):
        got = swap(block, "shard", k * stride)
        held = lax.dynamic_update_slice(held, got[None], (place ^ k, 0, 0))
    return held.reshape(-1, block.shape[1])


def gather_expert(held):
    n_expert = lax.axis_size("expert")
    mine = lax.axis_index("expert")
    rows, width = held.shape
    bit = n_expert // 2
    steps = 0
    while bit:
        got = swap(held, "expert", bit)
        low = (mine & bit) == 0
        held = jnp.stack([jnp.where(low, held, got), jnp.where(low, got, held)])
        bit //= 2
        steps += 1
    order = tuple(range(steps - 1, -1, -1)) + (steps, steps + 1)
    return held.transpose(order).reshape(n_expert * rows, width)


def sum_expert(away, kept):
    n_expert = lax.axis_size("expert")
    mine = lax.axis_index("expert")
    width = kept.shape[-1]
    steps = n_expert.bit_length() - 1
    shape = (2,) * (steps - 1) + (-1, width)
    terms = [kept.reshape(shape), swap(away, "expert", 1).reshape(shape)]
    for step in range(1, steps):
        bit = 1 << step
        axis = steps - 1 - step
        high = (mine & bit) >> step

        def half(which, axis=axis):
            return [lax.dynamic_index_in_dim(t, which, axis, keepdims=False) for t in terms]

        away = sum(t.astype(f32) for t in half(high ^ 1)).astype(bf16)
        terms = half(high) + [swap(away, "expert", bit)]
    return sum(t.astype(f32) for t in terms)


def along_shard(blocks):
    return lax.all_to_all(blocks, "shard", split_axis=0, concat_axis=0, tiled=True)


def to_experts(array, copies):
    if copies > 1:
        array = jnp.repeat(array, copies, axis=0)
    return along_shard(array)


def from_experts(array, copies):
    back = along_shard(array)
    if copies > 1:
        back = back.astype(f32).reshape((-1, copies) + back.shape[1:]).sum(axis=1)
    return back


def exchange(rows, copies):
    n_expert = lax.axis_size("expert")
    n_shard = lax.axis_size("shard")
    groups = None
    if copies > 1:
        groups = [
            [e * n_shard + s for e in range(n_expert) for s in range(p, n_shard, copies)]
            for p in range(copies)
        ]
    return lax.all_to_all(
        rows, BOTH, split_axis=0, concat_axis=0, tiled=True, axis_index_groups=groups
    )


def slots_of(routes, experts):
    groups = routes.shape[0]
    named = (routes[:, :, None] == jnp.arange(experts, dtype=jnp.int32)[None, None, :]).astype(f32)
    earlier = jnp.tril(jnp.ones((groups, groups), f32), -1).astype(bf16)
    before = product(earlier, jnp.sum(named, axis=1).astype(bf16))
    rank = jnp.sum(named * before[:, None, :], axis=2).astype(jnp.int32)
    return (routes * CAP + rank).reshape(-1)


def body(
    tokens,
    ln1_gain,
    ln2_gain,
    w_query,
    w_key,
    w_value,
    w_attn_out,
    w_ctrl,
    w_in,
    b_in,
    w_exp_out,
    routes,
    grad_out,
):
    experts = w_ctrl.shape[1]
    n_shard = lax.axis_size("shard")
    copies = n_shard * lax.axis_size("expert") // experts
    slots = slots_of(routes, experts)

    own = pack_small(
        (w_query, w_key, w_value, w_attn_out), w_ctrl, ln1_gain, ln2_gain, b_in
    )
    outer, inner = halves(n_shard)
    here = lax.axis_index("shard")
    held = spread(own, inner, 1, here & (inner - 1))
    held, w_in, w_exp_out = lax.optimization_barrier((held, w_in, w_exp_out))
    expert_w = to_experts(pack_weights(w_in, w_exp_out), copies)
    held = spread(held, outer, inner, here >> (inner.bit_length() - 1))
    small = gather_expert(held)
    local, hidden = b_in.shape
    biases = held.reshape(n_shard, -1, held.shape[1])[:, :, 4 * D + LANES :]
    bias = jnp.concatenate(
        [
            lax.dynamic_index_in_dim(biases, c * local + here // copies, 1, keepdims=False)
            for c in range(hidden // LANES)
        ],
        axis=1,
    ).astype(f32)

    qkv, normed_t = project(tokens, small)
    attended, lse, query_t, key_t, attended_t = attention_forward(qkv)
    residual, probs, outgoing = mix(
        attended, tokens, grad_out, small, routes, slots, experts * CAP
    )
    outgoing, expert_w = lax.optimization_barrier((outgoing, expert_w))
    arrived = exchange(outgoing, copies)
    results = expert_rows(arrived, expert_w, bias)
    returned = exchange(results, copies)
    expert_sums, bias_sums = expert_grads(arrived, expert_w, bias, own.shape[0])
    returned, expert_sums = lax.optimization_barrier((returned, expert_sums))
    expert_sums = from_experts(expert_sums, copies)
    output, residual_grad, grad_t, sums = combine(
        residual, grad_out, probs, attended, small, routes, slots, returned
    )
    grads = attention_backward(qkv, query_t, key_t, grad_t, attended_t, lse)
    core = (lax.axis_index("expert") & 1).reshape(1)
    away, kept = weight_grads(normed_t, grads, sums, core, lax.axis_size("expert"))
    late = sum_expert(away, kept).reshape(n_shard, own.shape[0], -1)
    late = late + jnp.pad(bias_sums.astype(f32), ((0, 0), (0, 0), (4 * D, 0)))
    late = late.astype(bf16)
    input_grad = input_grads(grads, small, tokens, residual_grad)
    late, input_grad, expert_sums = lax.optimization_barrier((late, input_grad, expert_sums))
    pieces = along_shard(late)
    w_in_grad, w_exp_out_grad = unpack_grads(expert_sums)
    wq_grad, wk_grad, wv_grad, wo_grad, wc_grad, ln1_grad, ln2_grad, b_in_grad = finish(
        pieces, own, experts, b_in.shape
    )
    return (
        output,
        input_grad,
        ln1_grad.reshape(-1),
        ln2_grad.reshape(-1),
        wq_grad,
        wk_grad,
        wv_grad,
        wo_grad,
        wc_grad,
        w_in_grad,
        b_in_grad,
        w_exp_out_grad,
    )


def solution(mesh):
    rows = P(BOTH, None)
    vector = P(BOTH)
    experts = (P("expert", None, "shard"), P("expert", "shard"), P("expert", "shard", None))
    in_specs = (rows, vector, vector) + (rows,) * 5 + experts + (rows, rows)
    out_specs = (rows, rows, vector, vector) + (rows,) * 5 + experts
    return jax.shard_map(body, mesh=mesh, in_specs=in_specs, out_specs=out_specs, check_vma=False)
```
